128 devices in a mesh: dp: 8 (over z, y_lo), tensor: 16 (over x, y_hi, core).
Axes of the slice: x: 4, y: 4 (y_hi: 2, y_lo: 2; y = y_hi * 2 + y_lo), z: 4, core: 2. Of those that a mesh axis runs over, the one named last changes fastest.
Arguments:
- doc_inputs: bfloat16 [4096, 8192], P('dp'), may hold values from -6 to 6
- doc_hidden_grads: bfloat16 [4096, 14336], P('dp', 'tensor'), may hold values from -6 to 6
- query_inputs: bfloat16 [2048, 8192], P('dp'), may hold values from -6 to 6
- query_hidden_grads: bfloat16 [2048, 14336], P('dp', 'tensor'), may hold values from -6 to 6
- gate_weight: bfloat16 [8192, 14336], P('dp', 'tensor'), may hold values from -0.0625 to 0.0625
- up_weight: bfloat16 [8192, 14336], P('dp', 'tensor'), may hold values from -0.0625 to 0.0625
- doc_ids: int32 [8, 512], P('dp'), may hold values from 0 to 3, never falling along the last dimension, each value on 1 to 256 neighbouring positions
- query_ids: int32 [8, 256], replicated, may hold values from 0 to 3, never falling along the last dimension, each value on 1 to 128 neighbouring positions
Outputs:
- scores: float32 [8, 4, 32], P('dp')
The draws below stay inside these ranges and needn't reach their ends.
Inputs may be any that keep to these rules, and one draw needn't show every extreme that they name: `doc_ids`: within each row the ids never fall, every id 0 to 3 occurs, and one document has exactly 256 tokens. `query_ids`: within each row the ids never fall, every id 0 to 3 occurs, and one query has exactly 128 tokens.
All inputs are finite; a program needn't handle non-finite values.
Results may differ from the reference program's by a relative error of at most 0.0039.
Values may be sent and summed in bfloat16 or wider, within the bound.
No kernel may reach another device: no remote copies, remote signals or barrier semaphores. Data moves between devices by JAX's collectives and lax.ppermute only.
A program may use at most 192 MiB of HBM per device.

```python
import math
import jax
import jax.numpy as jnp
import numpy as np
from jax import lax

D = 8192
FF = 14336
TOK_DEV = 512
DOCS_DEV = 4
QTOK_DEV = 256
Q_DEV = 4
TOKENS = 4096
QTOKENS = 2048
N_DP = 8


def steps_of(rng, extent, pieces, smallest, high):
    loudness, own = 1.0, jax.random.fold_in(rng, 6)
    for dim, blocks in pieces:
        heights = jnp.exp(jax.random.uniform(jax.random.fold_in(own, dim), (blocks,), jnp.float32, smallest / len(pieces), high / len(pieces)))
        loudness = loudness * jnp.repeat(heights, extent[dim] // blocks).reshape([-1 if axis == dim else 1 for axis in range(len(extent))])
    return loudness


def split_up(amount, total, bound, skew):
    weights = [(1 << 20) // math.isqrt(standing ** skew) + 1 for standing in range(2, amount + 1)]
    spare, given = total - bound - (amount - 1), [1] * (amount - 1)
    while spare > 0:
        candidates = [i for i in range(amount - 1) if given[i] < bound]
        whole, left = sum([weights[i] for i in candidates]), spare
        for i in candidates:
            more = min(bound - given[i], max(1, left * weights[i] // whole), spare)
            given[i] = given[i] + more
            spare = spare - more
    return np.array([bound] + given)


def ragged(own_key, amount, total, limit, lean):
    if amount == 2:
        one = jax.random.randint(own_key, (), max(1, total - limit), min(limit, total - 1) + 1)
        return jnp.stack([one, total - one])
    sizes = jnp.asarray(split_up(amount, total, limit, lean), jnp.int32)
    pairs = (amount - 1) // 2
    source_of, sink = sizes[1:1 + 2 * pairs:2], sizes[2:2 + 2 * pairs:2]
    margin = jnp.minimum(source_of - 1, limit - sink)
    moved = jax.random.randint(jax.random.fold_in(own_key, 1), (pairs,), 0, 1 << 20) % (margin + 1)
    sizes = sizes.at[1:1 + 2 * pairs:2].set(source_of - moved).at[2:2 + 2 * pairs:2].set(sink + moved)
    return sizes[jax.random.permutation(jax.random.fold_in(own_key, 2), amount)]


def centred(rng, shape, width, most, shards=(), kind=jnp.bfloat16):
    factor_of = steps_of(rng, shape, shards, -0.22, 0.18) if shards else 1.0
    entries = jax.random.normal(rng, shape, jnp.float32) * width * factor_of
    return jnp.minimum(jnp.maximum(entries, -most), most).astype(kind)


def setup_inputs(seed: int = 0) -> dict:
    key_list = jax.random.split(jax.random.key(seed), 9)
    doc_inputs = centred(key_list[0], (TOKENS, D), 1.0, 6.0, ((0, 8),))
    doc_hidden_grads = centred(key_list[1], (TOKENS, FF), 1.0, 6.0, ((0, 8), (1, 16)))
    query_inputs = centred(key_list[2], (QTOKENS, D), 1.0, 6.0, ((0, 8),))
    query_hidden_grads = centred(key_list[3], (QTOKENS, FF), 1.0, 6.0, ((0, 8), (1, 16)))
    gate_weight = centred(key_list[4], (D, FF), D ** -0.5, 0.0625, ((0, 8), (1, 16)))
    up_weight = centred(key_list[5], (D, FF), D ** -0.5, 0.0625, ((0, 8), (1, 16)))
    doc_ids = jax.vmap(lambda own: jnp.searchsorted(jnp.cumsum(ragged(own, DOCS_DEV, TOK_DEV, TOK_DEV // 2, 1)), jnp.arange(TOK_DEV), side="right"))(jax.random.split(key_list[6], N_DP)).reshape((N_DP, TOK_DEV)).astype(jnp.int32)
    query_ids = jax.vmap(lambda own: jnp.searchsorted(jnp.cumsum(ragged(own, Q_DEV, QTOK_DEV, QTOK_DEV // 2, 1)), jnp.arange(QTOK_DEV), side="right"))(jax.random.split(key_list[7], N_DP)).reshape((N_DP, QTOK_DEV)).astype(jnp.int32)
    return dict(doc_inputs=doc_inputs, doc_hidden_grads=doc_hidden_grads, query_inputs=query_inputs, query_hidden_grads=query_hidden_grads, gate_weight=gate_weight, up_weight=up_weight, doc_ids=doc_ids, query_ids=query_ids)


def grad_factors(inputs, grads, gate_weight, up_weight):
    gate = jnp.dot(inputs, gate_weight, preferred_element_type=jnp.float32)
    up_value = jnp.dot(inputs, up_weight, preferred_element_type=jnp.float32)
    sigmoid_gate = jax.nn.sigmoid(gate)
    hidden = grads.astype(jnp.float32)
    up_factor = (hidden * gate * sigmoid_gate).astype(jnp.bfloat16)
    gate_factor = (hidden * up_value * sigmoid_gate * (1.0 + gate * (1.0 - sigmoid_gate))).astype(jnp.bfloat16)
    return (gate_factor, up_factor)

def reference(doc_inputs, doc_hidden_grads, query_inputs, query_hidden_grads, gate_weight, up_weight, doc_ids, query_ids):
    doc_gate, doc_up = grad_factors(doc_inputs, doc_hidden_grads, gate_weight, up_weight)
    query_gate, query_up = grad_factors(query_inputs, query_hidden_grads, gate_weight, up_weight)
    gram_inputs = jnp.dot(doc_inputs, query_inputs.T, preferred_element_type=jnp.float32)
    gram_factors = jnp.dot(doc_gate, query_gate.T, preferred_element_type=jnp.float32) + jnp.dot(doc_up, query_up.T, preferred_element_type=jnp.float32)
    product = gram_inputs * gram_factors
    group_rows = jnp.arange(N_DP, dtype=jnp.int32)[:, None]
    doc_index = (group_rows * DOCS_DEV + doc_ids).reshape(-1).astype(jnp.int32)
    query_index = (group_rows * Q_DEV + query_ids).reshape(-1).astype(jnp.int32)
    doc_onehot = (doc_index[:, None] == jnp.arange(N_DP * DOCS_DEV, dtype=jnp.int32)[None, :]).astype(jnp.float32)
    query_onehot = (query_index[:, None] == jnp.arange(N_DP * Q_DEV, dtype=jnp.int32)[None, :]).astype(jnp.float32)
    per_doc = jnp.dot(doc_onehot.T, product, precision=lax.Precision.HIGHEST)
    scores = jnp.dot(per_doc, query_onehot, precision=lax.Precision.HIGHEST) / math.sqrt(D * FF)
    return scores.reshape(N_DP, DOCS_DEV, N_DP * Q_DEV)
```

```python
import functools
import math

import jax
import jax.numpy as jnp
from jax import lax
from jax.experimental import pallas as pl
from jax.experimental.pallas import tpu as pltpu
from jax.sharding import PartitionSpec as P

D = 8192
FF = 14336
DOCS = 4
QS = 4
TOK = 512
QTOK = 256
ROWS = TOK + QTOK
BLK = D // 8
AX = ("dp", "tensor")
F32 = jnp.float32
BF16 = jnp.bfloat16


def place(z, y, x, c):
    return ((z % 4) * 2 + (y % 2)) * 16 + (x % 4) * 4 + ((y % 4) // 2) * 2 + c


def perm(fn):
    return [
        (place(z, y, x, c), place(*fn(z, y, x, c)))
        for z in range(4)
        for y in range(4)
        for x in range(4)
        for c in range(2)
    ]


ZP = perm(lambda z, y, x, c: (z + 1, y, x, c))
ZM = perm(lambda z, y, x, c: (z - 1, y, x, c))
YP = perm(lambda z, y, x, c: (z, y + 1, x, c))
YM = perm(lambda z, y, x, c: (z, y - 1, x, c))
XP = perm(lambda z, y, x, c: (z, y, x + 1, c))
XM = perm(lambda z, y, x, c: (z, y, x - 1, c))
PARTNER = perm(lambda z, y, x, c: (z, y ^ 1, x, c))
OTHER = perm(lambda z, y, x, c: (z, (3 - y) % 4, x, c))
CORE = perm(lambda z, y, x, c: (z, y, x, 1 - c))


def send(v, p):
    return lax.ppermute(v, AX, p)


def ring(v, plus, minus):
    half = v.shape[0] // 2
    below = send(v, plus)
    above = send(v, minus)
    far0 = send(below[:half], plus)
    far1 = send(above[half:], minus)
    return below, above, far0, far1


def factor_kernel(lens, narrow, off, x, *refs):
    ws, h, out = refs[: len(lens)], refs[len(lens)], refs[len(lens) + 1]
    acc = None
    for i, n in enumerate(lens):
        xs = x[:, pl.ds(pl.multiple_of(off[i], 512), n)]
        part = jnp.dot(xs, ws[i][...], preferred_element_type=F32)
        acc = part if acc is None else acc + part
    hidden = h[...].astype(F32)
    if narrow:
        low = lax.broadcasted_iota(jnp.int32, acc.shape, 1) < 64
        turned = pltpu.roll(acc, 64, 1)
        gate = jnp.where(low, acc, turned)
        up = jnp.where(low, turned, acc)
    else:
        gate, up = acc[:, :128], acc[:, 128:]
    s = jax.nn.sigmoid(gate)
    up_factor = (hidden * gate * s).astype(BF16)
    gate_factor = (hidden * up * s * (1.0 + gate * (1.0 - s))).astype(BF16)
    if narrow:
        out[...] = jnp.where(low, gate_factor.astype(F32), up_factor.astype(F32)).astype(BF16)
    else:
        out[:, :128] = gate_factor
        out[:, 128:] = up_factor


def factors(off, x, ws, h):
    lens = tuple(w.shape[0] for w in ws)
    width = ws[0].shape[1]
    tile = 256
    grid_spec = pltpu.PrefetchScalarGridSpec(
        num_scalar_prefetch=1,
        grid=(ROWS // tile,),
        in_specs=[pl.BlockSpec((tile, D), lambda i, o: (i, 0))]
        + [pl.BlockSpec((n, width), lambda i, o: (0, 0)) for n in lens]
        + [pl.BlockSpec((tile, 128), lambda i, o: (i, 0))],
        out_specs=pl.BlockSpec((tile, width), lambda i, o: (i, 0)),
    )
    return pl.pallas_call(
        functools.partial(factor_kernel, lens, width == 128),
        grid_spec=grid_spec,
        out_shape=jax.ShapeDtypeStruct((ROWS, width), BF16),
        compiler_params=pltpu.CompilerParams(vmem_limit_bytes=40 << 20),
        cost_estimate=pl.CostEstimate(
            flops=2 * ROWS * D * width, bytes_accessed=ROWS * D * 2 + D * width * 2, transcendentals=ROWS * width
        ),
    )(off, x, *ws, h)


def chunk(v, j, ylo):
    if j < 3:
        return lax.dynamic_slice_in_dim(v, (ylo * 4 + j) * 128, 128, 1)
    return jnp.where(ylo == 0, v[:, 384:448], v[:, 448:512])


def local(doc_inputs, doc_grads, query_inputs, query_grads, gate_weight, up_weight, doc_ids, query_ids):
    dp = lax.axis_index("dp")
    tensor = lax.axis_index("tensor")
    z, ylo = dp // 2, dp % 2
    x, yhi, core = tensor // 4, (tensor // 2) % 2, tensor % 2
    y = yhi * 2 + ylo

    weights = []
    for j in range(4):
        keep = jnp.concatenate([chunk(gate_weight, j, ylo), chunk(up_weight, j, ylo)], 1)
        give = jnp.concatenate([chunk(gate_weight, j, 1 - ylo), chunk(up_weight, j, 1 - ylo)], 1)
        got = send(give, PARTNER)
        weights.append((keep, *ring(keep, ZP, ZM), got, *ring(got, ZP, ZM)))

    def row_of(dz, flip):
        return ((z + dz + 4) % 4 * 2 + (ylo ^ flip)) * BLK

    off = []
    for flip in (0, 1):
        off += [row_of(0, flip), row_of(-1, flip), row_of(1, flip), row_of(2, flip), row_of(2, flip) + BLK // 2]
    off = jnp.stack(off).astype(jnp.int32)

    grads = jnp.concatenate([doc_grads, query_grads], 0)
    mine = [chunk(grads, j, ylo) for j in range(4)]
    theirs = send(jnp.concatenate([chunk(grads, j, 1 - ylo) for j in range(4)], 1), PARTNER)
    theirs = [theirs[:, 128 * j : 128 * j + 128] for j in range(3)] + [theirs[:, 384:]]
    mine[3] = jnp.concatenate([mine[3], mine[3]], 1)
    theirs[3] = jnp.concatenate([theirs[3], theirs[3]], 1)

    own = jnp.concatenate([doc_inputs, query_inputs], 0)
    piece = send(lax.dynamic_slice_in_dim(own, (x * 2 + core) * BLK, BLK, 1), OTHER)
    other = jnp.zeros((ROWS, D), BF16)
    below, above, far0, far1 = ring(piece, XP, XM)
    for dx, v in ((0, piece), (-1, below), (1, above), (2, jnp.concatenate([far0, far1], 0))):
        base = (x + dx + 4) % 4 * 2
        other = lax.dynamic_update_slice(other, v, (0, (base + core) * BLK))
        other = lax.dynamic_update_slice(other, send(v, CORE), (0, (base + 1 - core) * BLK))

    mine_q = lax.dynamic_slice_in_dim(query_inputs, tensor * 16, 16, 0)
    below, above, far0, far1 = ring(mine_q, ZP, ZM)
    qs = jnp.concatenate([mine_q, below, above, far0, far1], 0)
    contract = (((1,), (1,)), ((), ()))
    gi_own = lax.dot_general(qs, doc_inputs, contract, preferred_element_type=F32)
    gi_other = lax.dot_general(qs, other[:TOK], contract, preferred_element_type=F32)
    gi = jnp.where(
        ylo == 0, jnp.concatenate([gi_own, gi_other], 1), jnp.concatenate([gi_other, gi_own], 1)
    ).reshape(4, 16, 2 * TOK)
    below, above, far0, far1 = ring(gi, YP, YM)
    plane = jnp.zeros((4, 2, 2, 16, 2 * TOK), F32)
    for dy, v in ((0, gi), (-1, below), (1, above), (2, jnp.concatenate([far0, far1], 0))):
        at = (y + dy + 4) % 4 // 2
        plane = lax.dynamic_update_slice(plane, v[:, None, None], (0, dy % 2, at, 0, 0))
    below, above, far0, far1 = ring(plane, XP, XM)
    gram_inputs = jnp.zeros((4, 2, 4, 2, 2, 16, 2 * TOK), F32)
    for dx, v in ((0, plane), (-1, below), (1, above), (2, jnp.concatenate([far0, far1], 0))):
        at = (x + dx + 4) % 4
        gram_inputs = lax.dynamic_update_slice(gram_inputs, v[:, :, None, :, None], (0, 0, at, 0, core, 0, 0))
        gram_inputs = lax.dynamic_update_slice(
            gram_inputs, send(v, CORE)[:, :, None, :, None], (0, 0, at, 0, 1 - core, 0, 0)
        )
    gram_inputs = gram_inputs.reshape(4 * 2 * QTOK, 2 * TOK)

    gram_factors = None
    for j in range(4):
        f_own = factors(off, own, weights[j], mine[j])
        f_other = factors(off, other, weights[j], theirs[j])
        fq = jnp.concatenate([f_own[TOK:], f_other[TOK:]], 0)
        fd = jnp.where(
            ylo == 0,
            jnp.concatenate([f_own[:TOK], f_other[:TOK]], 0),
            jnp.concatenate([f_other[:TOK], f_own[:TOK]], 0),
        )
        fq = jnp.concatenate([fq, *ring(fq, ZP, ZM)], 0)
        part = lax.dot_general(fq, fd, contract, preferred_element_type=F32)
        gram_factors = part if gram_factors is None else gram_factors + part

    ids = jnp.arange(8, dtype=jnp.int32)[:, None] * QS + query_ids
    order = jnp.stack(
        [(z + dz + 4) % 4 * 2 + (ylo ^ flip) for dz in (0, -1, 1, 2) for flip in (0, 1)]
    )
    ids = ids[order].reshape(-1)
    query_onehot = (ids[None, :] == jnp.arange(8 * QS, dtype=jnp.int32)[:, None]).astype(F32)
    other_ids = send(doc_ids, PARTNER)
    both = jnp.where(
        ylo == 0, jnp.concatenate([doc_ids, other_ids + DOCS], 1), jnp.concatenate([other_ids, doc_ids + DOCS], 1)
    )[0]
    doc_onehot = (both[:, None] == jnp.arange(2 * DOCS, dtype=jnp.int32)[None, :]).astype(F32)
    product = gram_inputs * gram_factors
    per_query = jnp.dot(query_onehot, product, precision=lax.Precision.HIGHEST)
    scores = jnp.dot(per_query, doc_onehot, precision=lax.Precision.HIGHEST).T
    scores = lax.psum(scores, "tensor")
    mine_s = jnp.where(ylo == 0, scores[:DOCS], scores[DOCS:])
    give_s = jnp.where(ylo == 0, scores[DOCS:], scores[:DOCS])
    scores = (mine_s + send(give_s, PARTNER)) / math.sqrt(D * FF)
    return scores[None]


def solution(mesh):
    placed = (
        P("dp", None),
        P("dp", "tensor"),
        P("dp", None),
        P("dp", "tensor"),
        P("dp", "tensor"),
        P("dp", "tensor"),
        P("dp", None),
        P(),
    )
    return jax.shard_map(
        local, mesh=mesh, in_specs=placed, out_specs=P("dp", None, None), check_vma=False
    )
```

```python
import functools
import math

import jax
import jax.numpy as jnp
from jax import lax
from jax.experimental import pallas as pl
from jax.experimental.pallas import tpu as pltpu
from jax.sharding import PartitionSpec as P

D = 8192
FF = 14336
DOCS = 4
QS = 4
TOK = 512
QTOK = 256
ROWS = TOK + QTOK
BLK = D // 8
THIN = BLK + 512
AX = ("dp", "tensor")
F32 = jnp.float32
BF16 = jnp.bfloat16


def place(z, y, x, c):
    return ((z % 4) * 2 + (y % 2)) * 16 + (x % 4) * 4 + ((y % 4) // 2) * 2 + c


def perm(fn):
    return [
        (place(z, y, x, c), place(*fn(z, y, x, c)))
        for z in range(4)
        for y in range(4)
        for x in range(4)
        for c in range(2)
    ]


ZP = perm(lambda z, y, x, c: (z + 1, y, x, c))
ZM = perm(lambda z, y, x, c: (z - 1, y, x, c))
YP = perm(lambda z, y, x, c: (z, y + 1, x, c))
YM = perm(lambda z, y, x, c: (z, y - 1, x, c))
XP = perm(lambda z, y, x, c: (z, y, x + 1, c))
XM = perm(lambda z, y, x, c: (z, y, x - 1, c))
PARTNER = perm(lambda z, y, x, c: (z, y ^ 1, x, c))
OTHER = perm(lambda z, y, x, c: (z, (3 - y) % 4, x, c))
CORE = perm(lambda z, y, x, c: (z, y, x, 1 - c))
Y2 = perm(lambda z, y, x, c: (z, y + 2, x, c))
X2 = perm(lambda z, y, x, c: (z, y, x + 2, c))
X1 = perm(lambda z, y, x, c: (z, y, x ^ 1, c))
XX = perm(lambda z, y, x, c: (z, y, x ^ 2, c))
Y1 = PARTNER
YY = perm(lambda z, y, x, c: (z, y ^ 2, x, c))
STEPS = (0, -1, 1, 2)
LIMIT = 56 << 20
SLOTS = 3
SMALL = pl.CostEstimate(flops=1 << 10, bytes_accessed=1 << 10, transcendentals=0)
ZGROUPS = [[place(z, y, x, c) for z in range(4)] for y in range(4) for x in range(4) for c in range(2)]
NT = (((1,), (1,)), ((), ()))


def send(v, p):
    return lax.ppermute(v, AX, p)


def ring(v, plus, minus):
    half = v.shape[0] // 2
    below = send(v, plus)
    above = send(v, minus)
    far0 = send(below[:half], plus)
    far1 = send(above[half:], minus)
    return below, above, far0, far1


def direct(v, plus, minus, two):
    return send(v, plus), send(v, minus), send(v, two)


def tie(*vs):
    return lax.optimization_barrier(vs)


def pack_kernel(s, gate, up, doc, query, some, keep0, keep1, give0, give1, piece):
    i = pl.program_id(0)
    ylo = s[0]
    rows = gate.shape[0]
    gh, uh = gate[:, 384:512].astype(F32), up[:, 384:512].astype(F32)
    gt, ut = pltpu.roll(gh, 64, 1), pltpu.roll(uh, 64, 1)
    low = lax.broadcasted_iota(jnp.int32, gh.shape, 1) < 64
    first = jnp.where(low, gh, ut)
    second = jnp.where(low, gt, uh)
    for half, wide, thin, at in ((ylo, keep0, keep1, pl.ds(i * rows, rows)), (1 - ylo, give0, give1, slice(None))):
        base = pl.multiple_of(half * 512, 128)
        wide[:, :256] = gate[:, pl.ds(base, 256)]
        wide[:, 256:512] = up[:, pl.ds(base, 256)]
        wide[:, 512:] = jnp.where(half == 0, first, second).astype(BF16)
        base = pl.multiple_of(half * 512 + 256, 128)
        thin[at, :128] = gate[:, pl.ds(base, 128)]
        thin[at, 128:] = up[:, pl.ds(base, 128)]
    piece[pl.ds(i * doc.shape[0], doc.shape[0])] = doc[...]
    piece[pl.ds(TOK + i * query.shape[0], query.shape[0])] = query[...]

    @pl.when(i == 0)
    def _():
        for j in range(32):
            keep1[BLK + 16 * j : BLK + 16 * j + 16] = some[:, 256 * j : 256 * j + 256]


def pack(scalars, gate, up, doc, query):
    steps = 4
    rows = BLK // steps
    spec = lambda n: pl.BlockSpec((rows, n), lambda i, s: (i, 0))
    whole = lambda *shape: pl.BlockSpec(shape, lambda i, s: (0, 0))
    shape = lambda r, n: jax.ShapeDtypeStruct((r, n), BF16)
    return pl.pallas_call(
        pack_kernel,
        grid_spec=pltpu.PrefetchScalarGridSpec(
            num_scalar_prefetch=1,
            grid=(steps,),
            in_specs=[
                spec(896),
                spec(896),
                pl.BlockSpec((TOK // steps, BLK), lambda i, s: (i, s[1])),
                pl.BlockSpec((QTOK // steps, BLK), lambda i, s: (i, s[1])),
                pl.BlockSpec((16, D), lambda i, s: (s[2], 0)),
            ],
            out_specs=[spec(640), whole(THIN, 256), spec(640), spec(256), whole(ROWS, BLK)],
        ),
        out_shape=[shape(BLK, 640), shape(THIN, 256), shape(BLK, 640), shape(BLK, 256), shape(ROWS, BLK)],
        compiler_params=pltpu.CompilerParams(vmem_limit_bytes=LIMIT),
        cost_estimate=SMALL,
    )(scalars, gate, up, doc, query, query)


def pack_grads_kernel(ylo_ref, doc, query, weights, keep, give):
    ylo = ylo_ref[0]
    give[2 * ROWS :] = weights[...]
    for src, lo, n in ((doc, 0, TOK), (query, TOK, QTOK)):
        h = src[:, 384:512].astype(F32)
        t = pltpu.roll(h, 64, 1)
        low = lax.broadcasted_iota(jnp.int32, h.shape, 1) < 64
        first, second = jnp.where(low, h, t), jnp.where(low, t, h)
        for s, out, below in ((ylo, keep, 0), (1 - ylo, give, ROWS)):
            base = pl.multiple_of(s * 512, 128)
            out[lo : lo + n, :256] = src[:, pl.ds(base, 256)]
            lo2, at = lo + below, 0 if below else 256
            out[lo2 : lo2 + n, at : at + 128] = src[:, pl.ds(pl.multiple_of(base + 256, 128), 128)]
            out[lo2 : lo2 + n, at + 128 : at + 256] = jnp.where(s == 0, first, second).astype(BF16)


def pack_grads(ylo, doc, query, weights):
    vmem = pl.BlockSpec(memory_space=pltpu.VMEM)
    return pl.pallas_call(
        pack_grads_kernel,
        in_specs=[pl.BlockSpec(memory_space=pltpu.SMEM), vmem, vmem, vmem],
        out_specs=[vmem, vmem],
        out_shape=[jax.ShapeDtypeStruct((ROWS, 512), BF16), jax.ShapeDtypeStruct((2 * ROWS + BLK, 256), BF16)],
        compiler_params=pltpu.CompilerParams(vmem_limit_bytes=LIMIT),
        cost_estimate=SMALL,
    )(ylo, doc, query, weights)


def halves_kernel(a_below, b_below, a_above, b_above, x_below, x_above, far0, far1, x_far0, x_far1):
    n = BLK // 2
    for src, lo, out, at in ((a_below, 0, far0, 0), (b_below, 0, far0, n), (a_above, n, far1, 0), (b_above, n, far1, n)):
        out[at : at + n] = src[...]
    x_far0[...] = x_below[...]
    x_far1[...] = x_above[...]


def halves(a_below, b_below, a_above, b_above, x_below, x_above):
    spec = lambda rows, n, at: pl.BlockSpec((rows, n), lambda i: (at, 0))
    n, m = BLK // 2, ROWS // 2
    return pl.pallas_call(
        halves_kernel,
        grid=(1,),
        in_specs=[spec(n, 640, 0)] * 2 + [spec(n, 640, 1)] * 2 + [spec(m, BLK, 0), spec(m, BLK, 1)],
        out_specs=[spec(BLK, 640, 0)] * 2 + [spec(m, BLK, 0)] * 2,
        out_shape=[jax.ShapeDtypeStruct((BLK, 640), BF16)] * 2 + [jax.ShapeDtypeStruct((m, BLK), BF16)] * 2,
        compiler_params=pltpu.CompilerParams(vmem_limit_bytes=LIMIT),
        cost_estimate=SMALL,
    )(a_below, b_below, a_above, b_above, x_below, x_above)


def gated(hidden, gate, up):
    s = jax.nn.sigmoid(gate)
    up_factor = (hidden * gate * s).astype(BF16)
    gate_factor = (hidden * up * s * (1.0 + gate * (1.0 - s))).astype(BF16)
    return gate_factor, up_factor


def factor_kernel(count, nw, nt, nx, begins, ends, s, *refs):
    ws, refs = refs[:nw], refs[nw:]
    thins, refs = refs[:nt], refs[nt:]
    xs, refs = refs[:nx], refs[nx:]
    if not begins:
        before, refs = refs[0], refs[1:]
    if ends:
        h, h2, out_d, out_q, acc, wv, tv, xv, wsem, tsem, xsem = refs
    else:
        out, acc, wv, tv, xv, wsem, tsem, xsem = refs
    i = pl.program_id(0)
    slot = lax.rem(i, SLOTS)

    def start(k):
        at = k % SLOTS
        block = s[k]
        for w in range(nw):

            @pl.when(s[16 + k] == w)
            def _():
                if w < 6:
                    pltpu.make_async_copy(ws[w], wv.at[at], wsem.at[at]).start()
                else:
                    n = BLK // 2
                    rows = pl.ds((w - 6) * n, n)
                    pltpu.make_async_copy(ws[6].at[rows], wv.at[at, pl.ds(0, n)], wsem.at[at]).start()
                    pltpu.make_async_copy(ws[7].at[rows], wv.at[at, pl.ds(n, n)], wsem.at[at]).start()

        for flip in range(nt):
            rows = pl.ds(pl.multiple_of(block // 2 * (BLK if flip else THIN), 512), BLK)

            @pl.when(lax.rem(block, 2) == (s[24] ^ flip))
            def _():
                pltpu.make_async_copy(thins[flip].at[rows], tv.at[at], tsem.at[at]).start()

        if nx == 2:
            cols = pl.ds(pl.multiple_of(block * BLK, BLK), BLK)
            pltpu.make_async_copy(xs[0].at[:, cols], xv.at[at, pl.ds(0, TOK)], xsem.at[at]).start()
            pltpu.make_async_copy(xs[1].at[:, cols], xv.at[at, pl.ds(TOK, QTOK)], xsem.at[at]).start()
        else:
            for p in range(8 if nx == 10 else 6):

                @pl.when(s[8 + k] == p)
                def _():
                    if p < 6:
                        pltpu.make_async_copy(xs[p], xv.at[at], xsem.at[at]).start()
                    else:
                        n = ROWS // 2
                        for part in (0, 1):
                            pltpu.make_async_copy(
                                xs[6 + (p - 6) * 2 + part], xv.at[at, pl.ds(part * n, n)], xsem.at[at]
                            ).start()

    @pl.when(i == 0)
    def _():
        for k in range(min(SLOTS - 1, count)):
            start(k)

    for k in range(SLOTS - 1, count):

        @pl.when(i == k - (SLOTS - 1))
        def _():
            start(k)

    for v, sem in ((wv, wsem), (tv, tsem), (xv, xsem)):
        pltpu.make_async_copy(v.at[slot], v.at[slot], sem.at[slot]).wait()

    @pl.when(i == 0)
    def _():
        x = xv[slot]
        wide = jnp.dot(x, wv[slot], preferred_element_type=F32)
        thin = jnp.dot(x, tv[slot], preferred_element_type=F32)
        if begins:
            acc[:, :640] = wide
            acc[:, 640:] = thin
        else:
            acc[:, :640] = before[:, :640] + wide
            acc[:, 640:] = before[:, 640:] + thin

    @pl.when(i != 0)
    def _():
        x = xv[slot]
        acc[:, :640] += jnp.dot(x, wv[slot], preferred_element_type=F32)
        acc[:, 640:] += jnp.dot(x, tv[slot], preferred_element_type=F32)

    @pl.when(i == count - 1)
    def _():
        if not ends:
            out[...] = acc[...]
            return
        for dst, lo, n in ((out_d, 0, TOK), (out_q, TOK, QTOK)):
            rows = slice(lo, lo + n)
            g, u = gated(h[rows, :256].astype(F32), acc[rows, :256], acc[rows, 256:512])
            dst[:, :256] = g
            dst[:, 256:512] = u
            both = acc[rows, 512:640]
            turned = pltpu.roll(both, 64, 1)
            low = lax.broadcasted_iota(jnp.int32, both.shape, 1) < 64
            g, u = gated(h2[rows, 128:].astype(F32), jnp.where(low, both, turned), jnp.where(low, turned, both))
            dst[:, 512:640] = jnp.where(low, g.astype(F32), u.astype(F32)).astype(BF16)
            g, u = gated(h2[rows, :128].astype(F32), acc[rows, 640:768], acc[rows, 768:])
            dst[:, 640:768] = g
            dst[:, 768:] = u


def factors(count, scalars, ws, thins, xs, before=None, hidden=None):
    hbm = pl.BlockSpec(memory_space=pl.ANY)
    whole = lambda v: pl.BlockSpec(v.shape, lambda i, s: (0, 0))
    args = [*ws, *thins, *xs]
    in_specs = [hbm] * len(args)
    if before is not None:
        args.append(before)
        in_specs.append(whole(before))
    if hidden is None:
        out_shape = [jax.ShapeDtypeStruct((ROWS, 896), F32)]
    else:
        args += hidden
        in_specs += [pl.BlockSpec((ROWS, 256), lambda i, s: (0, 0))]
        in_specs += [pl.BlockSpec((ROWS, 256), (lambda i, s: (0, 1)) if hidden[1].shape[1] > 256 else (lambda i, s: (1, 0)))]
        out_shape = [jax.ShapeDtypeStruct((TOK, 896), BF16), jax.ShapeDtypeStruct((QTOK, 896), BF16)]
    return pl.pallas_call(
        functools.partial(factor_kernel, count, len(ws), len(thins), len(xs), before is None, hidden is not None),
        grid_spec=pltpu.PrefetchScalarGridSpec(
            num_scalar_prefetch=1,
            grid=(count,),
            in_specs=in_specs,
            out_specs=[whole(v) for v in out_shape],
            scratch_shapes=[
                pltpu.VMEM((ROWS, 896), F32),
                pltpu.VMEM((SLOTS, BLK, 640), BF16),
                pltpu.VMEM((SLOTS, BLK, 256), BF16),
                pltpu.VMEM((SLOTS, ROWS, BLK), BF16),
                pltpu.SemaphoreType.DMA((SLOTS,)),
                pltpu.SemaphoreType.DMA((SLOTS,)),
                pltpu.SemaphoreType.DMA((SLOTS,)),
            ],
        ),
        out_shape=out_shape,
        compiler_params=pltpu.CompilerParams(vmem_limit_bytes=LIMIT),
        cost_estimate=SMALL,
    )(scalars, *args)


def gram_own_kernel(thin, doc, out, few_out, few, acc):
    k = pl.program_id(0)

    @pl.when(k == 0)
    def _():
        acc[...] = jnp.zeros_like(acc)
        for z in range(4):
            for j in range(32):
                lo = 16 * j
                few[16 * z : 16 * z + 16, 256 * j : 256 * j + 256] = thin[z, lo : lo + 16]
        few_out[...] = few[...]

    q = few[:, pl.ds(pl.multiple_of(k * BLK, BLK), BLK)]
    acc[...] += lax.dot_general(doc[...], q, NT, preferred_element_type=F32)

    @pl.when(k == 7)
    def _():
        out[...] = acc[...].T.astype(BF16)


def gram_own(thin, doc):
    return pl.pallas_call(
        gram_own_kernel,
        grid=(8,),
        in_specs=[
            pl.BlockSpec((4, 512, 256), lambda k: (0, 2, 0)),
            pl.BlockSpec((TOK, BLK), lambda k: (0, k)),
        ],
        out_specs=[pl.BlockSpec((64, TOK), lambda k: (0, 0)), pl.BlockSpec((64, D), lambda k: (0, 0))],
        scratch_shapes=[pltpu.VMEM((64, D), BF16), pltpu.VMEM((TOK, 64), F32)],
        out_shape=[jax.ShapeDtypeStruct((64, TOK), BF16), jax.ShapeDtypeStruct((64, D), BF16)],
        compiler_params=pltpu.CompilerParams(vmem_limit_bytes=LIMIT),
        cost_estimate=SMALL,
    )(thin.reshape(4, THIN, 256), doc)


def gram_near_kernel(s, few, *refs):
    pieces, out = refs[:6], refs[6]
    acc = None
    for p in range(6):
        q = few[:, pl.ds(pl.multiple_of(s[p] * BLK, BLK), BLK)]
        part = lax.dot_general(pieces[p][...], q, NT, preferred_element_type=F32)
        acc = part if acc is None else acc + part
    out[...] = acc


def gram_near(scalars, few, pieces):
    vmem = lambda *shape: pl.BlockSpec(shape, lambda k, s: (0, 0))
    return pl.pallas_call(
        gram_near_kernel,
        grid_spec=pltpu.PrefetchScalarGridSpec(
            num_scalar_prefetch=1,
            grid=(1,),
            in_specs=[vmem(64, D)] + [vmem(TOK, BLK)] * 6,
            out_specs=vmem(TOK, 64),
        ),
        out_shape=jax.ShapeDtypeStruct((TOK, 64), F32),
        compiler_params=pltpu.CompilerParams(vmem_limit_bytes=LIMIT),
        cost_estimate=SMALL,
    )(scalars, few, *pieces)


def gram_far_kernel(s, few, own, part, a0, a1, b0, b1, out, acc):
    acc[...] = part[...]
    half = ROWS // 2
    for p, refs in ((6, (a0, a1)), (7, (b0, b1))):
        q = few[:, pl.ds(pl.multiple_of(s[p] * BLK, BLK), BLK)]
        for ref, lo, hi in ((refs[0], 0, half), (refs[1], half, TOK)):
            acc[lo:hi] += lax.dot_general(ref[...], q, NT, preferred_element_type=F32)
    out[:, pl.ds(pl.multiple_of(s[8] * TOK, TOK), TOK)] = own[...]
    out[:, pl.ds(pl.multiple_of((1 - s[8]) * TOK, TOK), TOK)] = acc[...].T.astype(BF16)


def gram_far(scalars, few, own, part, pieces):
    vmem = lambda *shape: pl.BlockSpec(shape, lambda k, s: (0, 0))
    half = ROWS // 2
    return pl.pallas_call(
        gram_far_kernel,
        grid_spec=pltpu.PrefetchScalarGridSpec(
            num_scalar_prefetch=1,
            grid=(1,),
            in_specs=[vmem(64, D), vmem(64, TOK), vmem(TOK, 64)] + [vmem(half, BLK), vmem(TOK - half, BLK)] * 2,
            out_specs=vmem(64, 2 * TOK),
            scratch_shapes=[pltpu.VMEM((TOK, 64), F32)],
        ),
        out_shape=jax.ShapeDtypeStruct((64, 2 * TOK), BF16),
        compiler_params=pltpu.CompilerParams(vmem_limit_bytes=LIMIT),
        cost_estimate=SMALL,
    )(scalars, few, own, part, *pieces)


def hop(r):
    return jnp.where(r == 0, 0, jnp.where(r == 1, 3, jnp.where(r == 2, 1, 2)))


def score_kernel(flip, s, q, below, above, far0, far1, d_own, d_other, gram, sibling, ids, docs, before, out, f, b, acc):
    r = pl.program_id(0)
    x, y, core, z, ylo = s[0], s[1], s[2], s[3], s[4]

    @pl.when(r == 0)
    def _():
        acc[...] = jnp.zeros_like(acc)
        f[...] = q[...]

    @pl.when(r == 1)
    def _():
        f[...] = below[...]

    @pl.when(r == 2)
    def _():
        f[...] = above[...]

    @pl.when(r == 3)
    def _():
        f[: QTOK // 2] = far0[...]
        f[QTOK // 2 :] = far1[...]

    b[:, pl.ds(pl.multiple_of(ylo * TOK, TOK), TOK)] = lax.dot_general(
        f[...], d_own[...], NT, preferred_element_type=F32
    )
    b[:, pl.ds(pl.multiple_of((1 - ylo) * TOK, TOK), TOK)] = lax.dot_general(
        f[...], d_other[...], NT, preferred_element_type=F32
    )
    sums = [jnp.zeros((8, 2 * TOK), F32) for _ in range(QS)]
    for xr, dx in enumerate(STEPS):
        for yr, dy in enumerate(STEPS):
            if dy % 2 != flip:
                continue
            for cr, a in enumerate((gram, sibling)):
                lo = lax.rem(x + dx + 4, 4) * 64 + lax.rem(y + dy + 4, 4) // 2 * 32 + (core ^ cr) * 16
                lo = pl.multiple_of(lo, 16)
                p = a[xr, yr, 0].astype(F32) * b[pl.ds(lo, 16), :]
                who = ids[pl.ds(lo, 16), :]
                for k in range(QS):
                    t = jnp.where(who == k, p, 0.0)
                    sums[k] = sums[k] + (t[:8] + t[8:])
    group = lax.rem(z + hop(r), 4) * 2 + (ylo ^ flip)
    for k in range(QS):
        acc[pl.ds(group * QS + k, 1), :] = jnp.sum(sums[k], 0, keepdims=True)

    @pl.when(r == 3)
    def _():
        out[...] = before[...] + jnp.dot(
            acc[...], docs[...], preferred_element_type=F32, precision=lax.Precision.HIGHEST
        )


def score_sums(flip, scalars, queries, documents, gram, sibling, ids, docs, before):
    whole = lambda v: pl.BlockSpec(v.shape, lambda r, s: (0, 0))
    planes = pl.BlockSpec((4, 4, 1, 16, 2 * TOK), lambda r, s: (0, 0, lax.rem(s[3] + hop(r), 4), 0, 0))
    return pl.pallas_call(
        functools.partial(score_kernel, flip),
        grid_spec=pltpu.PrefetchScalarGridSpec(
            num_scalar_prefetch=1,
            grid=(4,),
            in_specs=[whole(v) for v in (*queries, *documents)]
            + [planes, planes, pl.BlockSpec((QTOK, 1), lambda r, s: (r, 0)), whole(docs), whole(before)],
            out_specs=whole(before),
            scratch_shapes=[
                pltpu.VMEM((QTOK, 896), BF16),
                pltpu.VMEM((QTOK, 2 * TOK), F32),
                pltpu.VMEM((8 * QS, 2 * TOK), F32),
            ],
        ),
        out_shape=jax.ShapeDtypeStruct(before.shape, F32),
        compiler_params=pltpu.CompilerParams(vmem_limit_bytes=LIMIT),
        cost_estimate=SMALL,
    )(scalars, *queries, *documents, gram, sibling, ids, docs, before)


def local(doc_inputs, doc_grads, query_inputs, query_grads, gate_weight, up_weight, doc_ids, query_ids):
    dp = lax.axis_index("dp")
    tensor = lax.axis_index("tensor")
    z, ylo = dp // 2, dp % 2
    x, yhi, core = tensor // 4, (tensor // 2) % 2, tensor % 2
    y = yhi * 2 + ylo
    ints = lambda *vs: jnp.stack([jnp.asarray(v, jnp.int32) for v in vs])

    def scalars(blocks):
        blocks = ints(*blocks)
        turn = (blocks // 2 - x + 4) % 4
        at = jnp.where(turn == 0, 0, jnp.where(turn == 3, 1, jnp.where(turn == 1, 2, 3)))
        which_x = at * 2 + ((blocks % 2) ^ core)
        turn = (blocks // 2 - z + 4) % 4
        flip = (blocks % 2) ^ ylo
        which_w = jnp.where(
            turn == 2, 6 + flip, flip * 3 + jnp.where(turn == 0, 0, jnp.where(turn == 3, 1, 2))
        )
        spare = jnp.zeros((8 - blocks.shape[0],), jnp.int32)
        return jnp.concatenate([blocks, spare, which_x, spare, which_w, spare, ints(ylo)]).astype(jnp.int32)

    first = scalars([(z + dz + 4) % 4 * 2 + ylo for dz in (0, -1, 1)])
    second = scalars([(z + dz + 4) % 4 * 2 + (ylo ^ 1) for dz in (0, -1, 1)])
    last = scalars([(z + 2) % 4 * 2 + flip for flip in (0, 1)])
    late = (z + 2) % 4, jnp.where(x == z, (z + 3) % 4, (x + 2) % 4)
    free = [jnp.logical_and(late[0] != v, late[1] != v) for v in range(4)]
    soon = jnp.where(free[0], 0, jnp.where(free[1], 1, 2)), jnp.where(free[3], 3, jnp.where(free[2], 2, 1))
    blocks_of = lambda zs: [v * 2 + flip for v in zs for flip in (0, 1)]
    soon, late = scalars(blocks_of(soon)), scalars(blocks_of(late))
    columns = ints(*[(x + dx + 4) % 4 * 2 + (core ^ c) for dx in STEPS for c in (0, 1)], ylo)
    where = ints(x, y, core, z, ylo)

    keep0, keep1, give0, give1, piece = pack(
        ints(ylo, x * 2 + core, tensor), gate_weight, up_weight, doc_inputs, query_inputs
    )
    thin_a = lax.all_gather(keep1, AX, axis_index_groups=ZGROUPS, axis=0, tiled=True)
    a_below, a_above = send(keep0, ZP), send(keep0, ZM)
    got0 = send(give0, PARTNER)
    piece = send(piece, OTHER)
    mine, give1 = pack_grads(ints(ylo), doc_grads, query_grads, give1)
    got1 = send(give1, PARTNER)
    order = jnp.stack([(z + dz + 4) % 4 * 2 + (ylo ^ flip) for flip in (0, 1) for dz in STEPS])
    ids = query_ids[order].reshape(-1, 1)
    got0, piece, a_below, a_above, got1, ids, first, second, last, soon, late, columns, where = tie(
        got0, piece, a_below, a_above, got1, ids, first, second, last, soon, late, columns, where
    )
    thin_b = lax.all_gather(got1[2 * ROWS :], AX, axis_index_groups=ZGROUPS, axis=0, tiled=True)
    b_below, b_above = send(got0, ZP), send(got0, ZM)
    x_below, x_above = send(piece, XP), send(piece, XM)
    own = (doc_inputs, query_inputs)
    a_w = [keep0, a_below, a_above]
    (own_part,) = factors(3, first, a_w, [thin_a], own)
    gram_mine, few = gram_own(thin_a, doc_inputs)
    piece_too = send(piece, CORE)
    other_ids = send(doc_ids, PARTNER)
    b_below, b_above, x_below, x_above, thin_b, piece_too, other_ids, own_part, gram_mine, few = tie(
        b_below, b_above, x_below, x_above, thin_b, piece_too, other_ids, own_part, gram_mine, few
    )
    thins = [thin_a, thin_b]
    far0, far1, x_far0, x_far1 = halves(a_below, b_below, a_above, b_above, x_below, x_above)
    far0, far1 = send(far0, ZP), send(far1, ZM)
    x_far0, x_far1 = send(x_far0, XP), send(x_far1, XM)
    near_x = [piece, piece_too, x_below, send(x_below, CORE), x_above, send(x_above, CORE)]
    both = jnp.where(
        ylo == 0, jnp.concatenate([doc_ids, other_ids + DOCS], 1), jnp.concatenate([other_ids, doc_ids + DOCS], 1)
    )[0]
    docs = (both[:, None] == jnp.arange(2 * DOCS, dtype=jnp.int32)[None, :]).astype(F32)
    near_w = [*a_w, got0, b_below, b_above]
    (own_part,) = factors(3, second, near_w, thins, own, own_part)
    (other_part,) = factors(4, soon, near_w, thins, near_x)
    gram_part = gram_near(columns, few, near_x)
    x_far0, x_far1, far0, far1, own_part, other_part, gram_part, docs = tie(
        x_far0, x_far1, far0, far1, own_part, other_part, gram_part, docs
    )
    all_w = [*near_w, far0, far1]
    far_x = [x_far0, x_far1, send(x_far0, CORE), send(x_far1, CORE)]

    gram = gram_far(columns, few, gram_mine, gram_part, far_x)
    gram, own_part = tie(gram, own_part)
    plane = direct(gram, YP, YM, Y2)
    d_own, q_own = factors(2, last, all_w, thins, own, own_part, (mine, mine))
    q_own, gram, other_part, *plane = tie(q_own, gram, other_part, *plane)
    q_below, q_above = send(q_own, ZP), send(q_own, ZM)
    gram = jnp.concatenate([gram, *plane], 0)
    planes = direct(gram, XP, XM, X2)
    d_other, q_other = factors(4, late, all_w, thins, [*near_x, *far_x], other_part, (got1, got1))
    q_other, d_other, q_below, q_above, gram, *planes = tie(q_other, d_other, q_below, q_above, gram, *planes)
    h = QTOK // 2
    q_own = (q_own, q_below, q_above, send(q_below[:h], ZP), send(q_above[h:], ZM))
    q_other = (q_other, *ring(q_other, ZP, ZM))
    gram = jnp.concatenate([gram, *planes], 0).reshape(4, 4, 4, 16, 2 * TOK)
    sibling = send(gram, CORE)

    scores = jnp.zeros((8 * QS, 2 * DOCS), F32)
    for flip, queries in ((0, q_own), (1, q_other)):
        part = ids[flip * 4 * QTOK : (flip + 1) * 4 * QTOK]
        scores = score_sums(flip, where, queries, (d_own, d_other), gram, sibling, part, docs, scores)

    for p in (CORE, X1, XX, Y1, YY):
        scores = scores + send(scores, p)
    scores = jnp.where(ylo == 0, scores[:, :DOCS], scores[:, DOCS:]).T / math.sqrt(D * FF)
    return scores[None]


def solution(mesh):
    placed = (
        P("dp", None),
        P("dp", "tensor"),
        P("dp", None),
        P("dp", "tensor"),
        P("dp", "tensor"),
        P("dp", "tensor"),
        P("dp", None),
        P(),
    )
    return jax.shard_map(
        local, mesh=mesh, in_specs=placed, out_specs=P("dp", None, None), check_vma=False
    )
```

```python
import functools
import math

import jax
import jax.numpy as jnp
from jax import lax
from jax.experimental import pallas as pl
from jax.experimental.pallas import tpu as pltpu
from jax.sharding import PartitionSpec as P

D = 8192
FF = 14336
DOCS = 4
QS = 4
TOK = 512
QTOK = 256
ROWS = TOK + QTOK
BLK = D // 8
THIN = BLK + 512
AX = ("dp", "tensor")
F32 = jnp.float32
BF16 = jnp.bfloat16


def place(z, y, x, c):
    return ((z % 4) * 2 + (y % 2)) * 16 + (x % 4) * 4 + ((y % 4) // 2) * 2 + c


def perm(fn):
    return [
        (place(z, y, x, c), place(*fn(z, y, x, c)))
        for z in range(4)
        for y in range(4)
        for x in range(4)
        for c in range(2)
    ]


ZP = perm(lambda z, y, x, c: (z + 1, y, x, c))
ZM = perm(lambda z, y, x, c: (z - 1, y, x, c))
XP = perm(lambda z, y, x, c: (z, y, x + 1, c))
XM = perm(lambda z, y, x, c: (z, y, x - 1, c))
PARTNER = perm(lambda z, y, x, c: (z, y ^ 1, x, c))
OTHER = perm(lambda z, y, x, c: (z, (3 - y) % 4, x, c))
CORE = perm(lambda z, y, x, c: (z, y, x, 1 - c))
X1 = perm(lambda z, y, x, c: (z, y, x ^ 1, c))
X3 = perm(lambda z, y, x, c: (z, y, 3 - x, c))
STEPS = (0, -1, 1, 2)
LIMIT = 56 << 20
SLOTS = 3
SMALL = pl.CostEstimate(flops=1 << 10, bytes_accessed=1 << 10, transcendentals=0)
PLANES = [[place(z, y, x, c) for x in range(4) for y in range(4) for c in range(2)] for z in range(4)]
ZGROUPS = [[place(z, y, x, c) for z in range(4)] for y in range(4) for x in range(4) for c in range(2)]
NT = (((1,), (1,)), ((), ()))


def send(v, p):
    return lax.ppermute(v, AX, p)


def tie(*vs):
    return lax.optimization_barrier(vs)


def pack_kernel(s, gate, up, doc, query, some, keep0, keep1, give0, give1, piece):
    i = pl.program_id(0)
    ylo = s[0]
    rows = gate.shape[0]
    gh, uh = gate[:, 384:512].astype(F32), up[:, 384:512].astype(F32)
    gt, ut = pltpu.roll(gh, 64, 1), pltpu.roll(uh, 64, 1)
    low = lax.broadcasted_iota(jnp.int32, gh.shape, 1) < 64
    first = jnp.where(low, gh, ut)
    second = jnp.where(low, gt, uh)
    for half, wide, thin, at in ((ylo, keep0, keep1, pl.ds(i * rows, rows)), (1 - ylo, give0, give1, slice(None))):
        base = pl.multiple_of(half * 512, 128)
        wide[:, :256] = gate[:, pl.ds(base, 256)]
        wide[:, 256:512] = up[:, pl.ds(base, 256)]
        wide[:, 512:] = jnp.where(half == 0, first, second).astype(BF16)
        base = pl.multiple_of(half * 512 + 256, 128)
        thin[at, :128] = gate[:, pl.ds(base, 128)]
        thin[at, 128:] = up[:, pl.ds(base, 128)]
    piece[pl.ds(i * doc.shape[0], doc.shape[0])] = doc[...]
    piece[pl.ds(TOK + i * query.shape[0], query.shape[0])] = query[...]

    @pl.when(i == 0)
    def _():
        for j in range(32):
            keep1[BLK + 16 * j : BLK + 16 * j + 16] = some[:, 256 * j : 256 * j + 256]


def pack(scalars, gate, up, doc, query):
    steps = 4
    rows = BLK // steps
    spec = lambda n: pl.BlockSpec((rows, n), lambda i, s: (i, 0))
    whole = lambda *shape: pl.BlockSpec(shape, lambda i, s: (0, 0))
    shape = lambda r, n: jax.ShapeDtypeStruct((r, n), BF16)
    return pl.pallas_call(
        pack_kernel,
        grid_spec=pltpu.PrefetchScalarGridSpec(
            num_scalar_prefetch=1,
            grid=(steps,),
            in_specs=[
                spec(896),
                spec(896),
                pl.BlockSpec((TOK // steps, BLK), lambda i, s: (i, s[1])),
                pl.BlockSpec((QTOK // steps, BLK), lambda i, s: (i, s[1])),
                pl.BlockSpec((16, D), lambda i, s: (s[2], 0)),
            ],
            out_specs=[spec(640), whole(THIN, 256), spec(640), spec(256), whole(ROWS, BLK)],
        ),
        out_shape=[shape(BLK, 640), shape(THIN, 256), shape(BLK, 640), shape(BLK, 256), shape(ROWS, BLK)],
        compiler_params=pltpu.CompilerParams(vmem_limit_bytes=LIMIT),
        cost_estimate=SMALL,
    )(scalars, gate, up, doc, query, query)


def pack_grads_kernel(ylo_ref, doc, query, ids, keep, give):
    ylo = ylo_ref[0]
    give[ROWS:] = jnp.broadcast_to(ids[...].astype(F32), (16, TOK)).astype(BF16)
    for src, lo, n in ((doc, 0, TOK), (query, TOK, QTOK)):
        h = src[:, 384:512].astype(F32)
        t = pltpu.roll(h, 64, 1)
        low = lax.broadcasted_iota(jnp.int32, h.shape, 1) < 64
        first, second = jnp.where(low, h, t), jnp.where(low, t, h)
        for s, out in ((ylo, keep), (1 - ylo, give)):
            out[lo : lo + n, :384] = src[:, pl.ds(pl.multiple_of(s * 512, 128), 384)]
            out[lo : lo + n, 384:] = jnp.where(s == 0, first, second).astype(BF16)


def pack_grads(ylo, doc, query, ids):
    vmem = pl.BlockSpec(memory_space=pltpu.VMEM)
    return pl.pallas_call(
        pack_grads_kernel,
        in_specs=[pl.BlockSpec(memory_space=pltpu.SMEM), vmem, vmem, vmem],
        out_specs=[vmem, vmem],
        out_shape=[jax.ShapeDtypeStruct((ROWS, 512), BF16), jax.ShapeDtypeStruct((ROWS + 16, 512), BF16)],
        compiler_params=pltpu.CompilerParams(vmem_limit_bytes=LIMIT),
        cost_estimate=SMALL,
    )(ylo, doc, query, ids)


def halves_kernel(a_below, b_below, a_above, b_above, x_below, x_above, far0, far1, x_far0, x_far1):
    n = BLK // 2
    for src, lo, out, at in ((a_below, 0, far0, 0), (b_below, 0, far0, n), (a_above, n, far1, 0), (b_above, n, far1, n)):
        out[at : at + n] = src[...]
    x_far0[...] = x_below[...]
    x_far1[...] = x_above[...]


def halves(a_below, b_below, a_above, b_above, x_below, x_above):
    spec = lambda rows, n, at: pl.BlockSpec((rows, n), lambda i: (at, 0))
    n, m = BLK // 2, ROWS // 2
    return pl.pallas_call(
        halves_kernel,
        grid=(1,),
        in_specs=[spec(n, 640, 0)] * 2 + [spec(n, 640, 1)] * 2 + [spec(m, BLK, 0), spec(m, BLK, 1)],
        out_specs=[spec(BLK, 640, 0)] * 2 + [spec(m, BLK, 0)] * 2,
        out_shape=[jax.ShapeDtypeStruct((BLK, 640), BF16)] * 2 + [jax.ShapeDtypeStruct((m, BLK), BF16)] * 2,
        compiler_params=pltpu.CompilerParams(vmem_limit_bytes=LIMIT),
        cost_estimate=SMALL,
    )(a_below, b_below, a_above, b_above, x_below, x_above)


def gated(hidden, gate, up):
    s = jax.nn.sigmoid(gate)
    up_factor = (hidden * gate * s).astype(BF16)
    gate_factor = (hidden * up * s * (1.0 + gate * (1.0 - s))).astype(BF16)
    return gate_factor, up_factor


def factor_kernel(phases, m, row, nw, nt, nx, s, *refs):
    def take(n):
        nonlocal refs
        got, refs = refs[:n], refs[n:]
        return got

    ends = phases[0][3]
    ws, thins, own_x, other_x = take(nw), take(nt), take(2), take(nx)
    befores = [None if begins else take(1)[0] for _, _, begins, _ in phases]
    hidden = [take(1)[0] for _ in phases] if ends else None
    outs = take(1 if ends else len(phases))
    acc, wv, tv, xv, wsem, tsem, xsem, bsem, osem = refs
    i = pl.program_id(0)
    slot = lax.rem(i, SLOTS)
    steps = [(p, k) for p, phase in enumerate(phases) for k in range(phase[1])]
    firsts = [sum(phase[1] for phase in phases[:p]) for p in range(len(phases) + 1)]
    half = ROWS // 2

    def start(g):
        p, k = steps[g]
        at = g % SLOTS
        base = 32 * p
        block = s[base + k]
        for w in range(nw):

            @pl.when(s[base + 16 + k] == w)
            def _():
                if w < 6:
                    pltpu.make_async_copy(ws[w], wv.at[at], wsem.at[at]).start()
                else:
                    n = BLK // 2
                    rows = pl.ds((w - 6) * n, n)
                    pltpu.make_async_copy(ws[6].at[rows], wv.at[at, pl.ds(0, n)], wsem.at[at]).start()
                    pltpu.make_async_copy(ws[7].at[rows], wv.at[at, pl.ds(n, n)], wsem.at[at]).start()

        for flip in range(nt):
            rows = pl.ds(pl.multiple_of(block // 2 * (BLK if flip else THIN), 512), BLK)

            @pl.when(lax.rem(block, 2) == (s[base + 24] ^ flip))
            def _():
                pltpu.make_async_copy(thins[flip].at[rows], tv.at[at], tsem.at[at]).start()

        if phases[p][0] == "own":
            cols = pl.ds(pl.multiple_of(block * BLK, BLK), BLK)
            for x, lo, n in ((own_x[0], 0, TOK), (own_x[1], TOK, QTOK)):
                if row <= lo < row + m:
                    pltpu.make_async_copy(x.at[:, cols], xv.at[at, pl.ds(lo - row, n)], xsem.at[at]).start()
        else:
            for q in range(min(nx, 8)):

                @pl.when(s[base + 8 + k] == q)
                def _():
                    if q < 6:
                        pltpu.make_async_copy(other_x[q].at[pl.ds(row, m)], xv.at[at], xsem.at[at]).start()
                    else:
                        for part in (0, 1):
                            lo = max(row, part * half)
                            hi = min(row + m, part * half + half)
                            if lo < hi:
                                pltpu.make_async_copy(
                                    other_x[6 + (q - 6) * 2 + part].at[pl.ds(lo - part * half, hi - lo)],
                                    xv.at[at, pl.ds(lo - row, hi - lo)],
                                    xsem.at[at],
                                ).start()

    @pl.when(i == 0)
    def _():
        start(0)
        if befores[0] is not None:
            pltpu.make_async_copy(befores[0].at[pl.ds(row, m)], acc.at[0], bsem.at[0]).start()

    for v, sem in ((wv, wsem), (tv, tsem), (xv, xsem)):
        pltpu.make_async_copy(v.at[slot], v.at[slot], sem.at[slot]).wait()

    for g in range(1, len(steps)):

        @pl.when(i == max(g - (SLOTS - 1), 0))
        def _():
            start(g)

    for p, before in enumerate(befores):
        if p and before is not None:

            @pl.when(i == 0)
            def _():
                pltpu.make_async_copy(before.at[pl.ds(row, m)], acc.at[p], bsem.at[p]).start()

    for p, before in enumerate(befores):

        @pl.when(i == firsts[p])
        def _():
            if before is None:
                acc[p] = jnp.zeros((m, 896), F32)
            else:
                pltpu.make_async_copy(before.at[pl.ds(row, m)], acc.at[p], bsem.at[p]).wait()

    now = jnp.where(i >= firsts[1], 1, 0) if len(phases) > 1 else 0
    x = xv[slot]
    acc[now, :, :640] += jnp.dot(x, wv[slot], preferred_element_type=F32)
    acc[now, :, 640:] += jnp.dot(x, tv[slot], preferred_element_type=F32)

    if ends:
        for p in range(len(phases)):

            @pl.when(i == firsts[p + 1] - 1)
            def _():
                h, dst = hidden[p], outs[0]
                rows, to = slice(row, row + m), slice(p * m, p * m + m)
                g, u = gated(h[rows, :256].astype(F32), acc[p, :, :256], acc[p, :, 256:512])
                dst[to, :256] = g
                dst[to, 256:512] = u
                both = acc[p, :, 512:640]
                turned = pltpu.roll(both, 64, 1)
                low = lax.broadcasted_iota(jnp.int32, both.shape, 1) < 64
                g, u = gated(h[rows, 384:].astype(F32), jnp.where(low, both, turned), jnp.where(low, turned, both))
                dst[to, 512:640] = jnp.where(low, g.astype(F32), u.astype(F32)).astype(BF16)
                g, u = gated(h[rows, 256:384].astype(F32), acc[p, :, 640:768], acc[p, :, 768:])
                dst[to, 640:768] = g
                dst[to, 768:] = u

    else:
        copy = lambda p: pltpu.make_async_copy(acc.at[p], outs[p], osem.at[p])
        for p in range(len(phases)):

            @pl.when(i == firsts[p + 1] - 1)
            def _():
                copy(p).start()

        @pl.when(i == len(steps) - 1)
        def _():
            for p in range(len(phases)):
                copy(p).wait()


def factors(phases, scalars, ws, thins, own, other=(), befores=(), hidden=(), rows=(0, ROWS)):
    row, m = rows
    ends = phases[0][3]
    hbm = pl.BlockSpec(memory_space=pl.ANY)
    whole = lambda v: pl.BlockSpec(v.shape, lambda i, s: (0, 0))
    args = [*ws, *thins, *own, *other, *befores]
    in_specs = [hbm] * len(args) + [whole(h) for h in hidden]
    if ends:
        out_shape = [jax.ShapeDtypeStruct((len(phases) * m, 896), BF16)]
        out_specs = [whole(out_shape[0])]
    else:
        out_shape = [jax.ShapeDtypeStruct((m, 896), F32)] * len(phases)
        out_specs = [hbm] * len(phases)
    count = sum(phase[1] for phase in phases)
    return pl.pallas_call(
        functools.partial(factor_kernel, phases, m, row, len(ws), len(thins), len(other)),
        grid_spec=pltpu.PrefetchScalarGridSpec(
            num_scalar_prefetch=1,
            grid=(count,),
            in_specs=in_specs,
            out_specs=out_specs,
            scratch_shapes=[
                pltpu.VMEM((len(phases), m, 896), F32),
                pltpu.VMEM((SLOTS, BLK, 640), BF16),
                pltpu.VMEM((SLOTS, BLK, 256), BF16),
                pltpu.VMEM((SLOTS, m, BLK), BF16),
                pltpu.SemaphoreType.DMA((SLOTS,)),
                pltpu.SemaphoreType.DMA((SLOTS,)),
                pltpu.SemaphoreType.DMA((SLOTS,)),
                pltpu.SemaphoreType.DMA((len(phases),)),
                pltpu.SemaphoreType.DMA((len(phases),)),
            ],
        ),
        out_shape=out_shape,
        compiler_params=pltpu.CompilerParams(vmem_limit_bytes=LIMIT),
        cost_estimate=SMALL,
    )(scalars, *args, *hidden)


def gram_own_kernel(thin, doc, out, few_out, few, acc):
    k = pl.program_id(0)

    @pl.when(k == 0)
    def _():
        acc[...] = jnp.zeros_like(acc)
        for z in range(4):
            for j in range(32):
                lo = 16 * j
                few[16 * z : 16 * z + 16, 256 * j : 256 * j + 256] = thin[z, lo : lo + 16]
        few_out[...] = few[...]

    q = few[:, pl.ds(pl.multiple_of(k * BLK, BLK), BLK)]
    acc[...] += lax.dot_general(doc[...], q, NT, preferred_element_type=F32)

    @pl.when(k == 7)
    def _():
        out[...] = acc[...].T.astype(BF16)


def gram_own(thin, doc):
    return pl.pallas_call(
        gram_own_kernel,
        grid=(8,),
        in_specs=[
            pl.BlockSpec((4, 512, 256), lambda k: (0, 2, 0)),
            pl.BlockSpec((TOK, BLK), lambda k: (0, k)),
        ],
        out_specs=[pl.BlockSpec((64, TOK), lambda k: (0, 0)), pl.BlockSpec((64, D), lambda k: (0, 0))],
        scratch_shapes=[pltpu.VMEM((64, D), BF16), pltpu.VMEM((TOK, 64), F32)],
        out_shape=[jax.ShapeDtypeStruct((64, TOK), BF16), jax.ShapeDtypeStruct((64, D), BF16)],
        compiler_params=pltpu.CompilerParams(vmem_limit_bytes=LIMIT),
        cost_estimate=SMALL,
    )(thin.reshape(4, THIN, 256), doc)


def gram_other_kernel(few, doc, out, acc):
    k = pl.program_id(0)

    @pl.when(k == 0)
    def _():
        acc[...] = jnp.zeros_like(acc)

    acc[...] += lax.dot_general(doc[...], few[...], NT, preferred_element_type=F32)

    @pl.when(k == 7)
    def _():
        out[...] = acc[...].T.astype(BF16)


def gram_other(few, doc):
    return pl.pallas_call(
        gram_other_kernel,
        grid=(8,),
        in_specs=[pl.BlockSpec((64, BLK), lambda k: (0, k)), pl.BlockSpec((TOK, BLK), lambda k: (0, k))],
        out_specs=pl.BlockSpec((64, TOK), lambda k: (0, 0)),
        scratch_shapes=[pltpu.VMEM((TOK, 64), F32)],
        out_shape=jax.ShapeDtypeStruct((64, TOK), BF16),
        compiler_params=pltpu.CompilerParams(vmem_limit_bytes=LIMIT),
        cost_estimate=SMALL,
    )(few, doc)


def hop(r):
    return jnp.where(r == 0, 0, jnp.where(r == 1, 3, jnp.where(r == 2, 1, 2)))


def score_kernel(first, count, s, *refs):
    qs, (d, gram, ids, docs, before, out, f, b, acc) = refs[:count], refs[count:]
    i = pl.program_id(0)
    r = first + i
    z, ylo = s[0], s[1]

    @pl.when(i == 0)
    def _():
        acc[...] = jnp.zeros_like(acc)

    if first == 3:
        f[:QTOK] = qs[0][...]
        f[QTOK:] = qs[1][...]
    else:
        for n in range(count):

            @pl.when(i == n)
            def _():
                f[...] = qs[n][...]

    for flip in (0, 1):
        b[...] = lax.dot_general(f[flip * QTOK : flip * QTOK + QTOK], d[...], NT, preferred_element_type=F32)
        sums = [[jnp.zeros((8, TOK), F32) for _ in range(QS)] for _ in (0, 1)]
        for y in range(4):
            whose = ylo ^ (y % 2)
            docs_at = pl.ds(pl.multiple_of(whose * TOK, TOK), TOK)
            for x in range(4):
                for core in range(2):
                    lo = x * 64 + y // 2 * 32 + core * 16
                    p = gram[x, y, core, whose ^ flip, 0].astype(F32) * b[lo : lo + 16, docs_at]
                    who = ids[flip * QTOK + lo : flip * QTOK + lo + 16, :]
                    for k in range(QS):
                        t = jnp.where(who == k, p, 0.0)
                        sums[y % 2][k] = sums[y % 2][k] + (t[:8] + t[8:])
        group = lax.rem(z + hop(r), 4) * 2 + (ylo ^ flip)
        for k in range(QS):
            for y in (0, 1):
                at = slice(y * TOK, y * TOK + TOK)
                acc[pl.ds(group * QS + k, 1), at] = jnp.sum(sums[y][k], 0, keepdims=True)

    @pl.when(i == pl.num_programs(0) - 1)
    def _():
        out[...] = before[...] + jnp.dot(
            acc[...], docs[...], preferred_element_type=F32, precision=lax.Precision.HIGHEST
        )


def score_sums(first, scalars, queries, documents, gram, ids, docs, before):
    whole = lambda v: pl.BlockSpec(v.shape, lambda r, s: (0, 0))
    planes = pl.BlockSpec((4, 4, 2, 2, 1, 16, TOK), lambda r, s: (0, 0, 0, 0, lax.rem(s[0] + hop(first + r), 4), 0, 0))
    return pl.pallas_call(
        functools.partial(score_kernel, first, len(queries)),
        grid_spec=pltpu.PrefetchScalarGridSpec(
            num_scalar_prefetch=1,
            grid=(1 if first == 3 else len(queries),),
            in_specs=[whole(v) for v in (*queries, documents)]
            + [planes, pl.BlockSpec((2 * QTOK, 1), lambda r, s: (first + r, 0)), whole(docs), whole(before)],
            out_specs=whole(before),
            scratch_shapes=[
                pltpu.VMEM((2 * QTOK, 896), BF16),
                pltpu.VMEM((QTOK, 2 * TOK), F32),
                pltpu.VMEM((8 * QS, 2 * TOK), F32),
            ],
        ),
        out_shape=jax.ShapeDtypeStruct(before.shape, F32),
        compiler_params=pltpu.CompilerParams(vmem_limit_bytes=LIMIT),
        cost_estimate=SMALL,
    )(scalars, *queries, documents, gram, ids, docs, before)


def local(doc_inputs, doc_grads, query_inputs, query_grads, gate_weight, up_weight, doc_ids, query_ids):
    dp = lax.axis_index("dp")
    tensor = lax.axis_index("tensor")
    z, ylo = dp // 2, dp % 2
    x, core = tensor // 4, tensor % 2
    ints = lambda *vs: jnp.stack([jnp.asarray(v, jnp.int32) for v in vs])

    def scalars(blocks):
        blocks = ints(*blocks)
        turn = (blocks // 2 - x + 4) % 4
        at = jnp.where(turn == 0, 0, jnp.where(turn == 3, 1, jnp.where(turn == 1, 2, 3)))
        which_x = at * 2 + ((blocks % 2) ^ core)
        turn = (blocks // 2 - z + 4) % 4
        flip = (blocks % 2) ^ ylo
        which_w = jnp.where(
            turn == 2, 6 + flip, flip * 3 + jnp.where(turn == 0, 0, jnp.where(turn == 3, 1, 2))
        )
        spare = jnp.zeros((8 - blocks.shape[0],), jnp.int32)
        last = jnp.full((8,), ylo)
        return jnp.concatenate([blocks, spare, which_x, spare, which_w, spare, last]).astype(jnp.int32)

    first = scalars([(z + dz + 4) % 4 * 2 + ylo for dz in (0, -1, 1)])
    second = scalars([(z + dz + 4) % 4 * 2 + (ylo ^ 1) for dz in (0, -1, 1)])
    last = scalars([(z + 2) % 4 * 2 + flip for flip in (0, 1)])
    late = (z + 2) % 4, jnp.where(x == z, (z + 3) % 4, (x + 2) % 4)
    free = [jnp.logical_and(late[0] != v, late[1] != v) for v in range(4)]
    soon = jnp.where(free[0], 0, jnp.where(free[1], 1, 2)), jnp.where(free[3], 3, jnp.where(free[2], 2, 1))
    blocks_of = lambda zs: [v * 2 + flip for v in zs for flip in (0, 1)]
    early = jnp.concatenate([second, scalars(blocks_of(soon))])
    late = jnp.concatenate([last, scalars(blocks_of(late))])
    where = ints(z, ylo)

    keep0, keep1, give0, give1, piece = pack(
        ints(ylo, x * 2 + core, tensor), gate_weight, up_weight, doc_inputs, query_inputs
    )
    thin_a = lax.all_gather(keep1, AX, axis_index_groups=ZGROUPS, axis=0, tiled=True)
    a_below, a_above = send(keep0, ZP), send(keep0, ZM)
    got0 = send(give0, PARTNER)
    piece = send(piece, OTHER)
    got1 = send(give1, PARTNER)
    mine, theirs = pack_grads(ints(ylo), doc_grads, query_grads, doc_ids)
    order = jnp.stack([(z + dz + 4) % 4 * 2 + (ylo ^ flip) for dz in STEPS for flip in (0, 1)])
    ids = query_ids[order].reshape(-1, 1)
    got0, piece, a_below, a_above, got1, ids, first, early, late, where, mine, theirs = tie(
        got0, piece, a_below, a_above, got1, ids, first, early, late, where, mine, theirs
    )
    thin_b = lax.all_gather(got1, AX, axis_index_groups=ZGROUPS, axis=0, tiled=True)
    b_below, b_above = send(got0, ZP), send(got0, ZM)
    x_below, x_above = send(piece, XP), send(piece, XM)
    own = (doc_inputs, query_inputs)
    a_w = [keep0, a_below, a_above]
    (own_part,) = factors((("own", 3, True, False),), first, a_w, [thin_a], own)
    gram_mine, few = gram_own(thin_a, doc_inputs)
    theirs = send(theirs, PARTNER)
    theirs, few = tie(theirs, few)
    few = send(few, PARTNER)
    b_below, b_above, x_below, x_above, piece, thin_b, own_part, gram_mine, few = tie(
        b_below, b_above, x_below, x_above, piece, thin_b, own_part, gram_mine, few
    )
    thins = [thin_a, thin_b]
    far0, far1, x_far0, x_far1 = halves(a_below, b_below, a_above, b_above, x_below, x_above)
    far0, far1, few = tie(far0, far1, few)
    far0, far1 = send(far0, ZP), send(far1, ZM)
    piece_too, x_below_too, x_above_too = send(piece, CORE), send(x_below, CORE), send(x_above, CORE)
    piece_too, x_below_too, x_above_too, x_far0, x_far1 = tie(piece_too, x_below_too, x_above_too, x_far0, x_far1)
    x_far0, x_far1 = send(x_far0, XP), send(x_far1, XM)
    near_x = [piece, piece_too, x_below, x_below_too, x_above, x_above_too]
    near_w = [*a_w, got0, b_below, b_above]
    own_part, other_part = factors(
        (("own", 3, False, False), ("other", 4, True, False)), early, near_w, thins, own, near_x, [own_part]
    )
    gram = jnp.concatenate([gram_mine, gram_other(few, doc_inputs)], 0)
    gram = lax.all_gather(gram, AX, axis_index_groups=PLANES, axis=0, tiled=True).reshape(4, 4, 2, 2, 4, 16, TOK)
    other_ids = theirs[ROWS : ROWS + 1].astype(jnp.int32)
    both = jnp.where(
        ylo == 0, jnp.concatenate([doc_ids, other_ids + DOCS], 1), jnp.concatenate([other_ids, doc_ids + DOCS], 1)
    )[0]
    docs = (both[:, None] == jnp.arange(2 * DOCS, dtype=jnp.int32)[None, :]).astype(F32)
    x_far0, x_far1, far0, far1, own_part, other_part, docs = tie(x_far0, x_far1, far0, far1, own_part, other_part, docs)
    all_w = [*near_w, far0, far1]
    all_x = [*near_x, x_far0, x_far1, send(x_far0, CORE), send(x_far1, CORE)]

    rest = (("own", 2, False, True), ("other", 4, False, True))
    parts, grads = (own_part, other_part), (mine, theirs)
    (q,) = factors(rest, late, all_w, thins, own, all_x, parts, grads, (TOK, QTOK))
    q, own_part = tie(q, own_part)
    q_below, q_above = send(q, ZP), send(q, ZM)
    (d,) = factors(rest, late, all_w, thins, own, all_x, (own_part, other_part), grads, (0, TOK))
    q_below, q_above, d = tie(q_below, q_above, d)
    q_far0, q_far1 = send(q_below[:QTOK], ZP), send(q_above[QTOK:], ZM)

    scores = jnp.zeros((8 * QS, 2 * DOCS), F32)
    scores = score_sums(0, where, (q, q_below, q_above), d, gram, ids, docs, scores)
    scores = score_sums(3, where, (q_far0, q_far1), d, gram, ids, docs, scores)

    for p in (CORE, X1, X3, PARTNER, OTHER):
        scores = scores + send(scores, p)
    scores = jnp.where(ylo == 0, scores[:, :DOCS], scores[:, DOCS:]).T / math.sqrt(D * FF)
    return scores[None]


def solution(mesh):
    placed = (
        P("dp", None),
        P("dp", "tensor"),
        P("dp", None),
        P("dp", "tensor"),
        P("dp", "tensor"),
        P("dp", "tensor"),
        P("dp", None),
        P(),
    )
    return jax.shard_map(
        local, mesh=mesh, in_specs=placed, out_specs=P("dp", None, None), check_vma=False
    )
```

```python
import functools
import math

import jax
import jax.numpy as jnp
from jax import lax
from jax.experimental import pallas as pl
from jax.experimental.pallas import tpu as pltpu
from jax.sharding import PartitionSpec as P

D = 8192
FF = 14336
DOCS = 4
QS = 4
TOK = 512
QTOK = 256
ROWS = TOK + QTOK
BLK = D // 8
THIN = BLK + 512
AX = ("dp", "tensor")
F32 = jnp.float32
BF16 = jnp.bfloat16


def place(z, y, x, c):
    return ((z % 4) * 2 + (y % 2)) * 16 + (x % 4) * 4 + ((y % 4) // 2) * 2 + c


def perm(fn):
    return [
        (place(z, y, x, c), place(*fn(z, y, x, c)))
        for z in range(4)
        for y in range(4)
        for x in range(4)
        for c in range(2)
    ]


ZP = perm(lambda z, y, x, c: (z + 1, y, x, c))
ZM = perm(lambda z, y, x, c: (z - 1, y, x, c))
XP = perm(lambda z, y, x, c: (z, y, x + 1, c))
XM = perm(lambda z, y, x, c: (z, y, x - 1, c))
PARTNER = perm(lambda z, y, x, c: (z, y ^ 1, x, c))
OTHER = perm(lambda z, y, x, c: (z, (3 - y) % 4, x, c))
CORE = perm(lambda z, y, x, c: (z, y, x, 1 - c))
X1 = perm(lambda z, y, x, c: (z, y, x ^ 1, c))
X3 = perm(lambda z, y, x, c: (z, y, 3 - x, c))
STEPS = (0, -1, 1, 2)
LIMIT = 56 << 20
SLOTS = 3
SMALL = pl.CostEstimate(flops=1 << 10, bytes_accessed=1 << 10, transcendentals=0)
PLANES = [[place(z, y, x, c) for x in range(4) for y in range(4) for c in range(2)] for z in range(4)]
ZGROUPS = [[place(z, y, x, c) for z in range(4)] for y in range(4) for x in range(4) for c in range(2)]
NT = (((1,), (1,)), ((), ()))


def send(v, p):
    return lax.ppermute(v, AX, p)


def tie(*vs):
    return lax.optimization_barrier(vs)


def columns_of(half, gate, up, wide, thin, thin_rows):
    gh, uh = gate[:, 384:512].astype(F32), up[:, 384:512].astype(F32)
    low = lax.broadcasted_iota(jnp.int32, gh.shape, 1) < 64
    first = jnp.where(low, gh, pltpu.roll(uh, 64, 1))
    second = jnp.where(low, pltpu.roll(gh, 64, 1), uh)
    base = pl.multiple_of(half * 512, 128)
    wide[:, :256] = gate[:, pl.ds(base, 256)]
    wide[:, 256:512] = up[:, pl.ds(base, 256)]
    wide[:, 512:] = jnp.where(half == 0, first, second).astype(BF16)
    base = pl.multiple_of(half * 512 + 256, 128)
    thin[thin_rows, :128] = gate[:, pl.ds(base, 128)]
    thin[thin_rows, 128:] = up[:, pl.ds(base, 128)]


def pack_kernel(s, gate, up, doc, query, some, keep0, keep1, give0, give1, piece):
    i = pl.program_id(0)
    columns_of(s[0], gate, up, keep0, keep1, pl.ds(i * gate.shape[0], gate.shape[0]))
    columns_of(1 - s[0], gate, up, give0, give1, slice(None))
    piece[pl.ds(i * doc.shape[0], doc.shape[0])] = doc[...]
    piece[pl.ds(TOK + i * query.shape[0], query.shape[0])] = query[...]

    @pl.when(i == 0)
    def _():
        for j in range(32):
            keep1[BLK + 16 * j : BLK + 16 * j + 16] = some[:, 256 * j : 256 * j + 256]


def pack(scalars, gate, up, doc, query):
    steps = 2
    rows = BLK // steps
    spec = lambda n: pl.BlockSpec((rows, n), lambda i, s: (i, 0))
    whole = lambda *shape: pl.BlockSpec(shape, lambda i, s: (0, 0))
    shape = lambda r, n: jax.ShapeDtypeStruct((r, n), BF16)
    column = lambda n: pl.BlockSpec((n // steps, BLK), lambda i, s: (i, s[1]))
    return pl.pallas_call(
        pack_kernel,
        grid_spec=pltpu.PrefetchScalarGridSpec(
            num_scalar_prefetch=1,
            grid=(steps,),
            in_specs=[spec(896), spec(896), column(TOK), column(QTOK), pl.BlockSpec((16, D), lambda i, s: (s[2], 0))],
            out_specs=[spec(640), whole(THIN, 256), spec(640), spec(256), whole(ROWS, BLK)],
        ),
        out_shape=[shape(BLK, 640), shape(THIN, 256), shape(BLK, 640), shape(BLK, 256), shape(ROWS, BLK)],
        compiler_params=pltpu.CompilerParams(vmem_limit_bytes=LIMIT),
        cost_estimate=SMALL,
    )(scalars, gate, up, doc, query, query)


def pack_grads_kernel(ylo_ref, doc, query, ids, keep, give):
    ylo = ylo_ref[0]
    give[ROWS:] = jnp.broadcast_to(ids[...].astype(F32), (16, TOK)).astype(BF16)
    for src, lo, n in ((doc, 0, TOK), (query, TOK, QTOK)):
        h = src[:, 384:512].astype(F32)
        t = pltpu.roll(h, 64, 1)
        low = lax.broadcasted_iota(jnp.int32, h.shape, 1) < 64
        first, second = jnp.where(low, h, t), jnp.where(low, t, h)
        for s, out in ((ylo, keep), (1 - ylo, give)):
            out[lo : lo + n, :384] = src[:, pl.ds(pl.multiple_of(s * 512, 128), 384)]
            out[lo : lo + n, 384:] = jnp.where(s == 0, first, second).astype(BF16)


def pack_grads(ylo, doc, query, ids):
    vmem = pl.BlockSpec(memory_space=pltpu.VMEM)
    return pl.pallas_call(
        pack_grads_kernel,
        in_specs=[pl.BlockSpec(memory_space=pltpu.SMEM), vmem, vmem, vmem],
        out_specs=[vmem, vmem],
        out_shape=[jax.ShapeDtypeStruct((ROWS, 512), BF16), jax.ShapeDtypeStruct((ROWS + 16, 512), BF16)],
        compiler_params=pltpu.CompilerParams(vmem_limit_bytes=LIMIT),
        cost_estimate=SMALL,
    )(ylo, doc, query, ids)


def halves_a_kernel(below, above, far0, far1):
    far0[0] = below[...]
    far1[0] = above[...]


def halves_b_kernel(below, above, x_below, x_above, _0, _1, far0, far1, x_far0, x_far1):
    far0[0] = below[...]
    far1[0] = above[...]
    x_far0[...] = x_below[...]
    x_far1[...] = x_above[...]


def halves(below, above, x=(), into=()):
    steps = 2
    spec = lambda rows, n, at: pl.BlockSpec((rows // steps, n), lambda i: (at * steps + i, 0))
    n, m = BLK // 2, ROWS // 2
    which = 1 if into else 0
    out_specs = [pl.BlockSpec((1, n // steps, 640), lambda i: (which, i, 0))] * 2
    out_shape = [jax.ShapeDtypeStruct((2, n, 640), BF16)] * 2
    in_specs = [spec(n, 640, 0), spec(n, 640, 1)]
    if into:
        in_specs += [spec(m, BLK, 0), spec(m, BLK, 1)] + [pl.BlockSpec(memory_space=pl.ANY)] * 2
        out_specs += [spec(m, BLK, 0)] * 2
        out_shape += [jax.ShapeDtypeStruct((m, BLK), BF16)] * 2
    return pl.pallas_call(
        halves_b_kernel if into else halves_a_kernel,
        grid=(steps,),
        in_specs=in_specs,
        out_specs=out_specs,
        out_shape=out_shape,
        input_output_aliases={4: 0, 5: 1} if into else {},
        compiler_params=pltpu.CompilerParams(vmem_limit_bytes=LIMIT),
        cost_estimate=SMALL,
    )(below, above, *x, *into)


def gated(hidden, gate, up):
    s = jax.nn.sigmoid(gate)
    up_factor = (hidden * gate * s).astype(BF16)
    gate_factor = (hidden * up * s * (1.0 + gate * (1.0 - s))).astype(BF16)
    return gate_factor, up_factor


def factor_kernel(phases, m, row, nw, nt, nx, s, *refs):
    def take(n):
        nonlocal refs
        got, refs = refs[:n], refs[n:]
        return got

    ends = phases[0][3]
    ws, thins, own_x, other_x = take(nw), take(nt), take(2), take(nx)
    befores = [None if begins else take(1)[0] for _, _, begins, _ in phases]
    hidden = [take(1)[0] for _ in phases] if ends else None
    outs = take(1 if ends else len(phases))
    acc, wv, xv, wsem, xsem, bsem, osem = refs[:7]
    hv, hsem = refs[7:] if ends else (None, None)
    steps = [(p, k) for p, phase in enumerate(phases) for k in range(phase[1])]
    half = ROWS // 2

    def start(g):
        p, k = steps[g]
        at = g % SLOTS
        base = 32 * p
        block = s[base + k]
        for w in range(nw):

            @pl.when(s[base + 16 + k] == w)
            def _():
                if w < 6:
                    pltpu.make_async_copy(ws[w], wv.at[at, :, pl.ds(0, 640)], wsem.at[at]).start()
                else:
                    n = BLK // 2
                    rows = pl.ds((w - 6) * n, n)
                    for part in (0, 1):
                        pltpu.make_async_copy(
                            ws[6 + part].at[rows], wv.at[at, pl.ds(part * n, n), pl.ds(0, 640)], wsem.at[at]
                        ).start()

        for flip in range(nt):
            rows = pl.ds(pl.multiple_of(block // 2 * (BLK if flip else THIN), 512), BLK)

            @pl.when(lax.rem(block, 2) == (s[base + 24] ^ flip))
            def _():
                pltpu.make_async_copy(thins[flip].at[rows], wv.at[at, :, pl.ds(640, 256)], wsem.at[at]).start()

        if phases[p][0] == "own":
            cols = pl.ds(pl.multiple_of(block * BLK, BLK), BLK)
            for x, lo, n in ((own_x[0], 0, TOK), (own_x[1], TOK, QTOK)):
                if row <= lo < row + m:
                    pltpu.make_async_copy(x.at[:, cols], xv.at[at, pl.ds(lo - row, n)], xsem.at[at]).start()
        else:
            for q in range(min(nx, 8)):

                @pl.when(s[base + 8 + k] == q)
                def _():
                    if q < 6:
                        pltpu.make_async_copy(other_x[q].at[pl.ds(row, m)], xv.at[at], xsem.at[at]).start()
                    else:
                        for part in (0, 1):
                            lo = max(row, part * half)
                            hi = min(row + m, part * half + half)
                            if lo < hi:
                                pltpu.make_async_copy(
                                    other_x[6 + (q - 6) * 2 + part].at[pl.ds(lo - part * half, hi - lo)],
                                    xv.at[at, pl.ds(lo - row, hi - lo)],
                                    xsem.at[at],
                                ).start()

    def load(p):
        if befores[p] is not None:
            pltpu.make_async_copy(befores[p].at[pl.ds(row, m)], acc.at[p], bsem.at[p]).start()

    def finish(p):
        hidden_copy(p).wait()
        dst, to = outs[0], slice(p * m, p * m + m)
        g, u = gated(hv[p, :, :256].astype(F32), acc[p, :, :256], acc[p, :, 256:512])
        dst[to, :256] = g
        dst[to, 256:512] = u
        both = acc[p, :, 512:640]
        turned = pltpu.roll(both, 64, 1)
        low = lax.broadcasted_iota(jnp.int32, both.shape, 1) < 64
        g, u = gated(hv[p, :, 384:].astype(F32), jnp.where(low, both, turned), jnp.where(low, turned, both))
        dst[to, 512:640] = jnp.where(low, g.astype(F32), u.astype(F32)).astype(BF16)
        g, u = gated(hv[p, :, 256:384].astype(F32), acc[p, :, 640:768], acc[p, :, 768:])
        dst[to, 640:768] = g
        dst[to, 768:] = u

    hidden_copy = lambda p: pltpu.make_async_copy(hidden[p].at[pl.ds(row, m)], hv.at[p], hsem.at[p])
    out_copy = lambda p: pltpu.make_async_copy(acc.at[p], outs[p], osem.at[p])
    start(0)
    load(0)
    for g, (p, k) in enumerate(steps):
        slot = g % SLOTS
        for v, sem in ((wv, wsem), (xv, xsem)):
            pltpu.make_async_copy(v.at[slot], v.at[slot], sem.at[slot]).wait()
        for later in range(1, len(steps)):
            if g == max(later - (SLOTS - 1), 0):
                start(later)
        if g == 0:
            for q in range(1, len(phases)):
                load(q)
            if ends:
                for q in range(len(phases)):
                    hidden_copy(q).start()
        part = jnp.dot(xv[slot], wv[slot], preferred_element_type=F32)
        if k == 0 and befores[p] is not None:
            pltpu.make_async_copy(befores[p].at[pl.ds(row, m)], acc.at[p], bsem.at[p]).wait()
        if k == 0 and befores[p] is None:
            acc[p] = part
        else:
            acc[p] += part
        if k == phases[p][1] - 1:
            if ends:
                finish(p)
            else:
                out_copy(p).start()
    if not ends:
        for p in range(len(phases)):
            out_copy(p).wait()


def factors(phases, scalars, ws, thins, own, other=(), befores=(), hidden=(), rows=(0, ROWS)):
    row, m = rows
    ends = phases[0][3]
    hbm = pl.BlockSpec(memory_space=pl.ANY)
    whole = lambda v: pl.BlockSpec(v.shape, lambda i, s: (0, 0))
    args = [*ws, *thins, *own, *other, *befores, *hidden]
    in_specs = [hbm] * len(args)
    if ends:
        out_shape = [jax.ShapeDtypeStruct((len(phases) * m, 896), BF16)]
        out_specs = [whole(out_shape[0])]
    else:
        out_shape = [jax.ShapeDtypeStruct((m, 896), F32)] * len(phases)
        out_specs = [hbm] * len(phases)
    return pl.pallas_call(
        functools.partial(factor_kernel, phases, m, row, len(ws), len(thins), len(other)),
        grid_spec=pltpu.PrefetchScalarGridSpec(
            num_scalar_prefetch=1,
            grid=(1,),
            in_specs=in_specs,
            out_specs=out_specs,
            scratch_shapes=[
                pltpu.VMEM((len(phases), m, 896), F32),
                pltpu.VMEM((SLOTS, BLK, 896), BF16),
                pltpu.VMEM((SLOTS, m, BLK), BF16),
                pltpu.SemaphoreType.DMA((SLOTS,)),
                pltpu.SemaphoreType.DMA((SLOTS,)),
                pltpu.SemaphoreType.DMA((len(phases),)),
                pltpu.SemaphoreType.DMA((len(phases),)),
            ]
            + ([pltpu.VMEM((len(phases), m, 512), BF16), pltpu.SemaphoreType.DMA((len(phases),))] if ends else []),
        ),
        out_shape=out_shape,
        compiler_params=pltpu.CompilerParams(vmem_limit_bytes=LIMIT),
        cost_estimate=SMALL,
    )(scalars, *args)


def unpack_kernel(thin, few):
    for z in range(4):
        for j in range(32):
            lo = 16 * j
            few[16 * z : 16 * z + 16, 256 * j : 256 * j + 256] = thin[z, lo : lo + 16]


def unpack(thin):
    return pl.pallas_call(
        unpack_kernel,
        grid=(1,),
        in_specs=[pl.BlockSpec((4, 512, 256), lambda k: (0, 2, 0))],
        out_specs=pl.BlockSpec((64, D), lambda k: (0, 0)),
        out_shape=jax.ShapeDtypeStruct((64, D), BF16),
        compiler_params=pltpu.CompilerParams(vmem_limit_bytes=LIMIT),
        cost_estimate=SMALL,
    )(thin.reshape(4, THIN, 256))


def gram_kernel(mine, theirs, doc, out, acc):
    k = pl.program_id(0)

    @pl.when(k == 0)
    def _():
        acc[...] = jnp.zeros_like(acc)

    few = jnp.concatenate([mine[...], theirs[...]], 0)
    acc[...] += lax.dot_general(doc[...], few, NT, preferred_element_type=F32)

    @pl.when(k == 7)
    def _():
        out[...] = acc[...].T.astype(BF16)


def gram_part(mine, theirs, doc):
    few = pl.BlockSpec((64, BLK), lambda k: (0, k))
    return pl.pallas_call(
        gram_kernel,
        grid=(8,),
        in_specs=[few, few, pl.BlockSpec((TOK, BLK), lambda k: (0, k))],
        out_specs=pl.BlockSpec((128, TOK), lambda k: (0, 0)),
        scratch_shapes=[pltpu.VMEM((TOK, 128), F32)],
        out_shape=jax.ShapeDtypeStruct((128, TOK), BF16),
        compiler_params=pltpu.CompilerParams(vmem_limit_bytes=LIMIT),
        cost_estimate=SMALL,
    )(mine, theirs, doc)


def hop(r):
    return jnp.where(r == 0, 0, jnp.where(r == 1, 3, jnp.where(r == 2, 1, 2)))


def score_kernel(first, count, s, *refs):
    qs, (d, gram, ids, docs, before, out, f, b, acc) = refs[:count], refs[count:]
    i = pl.program_id(0)
    r = first + i
    z, ylo = s[0], s[1]

    @pl.when(i == 0)
    def _():
        acc[...] = jnp.zeros_like(acc)

    if first == 3:
        f[:QTOK] = qs[0][...]
        f[QTOK:] = qs[1][...]
    else:
        for n in range(count):

            @pl.when(i == n)
            def _():
                f[...] = qs[n][...]

    for flip in (0, 1):
        b[...] = lax.dot_general(f[flip * QTOK : flip * QTOK + QTOK], d[...], NT, preferred_element_type=F32)
        sums = [[jnp.zeros((8, TOK), F32) for _ in range(QS)] for _ in (0, 1)]
        for y in range(4):
            whose = ylo ^ (y % 2)
            docs_at = pl.ds(pl.multiple_of(whose * TOK, TOK), TOK)
            for x in range(4):
                for core in range(2):
                    lo = x * 64 + y // 2 * 32 + core * 16
                    p = gram[x, y, core, whose ^ flip, 0].astype(F32) * b[lo : lo + 16, docs_at]
                    who = ids[flip * QTOK + lo : flip * QTOK + lo + 16, :]
                    for k in range(QS):
                        t = jnp.where(who == k, p, 0.0)
                        sums[y % 2][k] = sums[y % 2][k] + (t[:8] + t[8:])
        group = lax.rem(z + hop(r), 4) * 2 + (ylo ^ flip)
        for k in range(QS):
            for y in (0, 1):
                at = slice(y * TOK, y * TOK + TOK)
                acc[pl.ds(group * QS + k, 1), at] = jnp.sum(sums[y][k], 0, keepdims=True)

    @pl.when(i == pl.num_programs(0) - 1)
    def _():
        for k in range(2 * DOCS):
            at = slice(k // DOCS * TOK, k // DOCS * TOK + TOK)
            out[:, k : k + 1] = before[:, k : k + 1] + jnp.sum(acc[:, at] * docs[k : k + 1, at], 1, keepdims=True)


def score_sums(first, scalars, queries, documents, gram, ids, docs, before):
    whole = lambda v: pl.BlockSpec(v.shape, lambda r, s: (0, 0))
    planes = pl.BlockSpec((4, 4, 2, 2, 1, 16, TOK), lambda r, s: (0, 0, 0, 0, lax.rem(s[0] + hop(first + r), 4), 0, 0))
    return pl.pallas_call(
        functools.partial(score_kernel, first, len(queries)),
        grid_spec=pltpu.PrefetchScalarGridSpec(
            num_scalar_prefetch=1,
            grid=(1 if first == 3 else len(queries),),
            in_specs=[whole(v) for v in (*queries, documents)]
            + [planes, pl.BlockSpec((2 * QTOK, 1), lambda r, s: (first + r, 0)), whole(docs), whole(before)],
            out_specs=whole(before),
            scratch_shapes=[
                pltpu.VMEM((2 * QTOK, 896), BF16),
                pltpu.VMEM((QTOK, 2 * TOK), F32),
                pltpu.VMEM((8 * QS, 2 * TOK), F32),
            ],
        ),
        out_shape=jax.ShapeDtypeStruct(before.shape, F32),
        compiler_params=pltpu.CompilerParams(vmem_limit_bytes=LIMIT),
        cost_estimate=SMALL,
    )(scalars, *queries, documents, gram, ids, docs, before)


def local(doc_inputs, doc_grads, query_inputs, query_grads, gate_weight, up_weight, doc_ids, query_ids):
    dp = lax.axis_index("dp")
    tensor = lax.axis_index("tensor")
    z, ylo = dp // 2, dp % 2
    x, core = tensor // 4, tensor % 2
    ints = lambda *vs: jnp.stack([jnp.asarray(v, jnp.int32) for v in vs])

    def scalars(blocks):
        blocks = ints(*blocks)
        turn = (blocks // 2 - x + 4) % 4
        at = jnp.where(turn == 0, 0, jnp.where(turn == 3, 1, jnp.where(turn == 1, 2, 3)))
        which_x = at * 2 + ((blocks % 2) ^ core)
        turn = (blocks // 2 - z + 4) % 4
        flip = (blocks % 2) ^ ylo
        which_w = jnp.where(
            turn == 2, 6 + flip, flip * 3 + jnp.where(turn == 0, 0, jnp.where(turn == 3, 1, 2))
        )
        spare = jnp.zeros((8 - blocks.shape[0],), jnp.int32)
        last = jnp.full((8,), ylo)
        return jnp.concatenate([blocks, spare, which_x, spare, which_w, spare, last]).astype(jnp.int32)

    first = scalars([(z + dz + 4) % 4 * 2 + ylo for dz in (0, -1, 1)])
    second = scalars([(z + dz + 4) % 4 * 2 + (ylo ^ 1) for dz in (0, -1, 1)])
    last = scalars([(z + 2) % 4 * 2 + flip for flip in (0, 1)])
    late = (z + 2) % 4, jnp.where(x == z, (z + 3) % 4, (x + 2) % 4)
    free = [jnp.logical_and(late[0] != v, late[1] != v) for v in range(4)]
    soon = jnp.where(free[0], 0, jnp.where(free[1], 1, 2)), jnp.where(free[3], 3, jnp.where(free[2], 2, 1))
    blocks_of = lambda zs: [v * 2 + flip for v in zs for flip in (0, 1)]
    early = jnp.concatenate([second, scalars(blocks_of(soon))])
    late = jnp.concatenate([last, scalars(blocks_of(late))])
    where = ints(z, ylo)

    keep0, keep1, give0, give1, piece = pack(
        ints(ylo, x * 2 + core, tensor), gate_weight, up_weight, doc_inputs, query_inputs
    )
    thin_a = lax.all_gather(keep1, AX, axis_index_groups=ZGROUPS, axis=0, tiled=True)
    a_below, a_above = send(keep0, ZP), send(keep0, ZM)
    got0 = send(give0, PARTNER)
    piece = send(piece, OTHER)
    got1 = send(give1, PARTNER)
    mine, theirs = pack_grads(ints(ylo), doc_grads, query_grads, doc_ids)
    order = jnp.stack([(z + dz + 4) % 4 * 2 + (ylo ^ flip) for dz in STEPS for flip in (0, 1)])
    ids = query_ids[order].reshape(-1, 1)
    got0, piece, a_below, a_above, got1, ids, first, early, late, where, mine, theirs = tie(
        got0, piece, a_below, a_above, got1, ids, first, early, late, where, mine, theirs
    )
    thin_b = lax.all_gather(got1, AX, axis_index_groups=ZGROUPS, axis=0, tiled=True)
    b_below, b_above = send(got0, ZP), send(got0, ZM)
    x_below, x_above = send(piece, XP), send(piece, XM)
    own = (doc_inputs, query_inputs)
    a_w = [keep0, a_below, a_above]
    (own_part,) = factors((("own", 3, True, False),), first, a_w, [thin_a], own)
    few = unpack(thin_a)
    few_too = send(few, PARTNER)
    few_too, theirs = tie(few_too, theirs)
    gram = gram_part(few, few_too, doc_inputs)
    theirs = send(theirs, PARTNER)
    into = halves(a_below, a_above)
    b_below, b_above, x_below, x_above, piece, thin_b, own_part, gram, *into = tie(
        b_below, b_above, x_below, x_above, piece, thin_b, own_part, gram, *into
    )
    thins = [thin_a, thin_b]
    far0, far1, x_far0, x_far1 = halves(b_below, b_above, (x_below, x_above), into)
    far0, far1 = send(far0.reshape(BLK, 640), ZP), send(far1.reshape(BLK, 640), ZM)
    piece_too, x_below_too, x_above_too = send(piece, CORE), send(x_below, CORE), send(x_above, CORE)
    piece_too, x_below_too, x_above_too, x_far0, x_far1 = tie(piece_too, x_below_too, x_above_too, x_far0, x_far1)
    x_far0, x_far1 = send(x_far0, XP), send(x_far1, XM)
    near_x = [piece, piece_too, x_below, x_below_too, x_above, x_above_too]
    near_w = [*a_w, got0, b_below, b_above]
    own_part, other_part = factors(
        (("own", 3, False, False), ("other", 4, True, False)), early, near_w, thins, own, near_x, [own_part]
    )
    gram = lax.all_gather(gram, AX, axis_index_groups=PLANES, axis=0, tiled=True).reshape(4, 4, 2, 2, 4, 16, TOK)
    x_far0, x_far1, far0, far1, own_part, other_part, theirs = tie(
        x_far0, x_far1, far0, far1, own_part, other_part, theirs
    )
    all_w = [*near_w, far0, far1]
    all_x = [*near_x, x_far0, x_far1, send(x_far0, CORE), send(x_far1, CORE)]

    rest = (("own", 2, False, True), ("other", 4, False, True))
    parts, grads = (own_part, other_part), (mine, theirs)
    (q,) = factors(rest, late, all_w, thins, own, all_x, parts, grads, (TOK, QTOK))
    q, own_part, ids_too = tie(q, own_part, theirs[ROWS : ROWS + 1])
    ids_too = ids_too.astype(jnp.int32)
    lower, upper = jnp.where(ylo == 0, doc_ids, ids_too), jnp.where(ylo == 0, ids_too, doc_ids)
    both = jnp.concatenate([lower, upper + DOCS], 1)
    docs = (both == jnp.arange(2 * DOCS, dtype=jnp.int32)[:, None]).astype(F32)
    q_below, q_above = send(q, ZP), send(q, ZM)
    (d,) = factors(rest, late, all_w, thins, own, all_x, (own_part, other_part), grads, (0, TOK))
    q_below, q_above, d = tie(q_below, q_above, d)
    q_far0, q_far1 = send(q_below[:QTOK], ZP), send(q_above[QTOK:], ZM)

    scores = jnp.zeros((8 * QS, 2 * DOCS), F32)
    scores = score_sums(0, where, (q, q_below, q_above), d, gram, ids, docs, scores)
    scores = score_sums(3, where, (q_far0, q_far1), d, gram, ids, docs, scores)

    for p in (CORE, X1, X3, PARTNER, OTHER):
        scores = scores + send(scores, p)
    scores = jnp.where(ylo == 0, scores[:, :DOCS], scores[:, DOCS:]).T / math.sqrt(D * FF)
    return scores[None]


def solution(mesh):
    placed = (
        P("dp", None),
        P("dp", "tensor"),
        P("dp", None),
        P("dp", "tensor"),
        P("dp", "tensor"),
        P("dp", "tensor"),
        P("dp", None),
        P(),
    )
    return jax.shard_map(
        local, mesh=mesh, in_specs=placed, out_specs=P("dp", None, None), check_vma=False
    )
```

```python
import functools
import math

import jax
import jax.numpy as jnp
from jax import lax
from jax.experimental import pallas as pl
from jax.experimental.pallas import tpu as pltpu
from jax.sharding import PartitionSpec as P

D = 8192
FF = 14336
DOCS = 4
QS = 4
TOK = 512
QTOK = 256
ROWS = TOK + QTOK
BLK = D // 8
THIN = BLK + 512
AX = ("dp", "tensor")
F32 = jnp.float32
BF16 = jnp.bfloat16


def place(z, y, x, c):
    return ((z % 4) * 2 + (y % 2)) * 16 + (x % 4) * 4 + ((y % 4) // 2) * 2 + c


def perm(fn):
    return [
        (place(z, y, x, c), place(*fn(z, y, x, c)))
        for z in range(4)
        for y in range(4)
        for x in range(4)
        for c in range(2)
    ]


ZP = perm(lambda z, y, x, c: (z + 1, y, x, c))
ZM = perm(lambda z, y, x, c: (z - 1, y, x, c))
XP = perm(lambda z, y, x, c: (z, y, x + 1, c))
XM = perm(lambda z, y, x, c: (z, y, x - 1, c))
PARTNER = perm(lambda z, y, x, c: (z, y ^ 1, x, c))
OTHER = perm(lambda z, y, x, c: (z, (3 - y) % 4, x, c))
CORE = perm(lambda z, y, x, c: (z, y, x, 1 - c))
X1 = perm(lambda z, y, x, c: (z, y, x ^ 1, c))
X3 = perm(lambda z, y, x, c: (z, y, 3 - x, c))
STEPS = (0, -1, 1, 2)
LIMIT = 56 << 20
SLOTS = 3
SMALL = pl.CostEstimate(flops=1 << 10, bytes_accessed=1 << 10, transcendentals=0)
PLANES = [[place(z, y, x, c) for x in range(4) for y in range(4) for c in range(2)] for z in range(4)]
ZGROUPS = [[place(z, y, x, c) for z in range(4)] for y in range(4) for x in range(4) for c in range(2)]
NT = (((1,), (1,)), ((), ()))


def send(v, p):
    return lax.ppermute(v, AX, p)


def tie(*vs):
    return lax.optimization_barrier(vs)


def columns_of(half, gate, up, wide, thin, thin_rows):
    gh, uh = gate[:, 384:512].astype(F32), up[:, 384:512].astype(F32)
    low = lax.broadcasted_iota(jnp.int32, gh.shape, 1) < 64
    first = jnp.where(low, gh, pltpu.roll(uh, 64, 1))
    second = jnp.where(low, pltpu.roll(gh, 64, 1), uh)
    base = pl.multiple_of(half * 512, 128)
    wide[:, :256] = gate[:, pl.ds(base, 256)]
    wide[:, 256:512] = up[:, pl.ds(base, 256)]
    wide[:, 512:] = jnp.where(half == 0, first, second).astype(BF16)
    base = pl.multiple_of(half * 512 + 256, 128)
    thin[thin_rows, :128] = gate[:, pl.ds(base, 128)]
    thin[thin_rows, 128:] = up[:, pl.ds(base, 128)]


def pack_kernel(s, gate, up, doc, query, some, keep0, keep1, give0, give1, piece):
    i = pl.program_id(0)
    columns_of(s[0], gate, up, keep0, keep1, pl.ds(i * gate.shape[0], gate.shape[0]))
    columns_of(1 - s[0], gate, up, give0, give1, slice(None))
    piece[pl.ds(i * doc.shape[0], doc.shape[0])] = doc[...]
    piece[pl.ds(TOK + i * query.shape[0], query.shape[0])] = query[...]

    @pl.when(i == 0)
    def _():
        for j in range(32):
            keep1[BLK + 16 * j : BLK + 16 * j + 16] = some[:, 256 * j : 256 * j + 256]


def pack(scalars, gate, up, doc, query):
    steps = 2
    rows = BLK // steps
    spec = lambda n: pl.BlockSpec((rows, n), lambda i, s: (i, 0))
    whole = lambda *shape: pl.BlockSpec(shape, lambda i, s: (0, 0))
    shape = lambda r, n: jax.ShapeDtypeStruct((r, n), BF16)
    column = lambda n: pl.BlockSpec((n // steps, BLK), lambda i, s: (i, s[1]))
    return pl.pallas_call(
        pack_kernel,
        grid_spec=pltpu.PrefetchScalarGridSpec(
            num_scalar_prefetch=1,
            grid=(steps,),
            in_specs=[spec(896), spec(896), column(TOK), column(QTOK), pl.BlockSpec((16, D), lambda i, s: (s[2], 0))],
            out_specs=[spec(640), whole(THIN, 256), spec(640), spec(256), whole(ROWS, BLK)],
        ),
        out_shape=[shape(BLK, 640), shape(THIN, 256), shape(BLK, 640), shape(BLK, 256), shape(ROWS, BLK)],
        compiler_params=pltpu.CompilerParams(vmem_limit_bytes=LIMIT),
        cost_estimate=SMALL,
    )(scalars, gate, up, doc, query, query)


def pack_grads_kernel(ylo_ref, doc, query, ids, keep, give):
    ylo = ylo_ref[0]
    give[ROWS:] = jnp.broadcast_to(ids[...].astype(F32), (16, TOK)).astype(BF16)
    for src, lo, n in ((doc, 0, TOK), (query, TOK, QTOK)):
        h = src[:, 384:512].astype(F32)
        t = pltpu.roll(h, 64, 1)
        low = lax.broadcasted_iota(jnp.int32, h.shape, 1) < 64
        first, second = jnp.where(low, h, t), jnp.where(low, t, h)
        for s, out in ((ylo, keep), (1 - ylo, give)):
            out[lo : lo + n, :384] = src[:, pl.ds(pl.multiple_of(s * 512, 128), 384)]
            out[lo : lo + n, 384:] = jnp.where(s == 0, first, second).astype(BF16)


def pack_grads(ylo, doc, query, ids):
    vmem = pl.BlockSpec(memory_space=pltpu.VMEM)
    return pl.pallas_call(
        pack_grads_kernel,
        in_specs=[pl.BlockSpec(memory_space=pltpu.SMEM), vmem, vmem, vmem],
        out_specs=[vmem, vmem],
        out_shape=[jax.ShapeDtypeStruct((ROWS, 512), BF16), jax.ShapeDtypeStruct((ROWS + 16, 512), BF16)],
        compiler_params=pltpu.CompilerParams(vmem_limit_bytes=LIMIT),
        cost_estimate=SMALL,
    )(ylo, doc, query, ids)


def halves_a_kernel(below, above, far0, far1):
    far0[0] = below[...]
    far1[0] = above[...]


def halves_b_kernel(below, above, x_below, x_above, _0, _1, far0, far1, x_far0, x_far1):
    far0[0] = below[...]
    far1[0] = above[...]
    x_far0[...] = x_below[...]
    x_far1[...] = x_above[...]


def halves(below, above, x=(), into=()):
    steps = 2
    spec = lambda rows, n, at: pl.BlockSpec((rows // steps, n), lambda i: (at * steps + i, 0))
    n, m = BLK // 2, ROWS // 2
    which = 1 if into else 0
    out_specs = [pl.BlockSpec((1, n // steps, 640), lambda i: (which, i, 0))] * 2
    out_shape = [jax.ShapeDtypeStruct((2, n, 640), BF16)] * 2
    in_specs = [spec(n, 640, 0), spec(n, 640, 1)]
    if into:
        in_specs += [spec(m, BLK, 0), spec(m, BLK, 1)] + [pl.BlockSpec(memory_space=pl.ANY)] * 2
        out_specs += [spec(m, BLK, 0)] * 2
        out_shape += [jax.ShapeDtypeStruct((m, BLK), BF16)] * 2
    return pl.pallas_call(
        halves_b_kernel if into else halves_a_kernel,
        grid=(steps,),
        in_specs=in_specs,
        out_specs=out_specs,
        out_shape=out_shape,
        input_output_aliases={4: 0, 5: 1} if into else {},
        compiler_params=pltpu.CompilerParams(vmem_limit_bytes=LIMIT),
        cost_estimate=SMALL,
    )(below, above, *x, *into)


def gated(hidden, gate, up):
    s = jax.nn.sigmoid(gate)
    up_factor = (hidden * gate * s).astype(BF16)
    gate_factor = (hidden * up * s * (1.0 + gate * (1.0 - s))).astype(BF16)
    return gate_factor, up_factor


def factor_kernel(phases, m, row, nw, nt, nx, s, *refs):
    def take(n):
        nonlocal refs
        got, refs = refs[:n], refs[n:]
        return got

    ends = phases[0][3]
    ws, thins, own_x, other_x = take(nw), take(nt), take(2), take(nx)
    befores = [None if begins else take(1)[0] for _, _, begins, _ in phases]
    hidden = [take(1)[0] for _ in phases] if ends else None
    outs = take(1 if ends else len(phases))
    acc, wv, xv, wsem, xsem, bsem, osem = refs[:7]
    hv, hsem = refs[7:] if ends else (None, None)
    steps = [(p, k) for p, phase in enumerate(phases) for k in range(phase[1])]
    half = ROWS // 2

    def start(g):
        p, k = steps[g]
        at = g % SLOTS
        base = 32 * p
        block = s[base + k]
        for w in range(nw):

            @pl.when(s[base + 16 + k] == w)
            def _():
                if w < 6:
                    pltpu.make_async_copy(ws[w], wv.at[at, :, pl.ds(0, 640)], wsem.at[at]).start()
                else:
                    n = BLK // 2
                    rows = pl.ds((w - 6) * n, n)
                    for part in (0, 1):
                        pltpu.make_async_copy(
                            ws[6 + part].at[rows], wv.at[at, pl.ds(part * n, n), pl.ds(0, 640)], wsem.at[at]
                        ).start()

        for flip in range(nt):
            rows = pl.ds(pl.multiple_of(block // 2 * (BLK if flip else THIN), 512), BLK)

            @pl.when(lax.rem(block, 2) == (s[base + 24] ^ flip))
            def _():
                pltpu.make_async_copy(thins[flip].at[rows], wv.at[at, :, pl.ds(640, 256)], wsem.at[at]).start()

        if phases[p][0] == "own":
            cols = pl.ds(pl.multiple_of(block * BLK, BLK), BLK)
            for x, lo, n in ((own_x[0], 0, TOK), (own_x[1], TOK, QTOK)):
                if row <= lo < row + m:
                    pltpu.make_async_copy(x.at[:, cols], xv.at[at, pl.ds(lo - row, n)], xsem.at[at]).start()
        else:
            for q in range(min(nx, 8)):

                @pl.when(s[base + 8 + k] == q)
                def _():
                    if q < 6:
                        pltpu.make_async_copy(other_x[q].at[pl.ds(row, m)], xv.at[at], xsem.at[at]).start()
                    else:
                        for part in (0, 1):
                            lo = max(row, part * half)
                            hi = min(row + m, part * half + half)
                            if lo < hi:
                                pltpu.make_async_copy(
                                    other_x[6 + (q - 6) * 2 + part].at[pl.ds(lo - part * half, hi - lo)],
                                    xv.at[at, pl.ds(lo - row, hi - lo)],
                                    xsem.at[at],
                                ).start()

    def load(p):
        if befores[p] is not None:
            pltpu.make_async_copy(befores[p].at[pl.ds(row, m)], acc.at[p], bsem.at[p]).start()

    def finish(p):
        hidden_copy(p).wait()
        dst, to = outs[0], slice(p * m, p * m + m)
        g, u = gated(hv[p, :, :256].astype(F32), acc[p, :, :256], acc[p, :, 256:512])
        dst[to, :256] = g
        dst[to, 256:512] = u
        both = acc[p, :, 512:640]
        turned = pltpu.roll(both, 64, 1)
        low = lax.broadcasted_iota(jnp.int32, both.shape, 1) < 64
        g, u = gated(hv[p, :, 384:].astype(F32), jnp.where(low, both, turned), jnp.where(low, turned, both))
        dst[to, 512:640] = jnp.where(low, g.astype(F32), u.astype(F32)).astype(BF16)
        g, u = gated(hv[p, :, 256:384].astype(F32), acc[p, :, 640:768], acc[p, :, 768:])
        dst[to, 640:768] = g
        dst[to, 768:] = u

    hidden_copy = lambda p: pltpu.make_async_copy(hidden[p].at[pl.ds(row, m)], hv.at[p], hsem.at[p])
    out_copy = lambda p: pltpu.make_async_copy(acc.at[p], outs[p], osem.at[p])
    start(0)
    load(0)
    for g, (p, k) in enumerate(steps):
        slot = g % SLOTS
        for v, sem in ((wv, wsem), (xv, xsem)):
            pltpu.make_async_copy(v.at[slot], v.at[slot], sem.at[slot]).wait()
        for later in range(1, len(steps)):
            if g == max(later - (SLOTS - 1), 0):
                start(later)
        if g == 0:
            for q in range(1, len(phases)):
                load(q)
            if ends:
                for q in range(len(phases)):
                    hidden_copy(q).start()
        part = jnp.dot(xv[slot], wv[slot], preferred_element_type=F32)
        if k == 0 and befores[p] is not None:
            pltpu.make_async_copy(befores[p].at[pl.ds(row, m)], acc.at[p], bsem.at[p]).wait()
        if k == 0 and befores[p] is None:
            acc[p] = part
        else:
            acc[p] += part
        if k == phases[p][1] - 1:
            if ends:
                finish(p)
            else:
                out_copy(p).start()
    if not ends:
        for p in range(len(phases)):
            out_copy(p).wait()


def factors(phases, scalars, ws, thins, own, other=(), befores=(), hidden=(), rows=(0, ROWS)):
    row, m = rows
    ends = phases[0][3]
    hbm = pl.BlockSpec(memory_space=pl.ANY)
    whole = lambda v: pl.BlockSpec(v.shape, lambda i, s: (0, 0))
    args = [*ws, *thins, *own, *other, *befores, *hidden]
    in_specs = [hbm] * len(args)
    if ends:
        out_shape = [jax.ShapeDtypeStruct((len(phases) * m, 896), BF16)]
        out_specs = [whole(out_shape[0])]
    else:
        out_shape = [jax.ShapeDtypeStruct((m, 896), F32)] * len(phases)
        out_specs = [hbm] * len(phases)
    return pl.pallas_call(
        functools.partial(factor_kernel, phases, m, row, len(ws), len(thins), len(other)),
        grid_spec=pltpu.PrefetchScalarGridSpec(
            num_scalar_prefetch=1,
            grid=(1,),
            in_specs=in_specs,
            out_specs=out_specs,
            scratch_shapes=[
                pltpu.VMEM((len(phases), m, 896), F32),
                pltpu.VMEM((SLOTS, BLK, 896), BF16),
                pltpu.VMEM((SLOTS, m, BLK), BF16),
                pltpu.SemaphoreType.DMA((SLOTS,)),
                pltpu.SemaphoreType.DMA((SLOTS,)),
                pltpu.SemaphoreType.DMA((len(phases),)),
                pltpu.SemaphoreType.DMA((len(phases),)),
            ]
            + ([pltpu.VMEM((len(phases), m, 512), BF16), pltpu.SemaphoreType.DMA((len(phases),))] if ends else []),
        ),
        out_shape=out_shape,
        compiler_params=pltpu.CompilerParams(vmem_limit_bytes=LIMIT),
        cost_estimate=SMALL,
    )(scalars, *args)


def unpack_kernel(thin, few):
    for z in range(4):
        for j in range(32):
            lo = 16 * j
            few[16 * z : 16 * z + 16, 256 * j : 256 * j + 256] = thin[z, lo : lo + 16]


def unpack(thin):
    return pl.pallas_call(
        unpack_kernel,
        grid=(1,),
        in_specs=[pl.BlockSpec((4, 512, 256), lambda k: (0, 2, 0))],
        out_specs=pl.BlockSpec((64, D), lambda k: (0, 0)),
        out_shape=jax.ShapeDtypeStruct((64, D), BF16),
        compiler_params=pltpu.CompilerParams(vmem_limit_bytes=LIMIT),
        cost_estimate=SMALL,
    )(thin.reshape(4, THIN, 256))


def gram_kernel(mine, theirs, doc, out, acc):
    k = pl.program_id(0)

    @pl.when(k == 0)
    def _():
        acc[...] = jnp.zeros_like(acc)

    few = jnp.concatenate([mine[...], theirs[...]], 0)
    acc[...] += lax.dot_general(doc[...], few, NT, preferred_element_type=F32)

    @pl.when(k == 7)
    def _():
        out[...] = acc[...].T.astype(BF16)


def gram_part(mine, theirs, doc):
    few = pl.BlockSpec((64, BLK), lambda k: (0, k))
    return pl.pallas_call(
        gram_kernel,
        grid=(8,),
        in_specs=[few, few, pl.BlockSpec((TOK, BLK), lambda k: (0, k))],
        out_specs=pl.BlockSpec((128, TOK), lambda k: (0, 0)),
        scratch_shapes=[pltpu.VMEM((TOK, 128), F32)],
        out_shape=jax.ShapeDtypeStruct((128, TOK), BF16),
        compiler_params=pltpu.CompilerParams(vmem_limit_bytes=LIMIT),
        cost_estimate=SMALL,
    )(mine, theirs, doc)


def hop(r):
    return jnp.where(r == 0, 0, jnp.where(r == 1, 3, jnp.where(r == 2, 1, 2)))


def score_kernel(first, count, s, *refs):
    qs, (d, gram, ids, docs, before, out, f, b, acc) = refs[:count], refs[count:]
    i = pl.program_id(0)
    r = first + i
    z, ylo = s[0], s[1]

    @pl.when(i == 0)
    def _():
        acc[...] = jnp.zeros_like(acc)

    if first == 3:
        f[:QTOK] = qs[0][...]
        f[QTOK:] = qs[1][...]
    else:
        for n in range(count):

            @pl.when(i == n)
            def _():
                f[...] = qs[n][...]

    for flip in (0, 1):
        b[...] = lax.dot_general(f[flip * QTOK : flip * QTOK + QTOK], d[...], NT, preferred_element_type=F32)
        sums = [[jnp.zeros((8, TOK), F32) for _ in range(QS)] for _ in (0, 1)]
        for y in range(4):
            whose = ylo ^ (y % 2)
            docs_at = pl.ds(pl.multiple_of(whose * TOK, TOK), TOK)
            for x in range(4):
                for core in range(2):
                    lo = x * 64 + y // 2 * 32 + core * 16
                    p = gram[x, y, core, whose ^ flip, 0].astype(F32) * b[lo : lo + 16, docs_at]
                    who = ids[flip * QTOK + lo : flip * QTOK + lo + 16, :]
                    for k in range(QS):
                        t = jnp.where(who == k, p, 0.0)
                        sums[y % 2][k] = sums[y % 2][k] + (t[:8] + t[8:])
        group = lax.rem(z + hop(r), 4) * 2 + (ylo ^ flip)
        for k in range(QS):
            for y in (0, 1):
                at = slice(y * TOK, y * TOK + TOK)
                acc[pl.ds(group * QS + k, 1), at] = jnp.sum(sums[y][k], 0, keepdims=True)

    @pl.when(i == pl.num_programs(0) - 1)
    def _():
        for k in range(2 * DOCS):
            at = slice(k // DOCS * TOK, k // DOCS * TOK + TOK)
            out[:, k : k + 1] = before[:, k : k + 1] + jnp.sum(acc[:, at] * docs[k : k + 1, at], 1, keepdims=True)


def score_sums(first, scalars, queries, documents, gram, ids, docs, before):
    whole = lambda v: pl.BlockSpec(v.shape, lambda r, s: (0, 0))
    planes = pl.BlockSpec((4, 4, 2, 2, 1, 16, TOK), lambda r, s: (0, 0, 0, 0, lax.rem(s[0] + hop(first + r), 4), 0, 0))
    return pl.pallas_call(
        functools.partial(score_kernel, first, len(queries)),
        grid_spec=pltpu.PrefetchScalarGridSpec(
            num_scalar_prefetch=1,
            grid=(1 if first == 3 else len(queries),),
            in_specs=[whole(v) for v in (*queries, documents)]
            + [planes, pl.BlockSpec((2 * QTOK, 1), lambda r, s: (first + r, 0)), whole(docs), whole(before)],
            out_specs=whole(before),
            scratch_shapes=[
                pltpu.VMEM((2 * QTOK, 896), BF16),
                pltpu.VMEM((QTOK, 2 * TOK), F32),
                pltpu.VMEM((8 * QS, 2 * TOK), F32),
            ],
        ),
        out_shape=jax.ShapeDtypeStruct(before.shape, F32),
        compiler_params=pltpu.CompilerParams(vmem_limit_bytes=24 << 20),
        cost_estimate=SMALL,
    )(scalars, *queries, documents, gram, ids, docs, before)


def local(doc_inputs, doc_grads, query_inputs, query_grads, gate_weight, up_weight, doc_ids, query_ids):
    dp = lax.axis_index("dp")
    tensor = lax.axis_index("tensor")
    z, ylo = dp // 2, dp % 2
    x, core = tensor // 4, tensor % 2
    ints = lambda *vs: jnp.stack([jnp.asarray(v, jnp.int32) for v in vs])

    def scalars(blocks):
        blocks = ints(*blocks)
        turn = (blocks // 2 - x + 4) % 4
        at = jnp.where(turn == 0, 0, jnp.where(turn == 3, 1, jnp.where(turn == 1, 2, 3)))
        which_x = at * 2 + ((blocks % 2) ^ core)
        turn = (blocks // 2 - z + 4) % 4
        flip = (blocks % 2) ^ ylo
        which_w = jnp.where(
            turn == 2, 6 + flip, flip * 3 + jnp.where(turn == 0, 0, jnp.where(turn == 3, 1, 2))
        )
        spare = jnp.zeros((8 - blocks.shape[0],), jnp.int32)
        last = jnp.full((8,), ylo)
        return jnp.concatenate([blocks, spare, which_x, spare, which_w, spare, last]).astype(jnp.int32)

    first = scalars([(z + dz + 4) % 4 * 2 + ylo for dz in (0, -1, 1)])
    second = scalars([(z + dz + 4) % 4 * 2 + (ylo ^ 1) for dz in (0, -1, 1)])
    last = scalars([(z + 2) % 4 * 2 + flip for flip in (0, 1)])
    late = (z + 2) % 4, jnp.where(x == z, (z + 3) % 4, (x + 2) % 4)
    free = [jnp.logical_and(late[0] != v, late[1] != v) for v in range(4)]
    soon = jnp.where(free[0], 0, jnp.where(free[1], 1, 2)), jnp.where(free[3], 3, jnp.where(free[2], 2, 1))
    blocks_of = lambda zs: [v * 2 + flip for v in zs for flip in (0, 1)]
    early = jnp.concatenate([second, scalars(blocks_of(soon))])
    late = jnp.concatenate([last, scalars(blocks_of(late))])
    where = ints(z, ylo)

    keep0, keep1, give0, give1, piece = pack(
        ints(ylo, x * 2 + core, tensor), gate_weight, up_weight, doc_inputs, query_inputs
    )
    thin_a = lax.all_gather(keep1, AX, axis_index_groups=ZGROUPS, axis=0, tiled=True)
    a_below, a_above = send(keep0, ZP), send(keep0, ZM)
    got0 = send(give0, PARTNER)
    piece = send(piece, OTHER)
    got1 = send(give1, PARTNER)
    mine, theirs = pack_grads(ints(ylo), doc_grads, query_grads, doc_ids)
    order = jnp.stack([(z + dz + 4) % 4 * 2 + (ylo ^ flip) for dz in STEPS for flip in (0, 1)])
    ids = query_ids[order].reshape(-1, 1)
    got0, piece, a_below, a_above, got1, ids, first, early, late, where, mine, theirs = tie(
        got0, piece, a_below, a_above, got1, ids, first, early, late, where, mine, theirs
    )
    thin_b = lax.all_gather(got1, AX, axis_index_groups=ZGROUPS, axis=0, tiled=True)
    b_below, b_above = send(got0, ZP), send(got0, ZM)
    x_below, x_above = send(piece, XP), send(piece, XM)
    own = (doc_inputs, query_inputs)
    a_w = [keep0, a_below, a_above]
    (own_part,) = factors((("own", 3, True, False),), first, a_w, [thin_a], own)
    few = unpack(thin_a)
    few_too = send(few, PARTNER)
    few_too, theirs = tie(few_too, theirs)
    gram = gram_part(few, few_too, doc_inputs)
    theirs = send(theirs, PARTNER)
    into = halves(a_below, a_above)
    b_below, b_above, x_below, x_above, piece, own_part, gram, *into = tie(
        b_below, b_above, x_below, x_above, piece, own_part, gram, *into
    )
    thins = [thin_a, thin_b]
    far0, far1, x_far0, x_far1 = halves(b_below, b_above, (x_below, x_above), into)
    far0, far1 = send(far0.reshape(BLK, 640), ZP), send(far1.reshape(BLK, 640), ZM)
    piece_too, x_below_too, x_above_too = send(piece, CORE), send(x_below, CORE), send(x_above, CORE)
    piece_too, x_below_too, x_above_too, x_far0, x_far1 = tie(piece_too, x_below_too, x_above_too, x_far0, x_far1)
    x_far0, x_far1 = send(x_far0, XP), send(x_far1, XM)
    near_x = [piece, piece_too, x_below, x_below_too, x_above, x_above_too]
    near_w = [*a_w, got0, b_below, b_above]
    own_part, other_part = factors(
        (("own", 3, False, False), ("other", 4, True, False)), early, near_w, thins, own, near_x, [own_part]
    )
    gram = lax.all_gather(gram, AX, axis_index_groups=PLANES, axis=0, tiled=True).reshape(4, 4, 2, 2, 4, 16, TOK)
    x_far0, x_far1, far0, far1, own_part, other_part, theirs = tie(
        x_far0, x_far1, far0, far1, own_part, other_part, theirs
    )
    all_w = [*near_w, far0, far1]
    all_x = [*near_x, x_far0, x_far1, send(x_far0, CORE), send(x_far1, CORE)]

    rest = (("own", 2, False, True), ("other", 4, False, True))
    parts, grads = (own_part, other_part), (mine, theirs)
    (q,) = factors(rest, late, all_w, thins, own, all_x, parts, grads, (TOK, QTOK))
    q, own_part, ids_too = tie(q, own_part, theirs[ROWS : ROWS + 1])
    ids_too = ids_too.astype(jnp.int32)
    lower, upper = jnp.where(ylo == 0, doc_ids, ids_too), jnp.where(ylo == 0, ids_too, doc_ids)
    both = jnp.concatenate([lower, upper + DOCS], 1)
    docs = (both == jnp.arange(2 * DOCS, dtype=jnp.int32)[:, None]).astype(F32)
    q_below, q_above = send(q, ZP), send(q, ZM)
    (d,) = factors(rest, late, all_w, thins, own, all_x, (own_part, other_part), grads, (0, TOK))
    q_below, q_above, d = tie(q_below, q_above, d)
    q_far0, q_far1 = send(q_below[:QTOK], ZP), send(q_above[QTOK:], ZM)

    scores = jnp.zeros((8 * QS, 2 * DOCS), F32)
    scores = score_sums(0, where, (q, q_below, q_above), d, gram, ids, docs, scores)
    scores = score_sums(3, where, (q_far0, q_far1), d, gram, ids, docs, scores)

    for p in (CORE, X1, X3, PARTNER, OTHER):
        scores = scores + send(scores, p)
    scores = jnp.where(ylo == 0, scores[:, :DOCS], scores[:, DOCS:]).T / math.sqrt(D * FF)
    return scores[None]


def solution(mesh):
    placed = (
        P("dp", None),
        P("dp", "tensor"),
        P("dp", None),
        P("dp", "tensor"),
        P("dp", "tensor"),
        P("dp", "tensor"),
        P("dp", None),
        P(),
    )
    return jax.shard_map(
        local, mesh=mesh, in_specs=placed, out_specs=P("dp", None, None), check_vma=False
    )
```

```python
import functools
import math

import jax
import jax.numpy as jnp
from jax import lax
from jax.experimental import pallas as pl
from jax.experimental.pallas import tpu as pltpu
from jax.sharding import PartitionSpec as P

D = 8192
FF = 14336
DOCS = 4
QS = 4
TOK = 512
QTOK = 256
ROWS = TOK + QTOK
BLK = D // 8
THIN = BLK + 512
AX = ("dp", "tensor")
F32 = jnp.float32
BF16 = jnp.bfloat16


def place(z, y, x, c):
    return ((z % 4) * 2 + (y % 2)) * 16 + (x % 4) * 4 + ((y % 4) // 2) * 2 + c


def perm(fn):
    return [
        (place(z, y, x, c), place(*fn(z, y, x, c)))
        for z in range(4)
        for y in range(4)
        for x in range(4)
        for c in range(2)
    ]


ZP = perm(lambda z, y, x, c: (z + 1, y, x, c))
ZM = perm(lambda z, y, x, c: (z - 1, y, x, c))
XP = perm(lambda z, y, x, c: (z, y, x + 1, c))
XM = perm(lambda z, y, x, c: (z, y, x - 1, c))
PARTNER = perm(lambda z, y, x, c: (z, y ^ 1, x, c))
OTHER = perm(lambda z, y, x, c: (z, (3 - y) % 4, x, c))
CORE = perm(lambda z, y, x, c: (z, y, x, 1 - c))
X1 = perm(lambda z, y, x, c: (z, y, x ^ 1, c))
X3 = perm(lambda z, y, x, c: (z, y, 3 - x, c))
STEPS = (0, -1, 1, 2)
LIMIT = 56 << 20
SLOTS = 3
SMALL = pl.CostEstimate(flops=1 << 10, bytes_accessed=1 << 10, transcendentals=0)
PLANES = [[place(z, y, x, c) for x in range(4) for y in range(4) for c in range(2)] for z in range(4)]
ZGROUPS = [[place(z, y, x, c) for z in range(4)] for y in range(4) for x in range(4) for c in range(2)]
NT = (((1,), (1,)), ((), ()))


def send(v, p):
    return lax.ppermute(v, AX, p)


def tie(*vs):
    return lax.optimization_barrier(vs)


def columns_of(half, gate, up, wide, thin, thin_rows):
    gh, uh = gate[:, 384:512].astype(F32), up[:, 384:512].astype(F32)
    low = lax.broadcasted_iota(jnp.int32, gh.shape, 1) < 64
    first = jnp.where(low, gh, pltpu.roll(uh, 64, 1))
    second = jnp.where(low, pltpu.roll(gh, 64, 1), uh)
    base = pl.multiple_of(half * 512, 128)
    wide[:, :256] = gate[:, pl.ds(base, 256)]
    wide[:, 256:512] = up[:, pl.ds(base, 256)]
    wide[:, 512:] = jnp.where(half == 0, first, second).astype(BF16)
    base = pl.multiple_of(half * 512 + 256, 128)
    thin[thin_rows, :128] = gate[:, pl.ds(base, 128)]
    thin[thin_rows, 128:] = up[:, pl.ds(base, 128)]


def pack_kernel(s, gate, up, doc, query, some, keep0, keep1, give0, give1, piece):
    i = pl.program_id(0)
    columns_of(s[0], gate, up, keep0, keep1, pl.ds(i * gate.shape[0], gate.shape[0]))
    columns_of(1 - s[0], gate, up, give0, give1, slice(None))
    piece[pl.ds(i * doc.shape[0], doc.shape[0])] = doc[...]
    piece[pl.ds(TOK + i * query.shape[0], query.shape[0])] = query[...]

    @pl.when(i == 0)
    def _():
        for j in range(32):
            keep1[BLK + 16 * j : BLK + 16 * j + 16] = some[:, 256 * j : 256 * j + 256]


def pack(scalars, gate, up, doc, query):
    steps = 2
    rows = BLK // steps
    spec = lambda n: pl.BlockSpec((rows, n), lambda i, s: (i, 0))
    whole = lambda *shape: pl.BlockSpec(shape, lambda i, s: (0, 0))
    shape = lambda r, n: jax.ShapeDtypeStruct((r, n), BF16)
    column = lambda n: pl.BlockSpec((n // steps, BLK), lambda i, s: (i, s[1]))
    return pl.pallas_call(
        pack_kernel,
        grid_spec=pltpu.PrefetchScalarGridSpec(
            num_scalar_prefetch=1,
            grid=(steps,),
            in_specs=[spec(896), spec(896), column(TOK), column(QTOK), pl.BlockSpec((16, D), lambda i, s: (s[2], 0))],
            out_specs=[spec(640), whole(THIN, 256), spec(640), spec(256), whole(ROWS, BLK)],
        ),
        out_shape=[shape(BLK, 640), shape(THIN, 256), shape(BLK, 640), shape(BLK, 256), shape(ROWS, BLK)],
        compiler_params=pltpu.CompilerParams(vmem_limit_bytes=LIMIT),
        cost_estimate=SMALL,
    )(scalars, gate, up, doc, query, query)


def pack_grads_kernel(ylo_ref, doc, query, ids, keep, give):
    ylo = ylo_ref[0]
    give[ROWS:] = jnp.broadcast_to(ids[...].astype(F32), (16, TOK)).astype(BF16)
    for src, lo, n in ((doc, 0, TOK), (query, TOK, QTOK)):
        h = src[:, 384:512].astype(F32)
        t = pltpu.roll(h, 64, 1)
        low = lax.broadcasted_iota(jnp.int32, h.shape, 1) < 64
        first, second = jnp.where(low, h, t), jnp.where(low, t, h)
        for s, out in ((ylo, keep), (1 - ylo, give)):
            out[lo : lo + n, :384] = src[:, pl.ds(pl.multiple_of(s * 512, 128), 384)]
            out[lo : lo + n, 384:] = jnp.where(s == 0, first, second).astype(BF16)


def pack_grads(ylo, doc, query, ids):
    vmem = pl.BlockSpec(memory_space=pltpu.VMEM)
    return pl.pallas_call(
        pack_grads_kernel,
        in_specs=[pl.BlockSpec(memory_space=pltpu.SMEM), vmem, vmem, vmem],
        out_specs=[vmem, vmem],
        out_shape=[jax.ShapeDtypeStruct((ROWS, 512), BF16), jax.ShapeDtypeStruct((ROWS + 16, 512), BF16)],
        compiler_params=pltpu.CompilerParams(vmem_limit_bytes=LIMIT),
        cost_estimate=SMALL,
    )(ylo, doc, query, ids)


def halves_a_kernel(below, above, far0, far1):
    far0[0] = below[...]
    far1[0] = above[...]


def halves_b_kernel(below, above, x_below, x_above, _0, _1, far0, far1, x_far0, x_far1):
    far0[0] = below[...]
    far1[0] = above[...]
    x_far0[...] = x_below[...]
    x_far1[...] = x_above[...]


def halves(below, above, x=(), into=()):
    steps = 2
    spec = lambda rows, n, at: pl.BlockSpec((rows // steps, n), lambda i: (at * steps + i, 0))
    n, m = BLK // 2, ROWS // 2
    which = 1 if into else 0
    out_specs = [pl.BlockSpec((1, n // steps, 640), lambda i: (which, i, 0))] * 2
    out_shape = [jax.ShapeDtypeStruct((2, n, 640), BF16)] * 2
    in_specs = [spec(n, 640, 0), spec(n, 640, 1)]
    if into:
        in_specs += [spec(m, BLK, 0), spec(m, BLK, 1)] + [pl.BlockSpec(memory_space=pl.ANY)] * 2
        out_specs += [spec(m, BLK, 0)] * 2
        out_shape += [jax.ShapeDtypeStruct((m, BLK), BF16)] * 2
    return pl.pallas_call(
        halves_b_kernel if into else halves_a_kernel,
        grid=(steps,),
        in_specs=in_specs,
        out_specs=out_specs,
        out_shape=out_shape,
        input_output_aliases={4: 0, 5: 1} if into else {},
        compiler_params=pltpu.CompilerParams(vmem_limit_bytes=LIMIT),
        cost_estimate=SMALL,
    )(below, above, *x, *into)


def gated(hidden, gate, up):
    s = jax.nn.sigmoid(gate)
    up_factor = (hidden * gate * s).astype(BF16)
    gate_factor = (hidden * up * s * (1.0 + gate * (1.0 - s))).astype(BF16)
    return gate_factor, up_factor


def factor_kernel(phases, m, row, nw, nt, nx, s, *refs):
    def take(n):
        nonlocal refs
        got, refs = refs[:n], refs[n:]
        return got

    ends = phases[0][3]
    ws, thins, own_x, other_x = take(nw), take(nt), take(2), take(nx)
    befores = [None if begins else take(1)[0] for _, _, begins, _ in phases]
    hidden = [take(1)[0] for _ in phases] if ends else None
    outs = take(1 if ends else len(phases))
    acc, wv, xv, wsem, xsem, bsem, osem = refs[:7]
    hv, hsem = refs[7:] if ends else (None, None)
    steps = [(p, k) for p, phase in enumerate(phases) for k in range(phase[1])]
    half = ROWS // 2

    def start(g):
        p, k = steps[g]
        at = g % SLOTS
        base = 32 * p
        block = s[base + k]
        for w in range(nw):

            @pl.when(s[base + 16 + k] == w)
            def _():
                if w < 6:
                    pltpu.make_async_copy(ws[w], wv.at[at, :, pl.ds(0, 640)], wsem.at[at]).start()
                else:
                    n = BLK // 2
                    rows = pl.ds((w - 6) * n, n)
                    for part in (0, 1):
                        pltpu.make_async_copy(
                            ws[6 + part].at[rows], wv.at[at, pl.ds(part * n, n), pl.ds(0, 640)], wsem.at[at]
                        ).start()

        for flip in range(nt):
            rows = pl.ds(pl.multiple_of(block // 2 * (BLK if flip else THIN), 512), BLK)

            @pl.when(lax.rem(block, 2) == (s[base + 24] ^ flip))
            def _():
                pltpu.make_async_copy(thins[flip].at[rows], wv.at[at, :, pl.ds(640, 256)], wsem.at[at]).start()

        if phases[p][0] == "own":
            cols = pl.ds(pl.multiple_of(block * BLK, BLK), BLK)
            for x, lo, n in ((own_x[0], 0, TOK), (own_x[1], TOK, QTOK)):
                if row <= lo < row + m:
                    pltpu.make_async_copy(x.at[:, cols], xv.at[at, pl.ds(lo - row, n)], xsem.at[at]).start()
        else:
            for q in range(min(nx, 8)):

                @pl.when(s[base + 8 + k] == q)
                def _():
                    if q < 6:
                        pltpu.make_async_copy(other_x[q].at[pl.ds(row, m)], xv.at[at], xsem.at[at]).start()
                    else:
                        for part in (0, 1):
                            lo = max(row, part * half)
                            hi = min(row + m, part * half + half)
                            if lo < hi:
                                pltpu.make_async_copy(
                                    other_x[6 + (q - 6) * 2 + part].at[pl.ds(lo - part * half, hi - lo)],
                                    xv.at[at, pl.ds(lo - row, hi - lo)],
                                    xsem.at[at],
                                ).start()

    def load(p):
        if befores[p] is not None:
            pltpu.make_async_copy(befores[p].at[pl.ds(row, m)], acc.at[p], bsem.at[p]).start()

    def finish(p):
        hidden_copy(p).wait()
        dst, to = outs[0], slice(p * m, p * m + m)
        g, u = gated(hv[p, :, :256].astype(F32), acc[p, :, :256], acc[p, :, 256:512])
        dst[to, :256] = g
        dst[to, 256:512] = u
        both = acc[p, :, 512:640]
        turned = pltpu.roll(both, 64, 1)
        low = lax.broadcasted_iota(jnp.int32, both.shape, 1) < 64
        g, u = gated(hv[p, :, 384:].astype(F32), jnp.where(low, both, turned), jnp.where(low, turned, both))
        dst[to, 512:640] = jnp.where(low, g.astype(F32), u.astype(F32)).astype(BF16)
        g, u = gated(hv[p, :, 256:384].astype(F32), acc[p, :, 640:768], acc[p, :, 768:])
        dst[to, 640:768] = g
        dst[to, 768:] = u

    hidden_copy = lambda p: pltpu.make_async_copy(hidden[p].at[pl.ds(row, m)], hv.at[p], hsem.at[p])
    out_copy = lambda p: pltpu.make_async_copy(acc.at[p], outs[p], osem.at[p])
    i = pl.program_id(0)
    slot = lax.rem(i, SLOTS)
    firsts = [sum(phase[1] for phase in phases[:p]) for p in range(len(phases) + 1)]

    @pl.when(i == 0)
    def _():
        start(0)
        load(0)

    for v, sem in ((wv, wsem), (xv, xsem)):
        pltpu.make_async_copy(v.at[slot], v.at[slot], sem.at[slot]).wait()

    for g in range(1, len(steps)):

        @pl.when(i == max(g - (SLOTS - 1), 0))
        def _():
            start(g)

    @pl.when(i == 0)
    def _():
        for p in range(1, len(phases)):
            load(p)
        if ends:
            for p in range(len(phases)):
                hidden_copy(p).start()

    for p in range(len(phases)):

        @pl.when(i == firsts[p])
        def _():
            if befores[p] is None:
                acc[p] = jnp.zeros((m, 896), F32)
            else:
                pltpu.make_async_copy(befores[p].at[pl.ds(row, m)], acc.at[p], bsem.at[p]).wait()

    now = jnp.where(i >= firsts[1], 1, 0) if len(phases) > 1 else 0
    acc[now] += jnp.dot(xv[slot], wv[slot], preferred_element_type=F32)

    for p in range(len(phases)):

        @pl.when(i == firsts[p + 1] - 1)
        def _():
            if ends:
                finish(p)
            else:
                out_copy(p).start()

    if not ends:

        @pl.when(i == len(steps) - 1)
        def _():
            for p in range(len(phases)):
                out_copy(p).wait()


def factors(phases, scalars, ws, thins, own, other=(), befores=(), hidden=(), rows=(0, ROWS)):
    row, m = rows
    ends = phases[0][3]
    hbm = pl.BlockSpec(memory_space=pl.ANY)
    whole = lambda v: pl.BlockSpec(v.shape, lambda i, s: (0, 0))
    args = [*ws, *thins, *own, *other, *befores, *hidden]
    in_specs = [hbm] * len(args)
    if ends:
        out_shape = [jax.ShapeDtypeStruct((len(phases) * m, 896), BF16)]
        out_specs = [whole(out_shape[0])]
    else:
        out_shape = [jax.ShapeDtypeStruct((m, 896), F32)] * len(phases)
        out_specs = [hbm] * len(phases)
    return pl.pallas_call(
        functools.partial(factor_kernel, phases, m, row, len(ws), len(thins), len(other)),
        grid_spec=pltpu.PrefetchScalarGridSpec(
            num_scalar_prefetch=1,
            grid=(sum(phase[1] for phase in phases),),
            in_specs=in_specs,
            out_specs=out_specs,
            scratch_shapes=[
                pltpu.VMEM((len(phases), m, 896), F32),
                pltpu.VMEM((SLOTS, BLK, 896), BF16),
                pltpu.VMEM((SLOTS, m, BLK), BF16),
                pltpu.SemaphoreType.DMA((SLOTS,)),
                pltpu.SemaphoreType.DMA((SLOTS,)),
                pltpu.SemaphoreType.DMA((len(phases),)),
                pltpu.SemaphoreType.DMA((len(phases),)),
            ]
            + ([pltpu.VMEM((len(phases), m, 512), BF16), pltpu.SemaphoreType.DMA((len(phases),))] if ends else []),
        ),
        out_shape=out_shape,
        compiler_params=pltpu.CompilerParams(vmem_limit_bytes=LIMIT),
        cost_estimate=SMALL,
    )(scalars, *args)


def unpack_kernel(thin, few):
    for z in range(4):
        for j in range(32):
            lo = 16 * j
            few[16 * z : 16 * z + 16, 256 * j : 256 * j + 256] = thin[z, lo : lo + 16]


def unpack(thin):
    return pl.pallas_call(
        unpack_kernel,
        grid=(1,),
        in_specs=[pl.BlockSpec((4, 512, 256), lambda k: (0, 2, 0))],
        out_specs=pl.BlockSpec((64, D), lambda k: (0, 0)),
        out_shape=jax.ShapeDtypeStruct((64, D), BF16),
        compiler_params=pltpu.CompilerParams(vmem_limit_bytes=LIMIT),
        cost_estimate=SMALL,
    )(thin.reshape(4, THIN, 256))


def gram_kernel(mine, theirs, doc, out, acc):
    k = pl.program_id(0)

    @pl.when(k == 0)
    def _():
        acc[...] = jnp.zeros_like(acc)

    few = jnp.concatenate([mine[...], theirs[...]], 0)
    acc[...] += lax.dot_general(doc[...], few, NT, preferred_element_type=F32)

    @pl.when(k == 7)
    def _():
        out[...] = acc[...].T.astype(BF16)


def gram_part(mine, theirs, doc):
    few = pl.BlockSpec((64, BLK), lambda k: (0, k))
    return pl.pallas_call(
        gram_kernel,
        grid=(8,),
        in_specs=[few, few, pl.BlockSpec((TOK, BLK), lambda k: (0, k))],
        out_specs=pl.BlockSpec((128, TOK), lambda k: (0, 0)),
        scratch_shapes=[pltpu.VMEM((TOK, 128), F32)],
        out_shape=jax.ShapeDtypeStruct((128, TOK), BF16),
        compiler_params=pltpu.CompilerParams(vmem_limit_bytes=LIMIT),
        cost_estimate=SMALL,
    )(mine, theirs, doc)


def hop(r):
    return jnp.where(r == 0, 0, jnp.where(r == 1, 3, jnp.where(r == 2, 1, 2)))


def score_kernel(first, count, s, *refs):
    qs, (d, gram, ids, docs, before, out, f, b, acc) = refs[:count], refs[count:]
    i = pl.program_id(0)
    r = first + i
    z, ylo = s[0], s[1]

    @pl.when(i == 0)
    def _():
        acc[...] = jnp.zeros_like(acc)

    if first == 3:
        f[:QTOK] = qs[0][...]
        f[QTOK:] = qs[1][...]
    else:
        for n in range(count):

            @pl.when(i == n)
            def _():
                f[...] = qs[n][...]

    for flip in (0, 1):
        b[...] = lax.dot_general(f[flip * QTOK : flip * QTOK + QTOK], d[...], NT, preferred_element_type=F32)
        sums = [[jnp.zeros((8, TOK), F32) for _ in range(QS)] for _ in (0, 1)]
        for y in range(4):
            whose = ylo ^ (y % 2)
            docs_at = pl.ds(pl.multiple_of(whose * TOK, TOK), TOK)
            for x in range(4):
                for core in range(2):
                    lo = x * 64 + y // 2 * 32 + core * 16
                    p = gram[x, y, core, whose ^ flip, 0].astype(F32) * b[lo : lo + 16, docs_at]
                    who = ids[flip * QTOK + lo : flip * QTOK + lo + 16, :]
                    for k in range(QS):
                        t = jnp.where(who == k, p, 0.0)
                        sums[y % 2][k] = sums[y % 2][k] + (t[:8] + t[8:])
        group = lax.rem(z + hop(r), 4) * 2 + (ylo ^ flip)
        for k in range(QS):
            for y in (0, 1):
                at = slice(y * TOK, y * TOK + TOK)
                acc[pl.ds(group * QS + k, 1), at] = jnp.sum(sums[y][k], 0, keepdims=True)

    @pl.when(i == pl.num_programs(0) - 1)
    def _():
        for k in range(2 * DOCS):
            at = slice(k // DOCS * TOK, k // DOCS * TOK + TOK)
            out[:, k : k + 1] = before[:, k : k + 1] + jnp.sum(acc[:, at] * docs[k : k + 1, at], 1, keepdims=True)


def score_sums(first, scalars, queries, documents, gram, ids, docs, before):
    whole = lambda v: pl.BlockSpec(v.shape, lambda r, s: (0, 0))
    planes = pl.BlockSpec((4, 4, 2, 2, 1, 16, TOK), lambda r, s: (0, 0, 0, 0, lax.rem(s[0] + hop(first + r), 4), 0, 0))
    return pl.pallas_call(
        functools.partial(score_kernel, first, len(queries)),
        grid_spec=pltpu.PrefetchScalarGridSpec(
            num_scalar_prefetch=1,
            grid=(1 if first == 3 else len(queries),),
            in_specs=[whole(v) for v in (*queries, documents)]
            + [planes, pl.BlockSpec((2 * QTOK, 1), lambda r, s: (first + r, 0)), whole(docs), whole(before)],
            out_specs=whole(before),
            scratch_shapes=[
                pltpu.VMEM((2 * QTOK, 896), BF16),
                pltpu.VMEM((QTOK, 2 * TOK), F32),
                pltpu.VMEM((8 * QS, 2 * TOK), F32),
            ],
        ),
        out_shape=jax.ShapeDtypeStruct(before.shape, F32),
        compiler_params=pltpu.CompilerParams(vmem_limit_bytes=24 << 20),
        cost_estimate=SMALL,
    )(scalars, *queries, documents, gram, ids, docs, before)


def local(doc_inputs, doc_grads, query_inputs, query_grads, gate_weight, up_weight, doc_ids, query_ids):
    dp = lax.axis_index("dp")
    tensor = lax.axis_index("tensor")
    z, ylo = dp // 2, dp % 2
    x, core = tensor // 4, tensor % 2
    ints = lambda *vs: jnp.stack([jnp.asarray(v, jnp.int32) for v in vs])

    def scalars(blocks):
        blocks = ints(*blocks)
        turn = (blocks // 2 - x + 4) % 4
        at = jnp.where(turn == 0, 0, jnp.where(turn == 3, 1, jnp.where(turn == 1, 2, 3)))
        which_x = at * 2 + ((blocks % 2) ^ core)
        turn = (blocks // 2 - z + 4) % 4
        flip = (blocks % 2) ^ ylo
        which_w = jnp.where(
            turn == 2, 6 + flip, flip * 3 + jnp.where(turn == 0, 0, jnp.where(turn == 3, 1, 2))
        )
        spare = jnp.zeros((8 - blocks.shape[0],), jnp.int32)
        last = jnp.full((8,), ylo)
        return jnp.concatenate([blocks, spare, which_x, spare, which_w, spare, last]).astype(jnp.int32)

    first = scalars([(z + dz + 4) % 4 * 2 + ylo for dz in (0, -1, 1)])
    second = scalars([(z + dz + 4) % 4 * 2 + (ylo ^ 1) for dz in (0, -1, 1)])
    last = scalars([(z + 2) % 4 * 2 + flip for flip in (0, 1)])
    late = (z + 2) % 4, jnp.where(x == z, (z + 3) % 4, (x + 2) % 4)
    free = [jnp.logical_and(late[0] != v, late[1] != v) for v in range(4)]
    soon = jnp.where(free[0], 0, jnp.where(free[1], 1, 2)), jnp.where(free[3], 3, jnp.where(free[2], 2, 1))
    blocks_of = lambda zs: [v * 2 + flip for v in zs for flip in (0, 1)]
    early = jnp.concatenate([second, scalars(blocks_of(soon))])
    late = jnp.concatenate([last, scalars(blocks_of(late))])
    where = ints(z, ylo)

    keep0, keep1, give0, give1, piece = pack(
        ints(ylo, x * 2 + core, tensor), gate_weight, up_weight, doc_inputs, query_inputs
    )
    thin_a = lax.all_gather(keep1, AX, axis_index_groups=ZGROUPS, axis=0, tiled=True)
    a_below, a_above = send(keep0, ZP), send(keep0, ZM)
    got0 = send(give0, PARTNER)
    piece = send(piece, OTHER)
    got1 = send(give1, PARTNER)
    mine, theirs = pack_grads(ints(ylo), doc_grads, query_grads, doc_ids)
    order = jnp.stack([(z + dz + 4) % 4 * 2 + (ylo ^ flip) for dz in STEPS for flip in (0, 1)])
    ids = query_ids[order].reshape(-1, 1)
    got0, piece, a_below, a_above, got1, ids, first, early, late, where, mine, theirs = tie(
        got0, piece, a_below, a_above, got1, ids, first, early, late, where, mine, theirs
    )
    thin_b = lax.all_gather(got1, AX, axis_index_groups=ZGROUPS, axis=0, tiled=True)
    b_below, b_above = send(got0, ZP), send(got0, ZM)
    x_below, x_above = send(piece, XP), send(piece, XM)
    own = (doc_inputs, query_inputs)
    a_w = [keep0, a_below, a_above]
    (own_part,) = factors((("own", 3, True, False),), first, a_w, [thin_a], own)
    few = unpack(thin_a)
    few_too = send(few, PARTNER)
    few_too, theirs = tie(few_too, theirs)
    gram = gram_part(few, few_too, doc_inputs)
    theirs = send(theirs, PARTNER)
    into = halves(a_below, a_above)
    b_below, b_above, x_below, x_above, piece, own_part, gram, *into = tie(
        b_below, b_above, x_below, x_above, piece, own_part, gram, *into
    )
    thins = [thin_a, thin_b]
    far0, far1, x_far0, x_far1 = halves(b_below, b_above, (x_below, x_above), into)
    far0, far1 = send(far0.reshape(BLK, 640), ZP), send(far1.reshape(BLK, 640), ZM)
    piece_too, x_below_too, x_above_too = send(piece, CORE), send(x_below, CORE), send(x_above, CORE)
    piece_too, x_below_too, x_above_too, x_far0, x_far1 = tie(piece_too, x_below_too, x_above_too, x_far0, x_far1)
    x_far0, x_far1 = send(x_far0, XP), send(x_far1, XM)
    near_x = [piece, piece_too, x_below, x_below_too, x_above, x_above_too]
    near_w = [*a_w, got0, b_below, b_above]
    own_part, other_part = factors(
        (("own", 3, False, False), ("other", 4, True, False)), early, near_w, thins, own, near_x, [own_part]
    )
    gram = lax.all_gather(gram, AX, axis_index_groups=PLANES, axis=0, tiled=True).reshape(4, 4, 2, 2, 4, 16, TOK)
    x_far0, x_far1, far0, far1, own_part, other_part, theirs = tie(
        x_far0, x_far1, far0, far1, own_part, other_part, theirs
    )
    all_w = [*near_w, far0, far1]
    all_x = [*near_x, x_far0, x_far1, send(x_far0, CORE), send(x_far1, CORE)]

    rest = (("own", 2, False, True), ("other", 4, False, True))
    parts, grads = (own_part, other_part), (mine, theirs)
    (q,) = factors(rest, late, all_w, thins, own, all_x, parts, grads, (TOK, QTOK))
    q, own_part, ids_too = tie(q, own_part, theirs[ROWS : ROWS + 1])
    ids_too = ids_too.astype(jnp.int32)
    lower, upper = jnp.where(ylo == 0, doc_ids, ids_too), jnp.where(ylo == 0, ids_too, doc_ids)
    both = jnp.concatenate([lower, upper + DOCS], 1)
    docs = (both == jnp.arange(2 * DOCS, dtype=jnp.int32)[:, None]).astype(F32)
    q_below, q_above = send(q, ZP), send(q, ZM)
    (d,) = factors(rest, late, all_w, thins, own, all_x, (own_part, other_part), grads, (0, TOK))
    q_below, q_above, d = tie(q_below, q_above, d)
    q_far0, q_far1 = send(q_below[:QTOK], ZP), send(q_above[QTOK:], ZM)

    scores = jnp.zeros((8 * QS, 2 * DOCS), F32)
    scores = score_sums(0, where, (q, q_below, q_above), d, gram, ids, docs, scores)
    scores = score_sums(3, where, (q_far0, q_far1), d, gram, ids, docs, scores)

    for p in (CORE, X1, X3, PARTNER, OTHER):
        scores = scores + send(scores, p)
    scores = jnp.where(ylo == 0, scores[:, :DOCS], scores[:, DOCS:]).T / math.sqrt(D * FF)
    return scores[None]


def solution(mesh):
    placed = (
        P("dp", None),
        P("dp", "tensor"),
        P("dp", None),
        P("dp", "tensor"),
        P("dp", "tensor"),
        P("dp", "tensor"),
        P("dp", None),
        P(),
    )
    return jax.shard_map(
        local, mesh=mesh, in_specs=placed, out_specs=P("dp", None, None), check_vma=False
    )
```

```python
import functools
import math

import jax
import jax.numpy as jnp
from jax import lax
from jax.experimental import pallas as pl
from jax.experimental.pallas import tpu as pltpu
from jax.sharding import PartitionSpec as P

D = 8192
FF = 14336
DOCS = 4
QS = 4
TOK = 512
QTOK = 256
ROWS = TOK + QTOK
BLK = D // 8
THIN = BLK + 512
AX = ("dp", "tensor")
F32 = jnp.float32
BF16 = jnp.bfloat16


def place(z, y, x, c):
    return ((z % 4) * 2 + (y % 2)) * 16 + (x % 4) * 4 + ((y % 4) // 2) * 2 + c


def perm(fn):
    return [
        (place(z, y, x, c), place(*fn(z, y, x, c)))
        for z in range(4)
        for y in range(4)
        for x in range(4)
        for c in range(2)
    ]


ZP = perm(lambda z, y, x, c: (z + 1, y, x, c))
ZM = perm(lambda z, y, x, c: (z - 1, y, x, c))
XP = perm(lambda z, y, x, c: (z, y, x + 1, c))
XM = perm(lambda z, y, x, c: (z, y, x - 1, c))
PARTNER = perm(lambda z, y, x, c: (z, y ^ 1, x, c))
OTHER = perm(lambda z, y, x, c: (z, (3 - y) % 4, x, c))
CORE = perm(lambda z, y, x, c: (z, y, x, 1 - c))
X1 = perm(lambda z, y, x, c: (z, y, x ^ 1, c))
X3 = perm(lambda z, y, x, c: (z, y, 3 - x, c))
STEPS = (0, -1, 1, 2)
LIMIT = 56 << 20
SLOTS = 3
SMALL = pl.CostEstimate(flops=1 << 10, bytes_accessed=1 << 10, transcendentals=0)
PLANES = [[place(z, y, x, c) for x in range(4) for y in range(4) for c in range(2)] for z in range(4)]
ZGROUPS = [[place(z, y, x, c) for z in range(4)] for y in range(4) for x in range(4) for c in range(2)]
NT = (((1,), (1,)), ((), ()))


def send(v, p):
    return lax.ppermute(v, AX, p)


def tie(*vs):
    return lax.optimization_barrier(vs)


def columns_of(half, gate, up, wide, thin, thin_rows):
    gh, uh = gate[:, 384:512].astype(F32), up[:, 384:512].astype(F32)
    low = lax.broadcasted_iota(jnp.int32, gh.shape, 1) < 64
    first = jnp.where(low, gh, pltpu.roll(uh, 64, 1))
    second = jnp.where(low, pltpu.roll(gh, 64, 1), uh)
    base = pl.multiple_of(half * 512, 128)
    wide[:, :256] = gate[:, pl.ds(base, 256)]
    wide[:, 256:512] = up[:, pl.ds(base, 256)]
    wide[:, 512:] = jnp.where(half == 0, first, second).astype(BF16)
    base = pl.multiple_of(half * 512 + 256, 128)
    thin[thin_rows, :128] = gate[:, pl.ds(base, 128)]
    thin[thin_rows, 128:] = up[:, pl.ds(base, 128)]


def pack_kernel(s, gate, up, doc, query, some, keep0, keep1, give0, give1, piece):
    i = pl.program_id(0)
    columns_of(s[0], gate, up, keep0, keep1, pl.ds(i * gate.shape[0], gate.shape[0]))
    columns_of(1 - s[0], gate, up, give0, give1, slice(None))
    piece[pl.ds(i * doc.shape[0], doc.shape[0])] = doc[...]
    piece[pl.ds(TOK + i * query.shape[0], query.shape[0])] = query[...]

    @pl.when(i == 0)
    def _():
        for j in range(32):
            keep1[BLK + 16 * j : BLK + 16 * j + 16] = some[:, 256 * j : 256 * j + 256]


def pack(scalars, gate, up, doc, query):
    steps = 2
    rows = BLK // steps
    spec = lambda n: pl.BlockSpec((rows, n), lambda i, s: (i, 0))
    whole = lambda *shape: pl.BlockSpec(shape, lambda i, s: (0, 0))
    shape = lambda r, n: jax.ShapeDtypeStruct((r, n), BF16)
    column = lambda n: pl.BlockSpec((n // steps, BLK), lambda i, s: (i, s[1]))
    return pl.pallas_call(
        pack_kernel,
        grid_spec=pltpu.PrefetchScalarGridSpec(
            num_scalar_prefetch=1,
            grid=(steps,),
            in_specs=[spec(896), spec(896), column(TOK), column(QTOK), pl.BlockSpec((16, D), lambda i, s: (s[2], 0))],
            out_specs=[spec(640), whole(THIN, 256), spec(640), spec(256), whole(ROWS, BLK)],
        ),
        out_shape=[shape(BLK, 640), shape(THIN, 256), shape(BLK, 640), shape(BLK, 256), shape(ROWS, BLK)],
        compiler_params=pltpu.CompilerParams(vmem_limit_bytes=LIMIT),
        cost_estimate=SMALL,
    )(scalars, gate, up, doc, query, query)


def pack_grads_kernel(ylo_ref, doc, query, ids, keep, give):
    ylo = ylo_ref[0]
    give[ROWS:] = jnp.broadcast_to(ids[...].astype(F32), (16, TOK)).astype(BF16)
    for src, lo, n in ((doc, 0, TOK), (query, TOK, QTOK)):
        h = src[:, 384:512].astype(F32)
        t = pltpu.roll(h, 64, 1)
        low = lax.broadcasted_iota(jnp.int32, h.shape, 1) < 64
        first, second = jnp.where(low, h, t), jnp.where(low, t, h)
        for s, out in ((ylo, keep), (1 - ylo, give)):
            out[lo : lo + n, :384] = src[:, pl.ds(pl.multiple_of(s * 512, 128), 384)]
            out[lo : lo + n, 384:] = jnp.where(s == 0, first, second).astype(BF16)


def pack_grads(ylo, doc, query, ids):
    vmem = pl.BlockSpec(memory_space=pltpu.VMEM)
    return pl.pallas_call(
        pack_grads_kernel,
        in_specs=[pl.BlockSpec(memory_space=pltpu.SMEM), vmem, vmem, vmem],
        out_specs=[vmem, vmem],
        out_shape=[jax.ShapeDtypeStruct((ROWS, 512), BF16), jax.ShapeDtypeStruct((ROWS + 16, 512), BF16)],
        compiler_params=pltpu.CompilerParams(vmem_limit_bytes=LIMIT),
        cost_estimate=SMALL,
    )(ylo, doc, query, ids)


def halves_a_kernel(below, above, far0, far1):
    far0[0] = below[...]
    far1[0] = above[...]


def halves_b_kernel(below, above, x_below, x_above, _0, _1, far0, far1, x_far0, x_far1):
    far0[0] = below[...]
    far1[0] = above[...]
    x_far0[...] = x_below[...]
    x_far1[...] = x_above[...]


def halves(below, above, x=(), into=()):
    steps = 2
    spec = lambda rows, n, at: pl.BlockSpec((rows // steps, n), lambda i: (at * steps + i, 0))
    n, m = BLK // 2, ROWS // 2
    which = 1 if into else 0
    out_specs = [pl.BlockSpec((1, n // steps, 640), lambda i: (which, i, 0))] * 2
    out_shape = [jax.ShapeDtypeStruct((2, n, 640), BF16)] * 2
    in_specs = [spec(n, 640, 0), spec(n, 640, 1)]
    if into:
        in_specs += [spec(m, BLK, 0), spec(m, BLK, 1)] + [pl.BlockSpec(memory_space=pl.ANY)] * 2
        out_specs += [spec(m, BLK, 0)] * 2
        out_shape += [jax.ShapeDtypeStruct((m, BLK), BF16)] * 2
    return pl.pallas_call(
        halves_b_kernel if into else halves_a_kernel,
        grid=(steps,),
        in_specs=in_specs,
        out_specs=out_specs,
        out_shape=out_shape,
        input_output_aliases={4: 0, 5: 1} if into else {},
        compiler_params=pltpu.CompilerParams(vmem_limit_bytes=LIMIT),
        cost_estimate=SMALL,
    )(below, above, *x, *into)


def gated(hidden, gate, up):
    s = jax.nn.sigmoid(gate)
    up_factor = (hidden * gate * s).astype(BF16)
    gate_factor = (hidden * up * s * (1.0 + gate * (1.0 - s))).astype(BF16)
    return gate_factor, up_factor


def factor_kernel(phases, m, row, split, nw, nt, nx, s, *refs):
    def take(n):
        nonlocal refs
        got, refs = refs[:n], refs[n:]
        return got

    ends = phases[0][3]
    ws, thins, own_x, other_x = take(nw), take(nt), take(2), take(nx)
    befores = [None if begins else take(1)[0] for _, _, begins, _ in phases]
    hidden = [take(1)[0] for _ in phases] if ends else None
    outs = take(1 if ends and not split else len(phases))
    acc, wv, xv, wsem, xsem, bsem, osem = refs[:7]
    hv, hsem = refs[7:] if ends else (None, None)
    steps = [(p, k) for p, phase in enumerate(phases) for k in range(phase[1])]
    half = ROWS // 2

    def start(g):
        p, k = steps[g]
        at = g % SLOTS
        base = 32 * p
        block = s[base + k]
        for w in range(nw):

            @pl.when(s[base + 16 + k] == w)
            def _():
                if w < 6:
                    pltpu.make_async_copy(ws[w], wv.at[at, :, pl.ds(0, 640)], wsem.at[at]).start()
                else:
                    n = BLK // 2
                    rows = pl.ds((w - 6) * n, n)
                    for part in (0, 1):
                        pltpu.make_async_copy(
                            ws[6 + part].at[rows], wv.at[at, pl.ds(part * n, n), pl.ds(0, 640)], wsem.at[at]
                        ).start()

        for flip in range(nt):
            rows = pl.ds(pl.multiple_of(block // 2 * (BLK if flip else THIN), 512), BLK)

            @pl.when(lax.rem(block, 2) == (s[base + 24] ^ flip))
            def _():
                pltpu.make_async_copy(thins[flip].at[rows], wv.at[at, :, pl.ds(640, 256)], wsem.at[at]).start()

        if phases[p][0] == "own":
            cols = pl.ds(pl.multiple_of(block * BLK, BLK), BLK)
            for x, lo, n in ((own_x[0], 0, TOK), (own_x[1], TOK, QTOK)):
                if row <= lo < row + m:
                    pltpu.make_async_copy(x.at[:, cols], xv.at[at, pl.ds(lo - row, n)], xsem.at[at]).start()
        else:
            for q in range(min(nx, 8)):

                @pl.when(s[base + 8 + k] == q)
                def _():
                    if q < 6:
                        pltpu.make_async_copy(other_x[q].at[pl.ds(row, m)], xv.at[at], xsem.at[at]).start()
                    else:
                        for part in (0, 1):
                            lo = max(row, part * half)
                            hi = min(row + m, part * half + half)
                            if lo < hi:
                                pltpu.make_async_copy(
                                    other_x[6 + (q - 6) * 2 + part].at[pl.ds(lo - part * half, hi - lo)],
                                    xv.at[at, pl.ds(lo - row, hi - lo)],
                                    xsem.at[at],
                                ).start()

    def load(p):
        if befores[p] is not None:
            pltpu.make_async_copy(befores[p].at[pl.ds(row, m)], acc.at[p], bsem.at[p]).start()

    def finish(p):
        hidden_copy(p).wait()
        dst, to = (outs[p], slice(0, m)) if split else (outs[0], slice(p * m, p * m + m))
        g, u = gated(hv[p, :, :256].astype(F32), acc[p, :, :256], acc[p, :, 256:512])
        dst[to, :256] = g
        dst[to, 256:512] = u
        both = acc[p, :, 512:640]
        turned = pltpu.roll(both, 64, 1)
        low = lax.broadcasted_iota(jnp.int32, both.shape, 1) < 64
        g, u = gated(hv[p, :, 384:].astype(F32), jnp.where(low, both, turned), jnp.where(low, turned, both))
        dst[to, 512:640] = jnp.where(low, g.astype(F32), u.astype(F32)).astype(BF16)
        g, u = gated(hv[p, :, 256:384].astype(F32), acc[p, :, 640:768], acc[p, :, 768:])
        dst[to, 640:768] = g
        dst[to, 768:] = u

    hidden_copy = lambda p: pltpu.make_async_copy(hidden[p].at[pl.ds(row, m)], hv.at[p], hsem.at[p])
    out_copy = lambda p: pltpu.make_async_copy(acc.at[p], outs[p], osem.at[p])
    i = pl.program_id(0)
    slot = lax.rem(i, SLOTS)
    firsts = [sum(phase[1] for phase in phases[:p]) for p in range(len(phases) + 1)]

    @pl.when(i == 0)
    def _():
        start(0)
        load(0)

    for v, sem in ((wv, wsem), (xv, xsem)):
        pltpu.make_async_copy(v.at[slot], v.at[slot], sem.at[slot]).wait()

    for g in range(1, len(steps)):

        @pl.when(i == max(g - (SLOTS - 1), 0))
        def _():
            start(g)

    @pl.when(i == 0)
    def _():
        for p in range(1, len(phases)):
            load(p)
        if ends:
            for p in range(len(phases)):
                hidden_copy(p).start()

    for p in range(len(phases)):

        @pl.when(i == firsts[p])
        def _():
            if befores[p] is None:
                acc[p] = jnp.zeros((m, 896), F32)
            else:
                pltpu.make_async_copy(befores[p].at[pl.ds(row, m)], acc.at[p], bsem.at[p]).wait()

    now = jnp.where(i >= firsts[1], 1, 0) if len(phases) > 1 else 0
    acc[now] += jnp.dot(xv[slot], wv[slot], preferred_element_type=F32)

    for p in range(len(phases)):

        @pl.when(i == firsts[p + 1] - 1)
        def _():
            if ends:
                finish(p)
            else:
                out_copy(p).start()

    if not ends:

        @pl.when(i == len(steps) - 1)
        def _():
            for p in range(len(phases)):
                out_copy(p).wait()


def factors(phases, scalars, ws, thins, own, other=(), befores=(), hidden=(), rows=(0, ROWS), split=False):
    row, m = rows
    ends = phases[0][3]
    hbm = pl.BlockSpec(memory_space=pl.ANY)
    whole = lambda v: pl.BlockSpec(v.shape, lambda i, s: (0, 0))
    args = [*ws, *thins, *own, *other, *befores, *hidden]
    in_specs = [hbm] * len(args)
    if ends:
        count = len(phases) if split else 1
        out_shape = [jax.ShapeDtypeStruct((len(phases) // count * m, 896), BF16)] * count
        out_specs = [whole(v) for v in out_shape]
    else:
        out_shape = [jax.ShapeDtypeStruct((m, 896), F32)] * len(phases)
        out_specs = [hbm] * len(phases)
    return pl.pallas_call(
        functools.partial(factor_kernel, phases, m, row, split, len(ws), len(thins), len(other)),
        grid_spec=pltpu.PrefetchScalarGridSpec(
            num_scalar_prefetch=1,
            grid=(sum(phase[1] for phase in phases),),
            in_specs=in_specs,
            out_specs=out_specs,
            scratch_shapes=[
                pltpu.VMEM((len(phases), m, 896), F32),
                pltpu.VMEM((SLOTS, BLK, 896), BF16),
                pltpu.VMEM((SLOTS, m, BLK), BF16),
                pltpu.SemaphoreType.DMA((SLOTS,)),
                pltpu.SemaphoreType.DMA((SLOTS,)),
                pltpu.SemaphoreType.DMA((len(phases),)),
                pltpu.SemaphoreType.DMA((len(phases),)),
            ]
            + ([pltpu.VMEM((len(phases), m, 512), BF16), pltpu.SemaphoreType.DMA((len(phases),))] if ends else []),
        ),
        out_shape=out_shape,
        compiler_params=pltpu.CompilerParams(vmem_limit_bytes=LIMIT),
        cost_estimate=SMALL,
    )(scalars, *args)


def unpack_kernel(thin, few):
    for z in range(4):
        for j in range(32):
            lo = 16 * j
            few[16 * z : 16 * z + 16, 256 * j : 256 * j + 256] = thin[z, lo : lo + 16]


def unpack(thin):
    return pl.pallas_call(
        unpack_kernel,
        grid=(1,),
        in_specs=[pl.BlockSpec((4, 512, 256), lambda k: (0, 2, 0))],
        out_specs=pl.BlockSpec((64, D), lambda k: (0, 0)),
        out_shape=jax.ShapeDtypeStruct((64, D), BF16),
        compiler_params=pltpu.CompilerParams(vmem_limit_bytes=LIMIT),
        cost_estimate=SMALL,
    )(thin.reshape(4, THIN, 256))


def gram_kernel(mine, theirs, doc, out, acc):
    k = pl.program_id(0)

    @pl.when(k == 0)
    def _():
        acc[...] = jnp.zeros_like(acc)

    few = jnp.concatenate([mine[...], theirs[...]], 0)
    acc[...] += lax.dot_general(doc[...], few, NT, preferred_element_type=F32)

    @pl.when(k == 7)
    def _():
        out[...] = acc[...].T.astype(BF16)


def gram_part(mine, theirs, doc):
    few = pl.BlockSpec((64, BLK), lambda k: (0, k))
    return pl.pallas_call(
        gram_kernel,
        grid=(8,),
        in_specs=[few, few, pl.BlockSpec((TOK, BLK), lambda k: (0, k))],
        out_specs=pl.BlockSpec((128, TOK), lambda k: (0, 0)),
        scratch_shapes=[pltpu.VMEM((TOK, 128), F32)],
        out_shape=jax.ShapeDtypeStruct((128, TOK), BF16),
        compiler_params=pltpu.CompilerParams(vmem_limit_bytes=LIMIT),
        cost_estimate=SMALL,
    )(mine, theirs, doc)


def hop(r):
    return jnp.where(r == 0, 0, jnp.where(r == 1, 3, jnp.where(r == 2, 1, 2)))


def score_kernel(first, count, s, *refs):
    qs, (d, gram, ids, docs, before, out, f, b, acc) = refs[: 2 * count], refs[2 * count :]
    i = pl.program_id(0)
    r = first + i
    z, ylo = s[0], s[1]

    @pl.when(i == 0)
    def _():
        acc[...] = jnp.zeros_like(acc)

    for n in range(count):

        @pl.when(i == n)
        def _():
            f[:QTOK] = qs[2 * n][...]
            f[QTOK:] = qs[2 * n + 1][...]

    for flip in (0, 1):
        b[...] = lax.dot_general(f[flip * QTOK : flip * QTOK + QTOK], d[...], NT, preferred_element_type=F32)
        sums = [[jnp.zeros((8, TOK), F32) for _ in range(QS)] for _ in (0, 1)]
        for y in range(4):
            whose = ylo ^ (y % 2)
            docs_at = pl.ds(pl.multiple_of(whose * TOK, TOK), TOK)
            for x in range(4):
                for core in range(2):
                    lo = x * 64 + y // 2 * 32 + core * 16
                    p = gram[x, y, core, whose ^ flip, 0].astype(F32) * b[lo : lo + 16, docs_at]
                    who = ids[flip * QTOK + lo : flip * QTOK + lo + 16, :]
                    for k in range(QS):
                        t = jnp.where(who == k, p, 0.0)
                        sums[y % 2][k] = sums[y % 2][k] + (t[:8] + t[8:])
        group = lax.rem(z + hop(r), 4) * 2 + (ylo ^ flip)
        for k in range(QS):
            for y in (0, 1):
                at = slice(y * TOK, y * TOK + TOK)
                acc[pl.ds(group * QS + k, 1), at] = jnp.sum(sums[y][k], 0, keepdims=True)

    @pl.when(i == pl.num_programs(0) - 1)
    def _():
        for k in range(2 * DOCS):
            at = slice(k // DOCS * TOK, k // DOCS * TOK + TOK)
            out[:, k : k + 1] = before[:, k : k + 1] + jnp.sum(acc[:, at] * docs[k : k + 1, at], 1, keepdims=True)


def score_sums(first, scalars, queries, documents, gram, ids, docs, before):
    whole = lambda v: pl.BlockSpec(v.shape, lambda r, s: (0, 0))
    planes = pl.BlockSpec((4, 4, 2, 2, 1, 16, TOK), lambda r, s: (0, 0, 0, 0, lax.rem(s[0] + hop(first + r), 4), 0, 0))
    return pl.pallas_call(
        functools.partial(score_kernel, first, len(queries) // 2),
        grid_spec=pltpu.PrefetchScalarGridSpec(
            num_scalar_prefetch=1,
            grid=(len(queries) // 2,),
            in_specs=[whole(v) for v in (*queries, documents)]
            + [planes, pl.BlockSpec((2 * QTOK, 1), lambda r, s: (first + r, 0)), whole(docs), whole(before)],
            out_specs=whole(before),
            scratch_shapes=[
                pltpu.VMEM((2 * QTOK, 896), BF16),
                pltpu.VMEM((QTOK, 2 * TOK), F32),
                pltpu.VMEM((8 * QS, 2 * TOK), F32),
            ],
        ),
        out_shape=jax.ShapeDtypeStruct(before.shape, F32),
        compiler_params=pltpu.CompilerParams(vmem_limit_bytes=24 << 20),
        cost_estimate=SMALL,
    )(scalars, *queries, documents, gram, ids, docs, before)


def local(doc_inputs, doc_grads, query_inputs, query_grads, gate_weight, up_weight, doc_ids, query_ids):
    dp = lax.axis_index("dp")
    tensor = lax.axis_index("tensor")
    z, ylo = dp // 2, dp % 2
    x, core = tensor // 4, tensor % 2
    ints = lambda *vs: jnp.stack([jnp.asarray(v, jnp.int32) for v in vs])

    def scalars(blocks):
        blocks = ints(*blocks)
        turn = (blocks // 2 - x + 4) % 4
        at = jnp.where(turn == 0, 0, jnp.where(turn == 3, 1, jnp.where(turn == 1, 2, 3)))
        which_x = at * 2 + ((blocks % 2) ^ core)
        turn = (blocks // 2 - z + 4) % 4
        flip = (blocks % 2) ^ ylo
        which_w = jnp.where(
            turn == 2, 6 + flip, flip * 3 + jnp.where(turn == 0, 0, jnp.where(turn == 3, 1, 2))
        )
        spare = jnp.zeros((8 - blocks.shape[0],), jnp.int32)
        last = jnp.full((8,), ylo)
        return jnp.concatenate([blocks, spare, which_x, spare, which_w, spare, last]).astype(jnp.int32)

    first = scalars([(z + dz + 4) % 4 * 2 + ylo for dz in (0, -1, 1)])
    second = scalars([(z + dz + 4) % 4 * 2 + (ylo ^ 1) for dz in (0, -1, 1)])
    last = scalars([(z + 2) % 4 * 2 + flip for flip in (0, 1)])
    late = (z + 2) % 4, jnp.where(x == z, (z + 3) % 4, (x + 2) % 4)
    free = [jnp.logical_and(late[0] != v, late[1] != v) for v in range(4)]
    soon = jnp.where(free[0], 0, jnp.where(free[1], 1, 2)), jnp.where(free[3], 3, jnp.where(free[2], 2, 1))
    blocks_of = lambda zs: [v * 2 + flip for v in zs for flip in (0, 1)]
    early = jnp.concatenate([second, scalars(blocks_of(soon))])
    late = jnp.concatenate([last, scalars(blocks_of(late))])
    where = ints(z, ylo)

    keep0, keep1, give0, give1, piece = pack(
        ints(ylo, x * 2 + core, tensor), gate_weight, up_weight, doc_inputs, query_inputs
    )
    thin_a = lax.all_gather(keep1, AX, axis_index_groups=ZGROUPS, axis=0, tiled=True)
    a_below, a_above = send(keep0, ZP), send(keep0, ZM)
    got0 = send(give0, PARTNER)
    piece = send(piece, OTHER)
    got1 = send(give1, PARTNER)
    mine, theirs = pack_grads(ints(ylo), doc_grads, query_grads, doc_ids)
    order = jnp.stack([(z + dz + 4) % 4 * 2 + (ylo ^ flip) for dz in STEPS for flip in (0, 1)])
    ids = query_ids[order].reshape(-1, 1)
    got0, piece, a_below, a_above, got1, ids, first, early, late, where, mine, theirs = tie(
        got0, piece, a_below, a_above, got1, ids, first, early, late, where, mine, theirs
    )
    thin_b = lax.all_gather(got1, AX, axis_index_groups=ZGROUPS, axis=0, tiled=True)
    b_below, b_above = send(got0, ZP), send(got0, ZM)
    x_below, x_above = send(piece, XP), send(piece, XM)
    own = (doc_inputs, query_inputs)
    a_w = [keep0, a_below, a_above]
    (own_part,) = factors((("own", 3, True, False),), first, a_w, [thin_a], own)
    few = unpack(thin_a)
    few_too = send(few, PARTNER)
    few_too, theirs = tie(few_too, theirs)
    gram = gram_part(few, few_too, doc_inputs)
    theirs = send(theirs, PARTNER)
    into = halves(a_below, a_above)
    b_below, b_above, x_below, x_above, piece, own_part, gram, *into = tie(
        b_below, b_above, x_below, x_above, piece, own_part, gram, *into
    )
    thins = [thin_a, thin_b]
    far0, far1, x_far0, x_far1 = halves(b_below, b_above, (x_below, x_above), into)
    far0, far1 = send(far0.reshape(BLK, 640), ZP), send(far1.reshape(BLK, 640), ZM)
    piece_too, x_below_too, x_above_too = send(piece, CORE), send(x_below, CORE), send(x_above, CORE)
    piece_too, x_below_too, x_above_too, x_far0, x_far1 = tie(piece_too, x_below_too, x_above_too, x_far0, x_far1)
    x_far0, x_far1 = send(x_far0, XP), send(x_far1, XM)
    near_x = [piece, piece_too, x_below, x_below_too, x_above, x_above_too]
    near_w = [*a_w, got0, b_below, b_above]
    own_part, other_part = factors(
        (("own", 3, False, False), ("other", 4, True, False)), early, near_w, thins, own, near_x, [own_part]
    )
    gram = lax.all_gather(gram, AX, axis_index_groups=PLANES, axis=0, tiled=True).reshape(4, 4, 2, 2, 4, 16, TOK)
    x_far0, x_far1, far0, far1, own_part, other_part, theirs = tie(
        x_far0, x_far1, far0, far1, own_part, other_part, theirs
    )
    all_w = [*near_w, far0, far1]
    all_x = [*near_x, x_far0, x_far1, send(x_far0, CORE), send(x_far1, CORE)]

    rest = (("own", 2, False, True), ("other", 4, False, True))
    parts, grads = (own_part, other_part), (mine, theirs)
    q = factors(rest, late, all_w, thins, own, all_x, parts, grads, (TOK, QTOK), True)
    *q, own_part, ids_too = tie(*q, own_part, theirs[ROWS : ROWS + 1])
    ids_too = ids_too.astype(jnp.int32)
    lower, upper = jnp.where(ylo == 0, doc_ids, ids_too), jnp.where(ylo == 0, ids_too, doc_ids)
    both = jnp.concatenate([lower, upper + DOCS], 1)
    docs = (both == jnp.arange(2 * DOCS, dtype=jnp.int32)[:, None]).astype(F32)
    q_below, q_above = [send(v, ZP) for v in q], [send(v, ZM) for v in q]
    (d,) = factors(rest, late, all_w, thins, own, all_x, (own_part, other_part), grads, (0, TOK))
    *around, d = tie(*q_below, *q_above, d)
    q_far0, q_far1 = send(around[0], ZP), send(around[3], ZM)

    scores = jnp.zeros((8 * QS, 2 * DOCS), F32)
    scores = score_sums(0, where, (*q, *around), d, gram, ids, docs, scores)
    scores = score_sums(3, where, (q_far0, q_far1), d, gram, ids, docs, scores)

    for p in (CORE, X1, X3, PARTNER, OTHER):
        scores = scores + send(scores, p)
    scores = jnp.where(ylo == 0, scores[:, :DOCS], scores[:, DOCS:]).T / math.sqrt(D * FF)
    return scores[None]


def solution(mesh):
    placed = (
        P("dp", None),
        P("dp", "tensor"),
        P("dp", None),
        P("dp", "tensor"),
        P("dp", "tensor"),
        P("dp", "tensor"),
        P("dp", None),
        P(),
    )
    return jax.shard_map(
        local, mesh=mesh, in_specs=placed, out_specs=P("dp", None, None), check_vma=False
    )
```

```python
import functools
import math

import jax
import jax.numpy as jnp
from jax import lax
from jax.experimental import pallas as pl
from jax.experimental.pallas import tpu as pltpu
from jax.sharding import PartitionSpec as P

D = 8192
FF = 14336
DOCS = 4
QS = 4
TOK = 512
QTOK = 256
ROWS = TOK + QTOK
BLK = D // 8
THIN = BLK + 512
AX = ("dp", "tensor")
F32 = jnp.float32
BF16 = jnp.bfloat16


def place(z, y, x, c):
    return ((z % 4) * 2 + (y % 2)) * 16 + (x % 4) * 4 + ((y % 4) // 2) * 2 + c


def perm(fn):
    return [
        (place(z, y, x, c), place(*fn(z, y, x, c)))
        for z in range(4)
        for y in range(4)
        for x in range(4)
        for c in range(2)
    ]


ZP = perm(lambda z, y, x, c: (z + 1, y, x, c))
ZM = perm(lambda z, y, x, c: (z - 1, y, x, c))
XP = perm(lambda z, y, x, c: (z, y, x + 1, c))
XM = perm(lambda z, y, x, c: (z, y, x - 1, c))
PARTNER = perm(lambda z, y, x, c: (z, y ^ 1, x, c))
OTHER = perm(lambda z, y, x, c: (z, (3 - y) % 4, x, c))
CORE = perm(lambda z, y, x, c: (z, y, x, 1 - c))
X1 = perm(lambda z, y, x, c: (z, y, x ^ 1, c))
X3 = perm(lambda z, y, x, c: (z, y, 3 - x, c))
STEPS = (0, -1, 1, 2)
LIMIT = 56 << 20
SLOTS = 3
SMALL = pl.CostEstimate(flops=1 << 10, bytes_accessed=1 << 10, transcendentals=0)
PLANES = [[place(z, y, x, c) for x in range(4) for y in range(4) for c in range(2)] for z in range(4)]
ZGROUPS = [[place(z, y, x, c) for z in range(4)] for y in range(4) for x in range(4) for c in range(2)]
NT = (((1,), (1,)), ((), ()))


def send(v, p):
    return lax.ppermute(v, AX, p)


def tie(*vs):
    return lax.optimization_barrier(vs)


def columns_of(half, gate, up, wide, thin, thin_rows):
    gh, uh = gate[:, 384:512].astype(F32), up[:, 384:512].astype(F32)
    low = lax.broadcasted_iota(jnp.int32, gh.shape, 1) < 64
    first = jnp.where(low, gh, pltpu.roll(uh, 64, 1))
    second = jnp.where(low, pltpu.roll(gh, 64, 1), uh)
    base = pl.multiple_of(half * 512, 128)
    wide[:, :256] = gate[:, pl.ds(base, 256)]
    wide[:, 256:512] = up[:, pl.ds(base, 256)]
    wide[:, 512:] = jnp.where(half == 0, first, second).astype(BF16)
    base = pl.multiple_of(half * 512 + 256, 128)
    thin[thin_rows, :128] = gate[:, pl.ds(base, 128)]
    thin[thin_rows, 128:] = up[:, pl.ds(base, 128)]


def pack_kernel(s, gate, up, doc, query, some, keep0, keep1, give0, give1, piece):
    i = pl.program_id(0)
    columns_of(s[0], gate, up, keep0, keep1, pl.ds(i * gate.shape[0], gate.shape[0]))
    columns_of(1 - s[0], gate, up, give0, give1, slice(None))
    piece[pl.ds(i * doc.shape[0], doc.shape[0])] = doc[...]
    piece[pl.ds(TOK + i * query.shape[0], query.shape[0])] = query[...]

    @pl.when(i == 0)
    def _():
        for j in range(32):
            keep1[BLK + 16 * j : BLK + 16 * j + 16] = some[:, 256 * j : 256 * j + 256]


def pack(scalars, gate, up, doc, query):
    steps = 2
    rows = BLK // steps
    spec = lambda n: pl.BlockSpec((rows, n), lambda i, s: (i, 0))
    whole = lambda *shape: pl.BlockSpec(shape, lambda i, s: (0, 0))
    shape = lambda r, n: jax.ShapeDtypeStruct((r, n), BF16)
    column = lambda n: pl.BlockSpec((n // steps, BLK), lambda i, s: (i, s[1]))
    return pl.pallas_call(
        pack_kernel,
        grid_spec=pltpu.PrefetchScalarGridSpec(
            num_scalar_prefetch=1,
            grid=(steps,),
            in_specs=[spec(896), spec(896), column(TOK), column(QTOK), pl.BlockSpec((16, D), lambda i, s: (s[2], 0))],
            out_specs=[spec(640), whole(THIN, 256), spec(640), spec(256), whole(ROWS, BLK)],
        ),
        out_shape=[shape(BLK, 640), shape(THIN, 256), shape(BLK, 640), shape(BLK, 256), shape(ROWS, BLK)],
        compiler_params=pltpu.CompilerParams(vmem_limit_bytes=LIMIT),
        cost_estimate=SMALL,
    )(scalars, gate, up, doc, query, query)


def pack_grads_kernel(ylo_ref, doc, query, ids, keep, give):
    ylo = ylo_ref[0]
    give[ROWS:] = jnp.broadcast_to(ids[...].astype(F32), (16, TOK)).astype(BF16)
    for src, lo, n in ((doc, 0, TOK), (query, TOK, QTOK)):
        h = src[:, 384:512].astype(F32)
        t = pltpu.roll(h, 64, 1)
        low = lax.broadcasted_iota(jnp.int32, h.shape, 1) < 64
        first, second = jnp.where(low, h, t), jnp.where(low, t, h)
        for s, out in ((ylo, keep), (1 - ylo, give)):
            out[lo : lo + n, :384] = src[:, pl.ds(pl.multiple_of(s * 512, 128), 384)]
            out[lo : lo + n, 384:] = jnp.where(s == 0, first, second).astype(BF16)


def pack_grads(ylo, doc, query, ids):
    vmem = pl.BlockSpec(memory_space=pltpu.VMEM)
    return pl.pallas_call(
        pack_grads_kernel,
        in_specs=[pl.BlockSpec(memory_space=pltpu.SMEM), vmem, vmem, vmem],
        out_specs=[vmem, vmem],
        out_shape=[jax.ShapeDtypeStruct((ROWS, 512), BF16), jax.ShapeDtypeStruct((ROWS + 16, 512), BF16)],
        compiler_params=pltpu.CompilerParams(vmem_limit_bytes=LIMIT),
        cost_estimate=SMALL,
    )(ylo, doc, query, ids)


def halves_a_kernel(below, above, far0, far1):
    far0[0] = below[...]
    far1[0] = above[...]


def halves_b_kernel(below, above, x_below, x_above, _0, _1, far0, far1, x_far0, x_far1):
    far0[0] = below[...]
    far1[0] = above[...]
    x_far0[...] = x_below[...]
    x_far1[...] = x_above[...]


def halves(below, above, x=(), into=()):
    steps = 2
    spec = lambda rows, n, at: pl.BlockSpec((rows // steps, n), lambda i: (at * steps + i, 0))
    n, m = BLK // 2, ROWS // 2
    which = 1 if into else 0
    out_specs = [pl.BlockSpec((1, n // steps, 640), lambda i: (which, i, 0))] * 2
    out_shape = [jax.ShapeDtypeStruct((2, n, 640), BF16)] * 2
    in_specs = [spec(n, 640, 0), spec(n, 640, 1)]
    if into:
        in_specs += [spec(m, BLK, 0), spec(m, BLK, 1)] + [pl.BlockSpec(memory_space=pl.ANY)] * 2
        out_specs += [spec(m, BLK, 0)] * 2
        out_shape += [jax.ShapeDtypeStruct((m, BLK), BF16)] * 2
    return pl.pallas_call(
        halves_b_kernel if into else halves_a_kernel,
        grid=(steps,),
        in_specs=in_specs,
        out_specs=out_specs,
        out_shape=out_shape,
        input_output_aliases={4: 0, 5: 1} if into else {},
        compiler_params=pltpu.CompilerParams(vmem_limit_bytes=LIMIT),
        cost_estimate=SMALL,
    )(below, above, *x, *into)


def gated(hidden, gate, up):
    s = jax.nn.sigmoid(gate)
    up_factor = (hidden * gate * s).astype(BF16)
    gate_factor = (hidden * up * s * (1.0 + gate * (1.0 - s))).astype(BF16)
    return gate_factor, up_factor


def factor_kernel(phases, m, row, split, nw, nt, nx, s, *refs):
    def take(n):
        nonlocal refs
        got, refs = refs[:n], refs[n:]
        return got

    ends = phases[0][3]
    ws, thins, own_x, other_x = take(nw), take(nt), take(2), take(nx)
    befores = [None if begins else take(1)[0] for _, _, begins, _ in phases]
    hidden = [take(1)[0] for _ in phases] if ends else None
    outs = take(1 if ends and not split else len(phases))
    acc, wv, xv, wsem, xsem, bsem, osem = refs[:7]
    hv, hsem = refs[7:] if ends else (None, None)
    steps = [(p, k) for p, phase in enumerate(phases) for k in range(phase[1])]
    half = ROWS // 2

    def start(g):
        p, k = steps[g]
        at = g % SLOTS
        base = 32 * p
        block = s[base + k]
        for w in range(nw):

            @pl.when(s[base + 16 + k] == w)
            def _():
                if w < 6:
                    pltpu.make_async_copy(ws[w], wv.at[at, :, pl.ds(0, 640)], wsem.at[at]).start()
                else:
                    n = BLK // 2
                    rows = pl.ds((w - 6) * n, n)
                    for part in (0, 1):
                        pltpu.make_async_copy(
                            ws[6 + part].at[rows], wv.at[at, pl.ds(part * n, n), pl.ds(0, 640)], wsem.at[at]
                        ).start()

        for flip in range(nt):
            rows = pl.ds(pl.multiple_of(block // 2 * (BLK if flip else THIN), 512), BLK)

            @pl.when(lax.rem(block, 2) == (s[base + 24] ^ flip))
            def _():
                pltpu.make_async_copy(thins[flip].at[rows], wv.at[at, :, pl.ds(640, 256)], wsem.at[at]).start()

        if phases[p][0] == "own":
            cols = pl.ds(pl.multiple_of(block * BLK, BLK), BLK)
            for x, lo, n in ((own_x[0], 0, TOK), (own_x[1], TOK, QTOK)):
                if row <= lo < row + m:
                    pltpu.make_async_copy(x.at[:, cols], xv.at[at, pl.ds(lo - row, n)], xsem.at[at]).start()
        else:
            for q in range(min(nx, 8)):

                @pl.when(s[base + 8 + k] == q)
                def _():
                    if q < 6:
                        pltpu.make_async_copy(other_x[q].at[pl.ds(row, m)], xv.at[at], xsem.at[at]).start()
                    else:
                        for part in (0, 1):
                            lo = max(row, part * half)
                            hi = min(row + m, part * half + half)
                            if lo < hi:
                                pltpu.make_async_copy(
                                    other_x[6 + (q - 6) * 2 + part].at[pl.ds(lo - part * half, hi - lo)],
                                    xv.at[at, pl.ds(lo - row, hi - lo)],
                                    xsem.at[at],
                                ).start()

    def load(p):
        if befores[p] is not None:
            pltpu.make_async_copy(befores[p].at[pl.ds(row, m)], acc.at[p], bsem.at[p]).start()

    def finish(p):
        hidden_copy(p).wait()
        dst, to = (outs[p], slice(0, m)) if split else (outs[0], slice(p * m, p * m + m))
        g, u = gated(hv[p, :, :256].astype(F32), acc[p, :, :256], acc[p, :, 256:512])
        dst[to, :256] = g
        dst[to, 256:512] = u
        both = acc[p, :, 512:640]
        turned = pltpu.roll(both, 64, 1)
        low = lax.broadcasted_iota(jnp.int32, both.shape, 1) < 64
        g, u = gated(hv[p, :, 384:].astype(F32), jnp.where(low, both, turned), jnp.where(low, turned, both))
        dst[to, 512:640] = jnp.where(low, g.astype(F32), u.astype(F32)).astype(BF16)
        g, u = gated(hv[p, :, 256:384].astype(F32), acc[p, :, 640:768], acc[p, :, 768:])
        dst[to, 640:768] = g
        dst[to, 768:] = u

    hidden_copy = lambda p: pltpu.make_async_copy(hidden[p].at[pl.ds(row, m)], hv.at[p], hsem.at[p])
    out_copy = lambda p: pltpu.make_async_copy(acc.at[p], outs[p], osem.at[p])
    i = pl.program_id(0)
    slot = lax.rem(i, SLOTS)
    firsts = [sum(phase[1] for phase in phases[:p]) for p in range(len(phases) + 1)]

    @pl.when(i == 0)
    def _():
        start(0)
        load(0)

    for v, sem in ((wv, wsem), (xv, xsem)):
        pltpu.make_async_copy(v.at[slot], v.at[slot], sem.at[slot]).wait()

    for g in range(1, len(steps)):

        @pl.when(i == max(g - (SLOTS - 1), 0))
        def _():
            start(g)

    @pl.when(i == 0)
    def _():
        for p in range(1, len(phases)):
            load(p)
        if ends:
            for p in range(len(phases)):
                hidden_copy(p).start()

    for p in range(len(phases)):

        @pl.when(i == firsts[p])
        def _():
            if befores[p] is None:
                acc[p] = jnp.zeros((m, 896), F32)
            else:
                pltpu.make_async_copy(befores[p].at[pl.ds(row, m)], acc.at[p], bsem.at[p]).wait()

    now = jnp.where(i >= firsts[1], 1, 0) if len(phases) > 1 else 0
    acc[now] += jnp.dot(xv[slot], wv[slot], preferred_element_type=F32)

    for p in range(len(phases)):

        @pl.when(i == firsts[p + 1] - 1)
        def _():
            if ends:
                finish(p)
            else:
                out_copy(p).start()

    if not ends:

        @pl.when(i == len(steps) - 1)
        def _():
            for p in range(len(phases)):
                out_copy(p).wait()


def factors(phases, scalars, ws, thins, own, other=(), befores=(), hidden=(), rows=(0, ROWS), split=False):
    row, m = rows
    ends = phases[0][3]
    hbm = pl.BlockSpec(memory_space=pl.ANY)
    whole = lambda v: pl.BlockSpec(v.shape, lambda i, s: (0, 0))
    args = [*ws, *thins, *own, *other, *befores, *hidden]
    in_specs = [hbm] * len(args)
    if ends:
        count = len(phases) if split else 1
        out_shape = [jax.ShapeDtypeStruct((len(phases) // count * m, 896), BF16)] * count
        out_specs = [whole(v) for v in out_shape]
    else:
        out_shape = [jax.ShapeDtypeStruct((m, 896), F32)] * len(phases)
        out_specs = [hbm] * len(phases)
    return pl.pallas_call(
        functools.partial(factor_kernel, phases, m, row, split, len(ws), len(thins), len(other)),
        grid_spec=pltpu.PrefetchScalarGridSpec(
            num_scalar_prefetch=1,
            grid=(sum(phase[1] for phase in phases),),
            in_specs=in_specs,
            out_specs=out_specs,
            scratch_shapes=[
                pltpu.VMEM((len(phases), m, 896), F32),
                pltpu.VMEM((SLOTS, BLK, 896), BF16),
                pltpu.VMEM((SLOTS, m, BLK), BF16),
                pltpu.SemaphoreType.DMA((SLOTS,)),
                pltpu.SemaphoreType.DMA((SLOTS,)),
                pltpu.SemaphoreType.DMA((len(phases),)),
                pltpu.SemaphoreType.DMA((len(phases),)),
            ]
            + ([pltpu.VMEM((len(phases), m, 512), BF16), pltpu.SemaphoreType.DMA((len(phases),))] if ends else []),
        ),
        out_shape=out_shape,
        compiler_params=pltpu.CompilerParams(vmem_limit_bytes=LIMIT),
        cost_estimate=SMALL,
    )(scalars, *args)


def unpack_kernel(thin, few):
    for z in range(4):
        for j in range(32):
            lo = 16 * j
            few[16 * z : 16 * z + 16, 256 * j : 256 * j + 256] = thin[z, lo : lo + 16]


def unpack(thin):
    return pl.pallas_call(
        unpack_kernel,
        grid=(1,),
        in_specs=[pl.BlockSpec((4, 512, 256), lambda k: (0, 2, 0))],
        out_specs=pl.BlockSpec((64, D), lambda k: (0, 0)),
        out_shape=jax.ShapeDtypeStruct((64, D), BF16),
        compiler_params=pltpu.CompilerParams(vmem_limit_bytes=LIMIT),
        cost_estimate=SMALL,
    )(thin.reshape(4, THIN, 256))


def gram_kernel(mine, theirs, doc, out, acc):
    k = pl.program_id(0)

    @pl.when(k == 0)
    def _():
        acc[...] = jnp.zeros_like(acc)

    few = jnp.concatenate([mine[...], theirs[...]], 0)
    acc[...] += lax.dot_general(doc[...], few, NT, preferred_element_type=F32)

    @pl.when(k == 7)
    def _():
        out[...] = acc[...].T.astype(BF16)


def gram_part(mine, theirs, doc):
    few = pl.BlockSpec((64, BLK), lambda k: (0, k))
    return pl.pallas_call(
        gram_kernel,
        grid=(8,),
        in_specs=[few, few, pl.BlockSpec((TOK, BLK), lambda k: (0, k))],
        out_specs=pl.BlockSpec((128, TOK), lambda k: (0, 0)),
        scratch_shapes=[pltpu.VMEM((TOK, 128), F32)],
        out_shape=jax.ShapeDtypeStruct((128, TOK), BF16),
        compiler_params=pltpu.CompilerParams(vmem_limit_bytes=LIMIT),
        cost_estimate=SMALL,
    )(mine, theirs, doc)


def hop(r):
    return jnp.where(r == 0, 0, jnp.where(r == 1, 3, jnp.where(r == 2, 1, 2)))


def score_kernel(first, count, s, *refs):
    qs, (d, gram, ids, docs, before, out, f, b, acc) = refs[: 2 * count], refs[2 * count :]
    i = pl.program_id(0)
    r = first + i
    z, ylo = s[0], s[1]

    @pl.when(i == 0)
    def _():
        acc[...] = jnp.zeros_like(acc)

    for n in range(count):

        @pl.when(i == n)
        def _():
            f[:QTOK] = qs[2 * n][...]
            f[QTOK:] = qs[2 * n + 1][...]

    for flip in (0, 1):
        b[...] = lax.dot_general(f[flip * QTOK : flip * QTOK + QTOK], d[...], NT, preferred_element_type=F32)
        sums = [[jnp.zeros((8, TOK), F32) for _ in range(QS)] for _ in (0, 1)]
        for y in range(4):
            whose = ylo ^ (y % 2)
            docs_at = pl.ds(pl.multiple_of(whose * TOK, TOK), TOK)
            for x in range(4):
                for core in range(2):
                    lo = x * 64 + y // 2 * 32 + core * 16
                    p = gram[x, y, core, whose ^ flip, 0].astype(F32) * b[lo : lo + 16, docs_at]
                    who = ids[flip * QTOK + lo : flip * QTOK + lo + 16, :]
                    for k in range(QS):
                        t = jnp.where(who == k, p, 0.0)
                        sums[y % 2][k] = sums[y % 2][k] + (t[:8] + t[8:])
        group = lax.rem(z + hop(r), 4) * 2 + (ylo ^ flip)
        for k in range(QS):
            for y in (0, 1):
                at = slice(y * TOK, y * TOK + TOK)
                acc[pl.ds(group * QS + k, 1), at] = jnp.sum(sums[y][k], 0, keepdims=True)

    @pl.when(i == pl.num_programs(0) - 1)
    def _():
        for k in range(2 * DOCS):
            at = slice(k // DOCS * TOK, k // DOCS * TOK + TOK)
            out[:, k : k + 1] = before[:, k : k + 1] + jnp.sum(acc[:, at] * docs[k : k + 1, at], 1, keepdims=True)


def score_sums(first, scalars, queries, documents, gram, ids, docs, before):
    whole = lambda v: pl.BlockSpec(v.shape, lambda r, s: (0, 0))
    planes = pl.BlockSpec((4, 4, 2, 2, 1, 16, TOK), lambda r, s: (0, 0, 0, 0, lax.rem(s[0] + hop(first + r), 4), 0, 0))
    return pl.pallas_call(
        functools.partial(score_kernel, first, len(queries) // 2),
        grid_spec=pltpu.PrefetchScalarGridSpec(
            num_scalar_prefetch=1,
            grid=(len(queries) // 2,),
            in_specs=[whole(v) for v in (*queries, documents)]
            + [planes, pl.BlockSpec((2 * QTOK, 1), lambda r, s: (first + r, 0)), whole(docs), whole(before)],
            out_specs=whole(before),
            scratch_shapes=[
                pltpu.VMEM((2 * QTOK, 896), BF16),
                pltpu.VMEM((QTOK, 2 * TOK), F32),
                pltpu.VMEM((8 * QS, 2 * TOK), F32),
            ],
        ),
        out_shape=jax.ShapeDtypeStruct(before.shape, F32),
        compiler_params=pltpu.CompilerParams(vmem_limit_bytes=24 << 20),
        cost_estimate=SMALL,
    )(scalars, *queries, documents, gram, ids, docs, before)


def local(doc_inputs, doc_grads, query_inputs, query_grads, gate_weight, up_weight, doc_ids, query_ids):
    dp = lax.axis_index("dp")
    tensor = lax.axis_index("tensor")
    z, ylo = dp // 2, dp % 2
    x, core = tensor // 4, tensor % 2
    ints = lambda *vs: jnp.stack([jnp.asarray(v, jnp.int32) for v in vs])

    def scalars(blocks):
        blocks = ints(*blocks)
        turn = (blocks // 2 - x + 4) % 4
        at = jnp.where(turn == 0, 0, jnp.where(turn == 3, 1, jnp.where(turn == 1, 2, 3)))
        which_x = at * 2 + ((blocks % 2) ^ core)
        turn = (blocks // 2 - z + 4) % 4
        flip = (blocks % 2) ^ ylo
        which_w = jnp.where(
            turn == 2, 6 + flip, flip * 3 + jnp.where(turn == 0, 0, jnp.where(turn == 3, 1, 2))
        )
        spare = jnp.zeros((8 - blocks.shape[0],), jnp.int32)
        last = jnp.full((8,), ylo)
        return jnp.concatenate([blocks, spare, which_x, spare, which_w, spare, last]).astype(jnp.int32)

    first = scalars([(z + dz + 4) % 4 * 2 + ylo for dz in (0, -1, 1)])
    second = scalars([(z + dz + 4) % 4 * 2 + (ylo ^ 1) for dz in (0, -1, 1)])
    last = scalars([(z + 2) % 4 * 2 + flip for flip in (0, 1)])
    late = (z + 2) % 4, jnp.where(x == z, (z + 3) % 4, (x + 2) % 4)
    free = [jnp.logical_and(late[0] != v, late[1] != v) for v in range(4)]
    soon = jnp.where(free[0], 0, jnp.where(free[1], 1, 2)), jnp.where(free[3], 3, jnp.where(free[2], 2, 1))
    blocks_of = lambda zs: [v * 2 + flip for v in zs for flip in (0, 1)]
    early = jnp.concatenate([second, scalars(blocks_of(soon))])
    late = jnp.concatenate([last, scalars(blocks_of(late))])
    where = ints(z, ylo)

    keep0, keep1, give0, give1, piece = pack(
        ints(ylo, x * 2 + core, tensor), gate_weight, up_weight, doc_inputs, query_inputs
    )
    thin_a = lax.all_gather(keep1, AX, axis_index_groups=ZGROUPS, axis=0, tiled=True)
    a_below, a_above = send(keep0, ZP), send(keep0, ZM)
    got0 = send(give0, PARTNER)
    piece = send(piece, OTHER)
    got1 = send(give1, PARTNER)
    mine, theirs = pack_grads(ints(ylo), doc_grads, query_grads, doc_ids)
    order = jnp.stack([(z + dz + 4) % 4 * 2 + (ylo ^ flip) for dz in STEPS for flip in (0, 1)])
    ids = query_ids[order].reshape(-1, 1)
    got0, piece, a_below, a_above, got1, ids, first, early, late, where, mine, theirs = tie(
        got0, piece, a_below, a_above, got1, ids, first, early, late, where, mine, theirs
    )
    thin_b = lax.all_gather(got1, AX, axis_index_groups=ZGROUPS, axis=0, tiled=True)
    b_below, b_above = send(got0, ZP), send(got0, ZM)
    x_below, x_above = send(piece, XP), send(piece, XM)
    own = (doc_inputs, query_inputs)
    a_w = [keep0, a_below, a_above]
    (own_part,) = factors((("own", 3, True, False),), first, a_w, [thin_a], own)
    few = unpack(thin_a)
    few_too = send(few, PARTNER)
    few_too, theirs = tie(few_too, theirs)
    gram = gram_part(few, few_too, doc_inputs)
    theirs = send(theirs, PARTNER)
    into = halves(a_below, a_above)
    b_below, b_above, x_below, x_above, piece, own_part, gram, *into = tie(
        b_below, b_above, x_below, x_above, piece, own_part, gram, *into
    )
    thins = [thin_a, thin_b]
    far0, far1, x_far0, x_far1 = halves(b_below, b_above, (x_below, x_above), into)
    far0, far1 = send(far0.reshape(BLK, 640), ZP), send(far1.reshape(BLK, 640), ZM)
    piece_too, x_below_too, x_above_too = send(piece, CORE), send(x_below, CORE), send(x_above, CORE)
    piece_too, x_below_too, x_above_too, x_far0, x_far1 = tie(piece_too, x_below_too, x_above_too, x_far0, x_far1)
    x_far0, x_far1 = send(x_far0, XP), send(x_far1, XM)
    near_x = [piece, piece_too, x_below, x_below_too, x_above, x_above_too]
    near_w = [*a_w, got0, b_below, b_above]
    own_part, other_part = factors(
        (("own", 3, False, False), ("other", 4, True, False)), early, near_w, thins, own, near_x, [own_part]
    )
    gram = lax.all_gather(gram, AX, axis_index_groups=PLANES, axis=0, tiled=True).reshape(4, 4, 2, 2, 4, 16, TOK)
    x_far0, x_far1, far0, far1, own_part, other_part, theirs = tie(
        x_far0, x_far1, far0, far1, own_part, other_part, theirs
    )
    all_w = [*near_w, far0, far1]
    all_x = [*near_x, x_far0, x_far1, send(x_far0, CORE), send(x_far1, CORE)]

    rest = (("own", 2, False, True), ("other", 4, False, True))
    parts, grads = (own_part, other_part), (mine, theirs)
    q = factors(rest, late, all_w, thins, own, all_x, parts, grads, (TOK, QTOK), True)
    *q, own_part, ids_too = tie(*q, own_part, theirs[ROWS : ROWS + 1])
    ids_too = ids_too.astype(jnp.int32)
    lower, upper = jnp.where(ylo == 0, doc_ids, ids_too), jnp.where(ylo == 0, ids_too, doc_ids)
    both = jnp.concatenate([lower, upper + DOCS], 1)
    docs = (both == jnp.arange(2 * DOCS, dtype=jnp.int32)[:, None]).astype(F32)
    q_below, q_above = [send(v, ZP) for v in q], [send(v, ZM) for v in q[::-1]][::-1]
    (d,) = factors(rest, late, all_w, thins, own, all_x, (own_part, other_part), grads, (0, TOK))
    q_below[0], q_above[1], d = tie(q_below[0], q_above[1], d)
    q_far0, q_far1 = send(q_below[0], ZP), send(q_above[1], ZM)
    around = (*q_below, *q_above)

    scores = jnp.zeros((8 * QS, 2 * DOCS), F32)
    scores = score_sums(0, where, (*q, *around), d, gram, ids, docs, scores)
    scores = score_sums(3, where, (q_far0, q_far1), d, gram, ids, docs, scores)

    for p in (CORE, X1, X3, PARTNER, OTHER):
        scores = scores + send(scores, p)
    scores = jnp.where(ylo == 0, scores[:, :DOCS], scores[:, DOCS:]).T / math.sqrt(D * FF)
    return scores[None]


def solution(mesh):
    placed = (
        P("dp", None),
        P("dp", "tensor"),
        P("dp", None),
        P("dp", "tensor"),
        P("dp", "tensor"),
        P("dp", "tensor"),
        P("dp", None),
        P(),
    )
    return jax.shard_map(
        local, mesh=mesh, in_specs=placed, out_specs=P("dp", None, None), check_vma=False
    )
```
